32 devices in a mesh: grp: 2 (over x), dim: 8 (over z, y), blk: 2 (over core).
Axes of the slice: x: 2, y: 2, z: 4, core: 2. Of those that a mesh axis runs over, the one named last changes fastest.
Arguments:
- particles: float32 [1024, 131072], P(('grp', 'blk'), 'dim'), parts along dimension 0, may hold values from -30 to 30, as said below
- scores: float32 [1024, 131072], P(('grp', 'blk'), 'dim'), parts along dimension 0, may hold values from -0.00048828125 to 0.00048828125
Outputs:
- velocity: float32 [1024, 131072], P(('grp', 'blk'), 'dim'), parts along dimension 0
The draws below stay inside these ranges and needn't reach their ends.
There are 2 independent parts, one for each index of `grp`. The reference program is written for one: setup_inputs(seed, part) draws one part's arguments, and reference() takes and returns one part's arrays. A program takes and returns all parts, laid end to end along the dimension named above; each array names one. Nothing has to cross between parts.
Inputs may be any that keep to these rules, and one draw needn't show every extreme that they name: `particles`: finite positions.
All inputs are finite; a program needn't handle non-finite values.
Results may differ from the reference program's by a relative error of at most 0.000084.
Values sent between devices are 32-bit elements; how exact they have to be, the bound alone decides.
No kernel may reach another device: no remote copies, remote signals or barrier semaphores. Data moves between devices by JAX's collectives and lax.ppermute only.
A program may use at most 192 MiB of HBM per device.

```python
import math
import jax
import jax.numpy as jnp
from jax import lax

DIMS = 131072
PARTICLES = 512


def draw_particles(key, part):
    key = jax.random.fold_in(key, 11)
    key_centers, key_member, key_mixing, key_scale, key_jitter, key_column = jax.random.split(key, 6)
    centers = jax.random.truncated_normal(key_centers, -4.0, 4.0, (8, DIMS), jnp.float32)
    member = jax.random.randint(key_member, (PARTICLES,), 0, 8)
    mixing = jax.random.uniform(key_mixing, (PARTICLES, 1), jnp.float32, 0.3, 1.0)
    ramp = jnp.arange(DIMS, dtype=jnp.float32) / DIMS
    rough = jnp.exp(jax.random.uniform(key_column, (DIMS,), jnp.float32, -0.35, 0.35))
    column_scale = jnp.exp(0.55 * ramp) * rough
    row_scale = jnp.exp(jax.random.uniform(key_scale, (PARTICLES, 1), jnp.float32, math.log(0.4), math.log(1.2)))
    jitter = jax.random.truncated_normal(key_jitter, -4.0, 4.0, (PARTICLES, DIMS), jnp.float32)
    return (mixing * centers[member] + row_scale * jitter) * column_scale[None, :]


def block_scale(own_key, dims, cuts, least, high):
    def one(dim, blocks):
        draws = jax.random.uniform(jax.random.fold_in(jax.random.fold_in(own_key, 6), dim), (blocks,), jnp.float32, least / len(cuts), high / len(cuts))
        return jnp.repeat(jnp.exp(draws), dims[dim] // blocks).reshape((-1,) + (1,) * (len(dims) - dim - 1))

    factor_of = one(*cuts[0])
    for cut in cuts[1:]:
        factor_of = factor_of * one(*cut)
    return factor_of


def noise(key, extent, deviation, limit, pieces=(), kind=jnp.bfloat16):
    values = deviation * jax.random.normal(key, extent, jnp.float32)
    if pieces:
        values = values * block_scale(key, extent, pieces, -0.22, 0.18)
    return jnp.clip(values, -limit, limit).astype(kind)


def setup_inputs(seed: int = 0, part: int = 0) -> dict:
    splits = jax.random.split(jax.random.key(seed), 3)
    part_splits = jax.random.split(jax.random.fold_in(splits[2], part), 3)
    particles = draw_particles(jax.random.fold_in(jax.random.fold_in(splits[2], part), 71), part)
    scores = noise(part_splits[1], (PARTICLES, DIMS), (4.0 / DIMS), 0.00048828125, ((0, 2), (1, 8)), jnp.float32)
    return dict(particles=particles, scores=scores)


def reference(particles, scores):
    row_norms = jnp.sum(particles * particles, axis=1)
    products = jnp.dot(particles, particles.T, precision=lax.Precision.HIGHEST, preferred_element_type=jnp.float32)
    distance = row_norms[:, None] + row_norms[None, :] - 2.0 * products
    kernel_width = jnp.sum(distance) / (PARTICLES * PARTICLES * math.log(PARTICLES))
    kernel = jnp.exp(-distance / kernel_width)
    weight = jnp.sum(kernel, axis=1)
    pulled = jnp.dot(kernel, scores, precision=lax.Precision.HIGHEST, preferred_element_type=jnp.float32)
    averaged = jnp.dot(kernel, particles, precision=lax.Precision.HIGHEST, preferred_element_type=jnp.float32)
    return 0.5 * kernel_width * pulled + particles * weight[:, None] - averaged
```

```python
import functools
import math

import jax
import jax.numpy as jnp
from jax import lax
from jax.experimental import pallas as pl
from jax.experimental.pallas import tpu as pltpu
from jax.sharding import PartitionSpec as P

CHUNKS = 4
TILE = 1024
VMEM_LIMIT = 40 * 1024 * 1024


def params():
    return pltpu.CompilerParams(vmem_limit_bytes=VMEM_LIMIT)


def split(x):
    hi = x.astype(jnp.bfloat16)
    lo = (x - hi.astype(jnp.float32)).astype(jnp.bfloat16)
    return hi, lo


def nt_dot(left, right):
    return lax.dot_general(left, right, (((1,), (1,)), ((), ())), preferred_element_type=jnp.float32)


def nn_dot(left, right):
    return jnp.dot(left, right, preferred_element_type=jnp.float32)


def lane_sums(values):
    total = values[:, :128]
    for start in range(128, values.shape[1], 128):
        total = total + values[:, start:start + 128]
    return total


def whole(array_or_shape):
    shape = getattr(array_or_shape, "shape", array_or_shape)
    return pl.BlockSpec(shape, lambda i: (0,) * len(shape))


def f32(*shape):
    return jax.ShapeDtypeStruct(shape, jnp.float32)


def write_shards(distance_ref, shard_refs):
    count = len(shard_refs)
    rows = shard_refs[0].shape[0]
    me = lax.axis_index("dim")
    for step, shard_ref in enumerate(shard_refs):
        owner = lax.rem(me + step, count)
        shard_ref[...] = distance_ref[pl.ds(pl.multiple_of(owner * rows, rows), rows), :]


def read_shards(shard_refs, distance_ref):
    count = len(shard_refs)
    rows = shard_refs[0].shape[0]
    me = lax.axis_index("dim")
    for step, shard_ref in enumerate(shard_refs):
        owner = lax.rem(me - step + count, count)
        distance_ref[pl.ds(pl.multiple_of(owner * rows, rows), rows), :] = shard_ref[...]


def own_kernel(first, last, *refs):
    refs = list(refs)
    x_ref = refs.pop(0)
    gram_in, cross_in, squares_in = (None, None, None) if first else [refs.pop(0) for _ in range(3)]
    copy_ref = refs.pop(0)
    gram_ref, cross_ref, squares_ref = [refs.pop(0) for _ in range(3)]

    @pl.when(pl.program_id(0) == 0)
    def _():
        gram_ref[...] = jnp.zeros_like(gram_ref) if first else gram_in[...]
        cross_ref[...] = jnp.zeros_like(cross_ref) if first else cross_in[...]
        squares_ref[...] = jnp.zeros_like(squares_ref) if first else squares_in[...]

    x = x_ref[...]
    copy_ref[...] = x
    hi, lo = split(x)
    gram_ref[...] += nt_dot(hi, hi)
    cross_ref[...] += nt_dot(hi, lo)
    squares_ref[...] += lane_sums(x * x)

    if last:
        distance_ref = refs.pop()
        shard_refs = refs

        @pl.when(pl.program_id(0) == pl.num_programs(0) - 1)
        def _():
            mixed = cross_ref[...]
            gram = gram_ref[...] + mixed + mixed.T
            norms = jnp.sum(squares_ref[...], axis=1, keepdims=True)
            distance_ref[...] = norms + norms.T - 2.0 * gram
            write_shards(distance_ref, shard_refs)


def own_part(particles, carried, chunk, chunks, count):
    rows, columns = particles.shape
    width = columns // chunks
    tile = min(TILE, width)
    tiles = width // tile
    first, last = chunk == 0, chunk == chunks - 1
    offset = chunk * tiles
    shard = f32(rows // count, rows)
    outs = [f32(rows, width), f32(rows, rows), f32(rows, rows), f32(rows, 128)] + ([shard] * count if last else [])
    out_specs = [pl.BlockSpec((rows, tile), lambda i: (0, i))] + [whole(o) for o in outs[1:]]
    results = pl.pallas_call(
        functools.partial(own_kernel, first, last),
        grid=(tiles,),
        in_specs=[pl.BlockSpec((rows, tile), lambda i: (0, offset + i))] + [whole(c) for c in carried],
        out_specs=out_specs,
        out_shape=outs,
        scratch_shapes=[pltpu.VMEM((rows, rows), jnp.float32)] if last else [],
        compiler_params=params(),
        cost_estimate=pl.CostEstimate(flops=4 * rows * rows * width, bytes_accessed=8 * rows * width, transcendentals=0),
        name="own_gram",
    )(particles, *carried)
    return results[0], results[1:4], results[4:]


def pair_kernel(first, last, *refs):
    refs = list(refs)
    mine_ref, other_ref = refs.pop(0), refs.pop(0)
    own_squares = refs.pop(0) if last else None
    gram_in, squares_in = (None, None) if first else [refs.pop(0) for _ in range(2)]
    gram_ref, squares_ref = [refs.pop(0) for _ in range(2)]

    @pl.when(pl.program_id(0) == 0)
    def _():
        gram_ref[...] = jnp.zeros_like(gram_ref) if first else gram_in[...]
        squares_ref[...] = jnp.zeros_like(squares_ref) if first else squares_in[...]

    other = other_ref[...]
    my_hi, my_lo = split(mine_ref[...])
    hi, lo = split(other)
    gram_ref[...] += nt_dot(my_hi, hi) + nt_dot(my_lo, hi) + nt_dot(my_hi, lo)
    squares_ref[...] += lane_sums(other * other)

    if last:
        distance_ref = refs.pop()
        shard_refs = refs

        @pl.when(pl.program_id(0) == pl.num_programs(0) - 1)
        def _():
            norms = jnp.sum(own_squares[...], axis=1, keepdims=True)
            others = jnp.sum(squares_ref[...], axis=1, keepdims=True)
            distance_ref[...] = norms + others.T - 2.0 * gram_ref[...]
            write_shards(distance_ref, shard_refs)


def pair_part(particles, visitor, own_squares, carried, chunk, chunks, count):
    rows, columns = particles.shape
    width = columns // chunks
    tile = min(TILE, width)
    tiles = width // tile
    first, last = chunk == 0, chunk == chunks - 1
    offset = chunk * tiles
    outs = [f32(rows, rows), f32(rows, 128)] + ([f32(rows // count, rows)] * count if last else [])
    extra = ([own_squares] if last else []) + list(carried)
    results = pl.pallas_call(
        functools.partial(pair_kernel, first, last),
        grid=(tiles,),
        in_specs=[
            pl.BlockSpec((rows, tile), lambda i: (0, offset + i)),
            pl.BlockSpec((rows, tile), lambda i: (0, i)),
        ] + [whole(e) for e in extra],
        out_specs=[whole(o) for o in outs],
        out_shape=outs,
        scratch_shapes=[pltpu.VMEM((rows, rows), jnp.float32)] if last else [],
        compiler_params=params(),
        cost_estimate=pl.CostEstimate(flops=6 * rows * rows * width, bytes_accessed=8 * rows * width, transcendentals=0),
        name="pair_gram",
    )(particles, visitor, *extra)
    return results[:2], results[2:]


def exchange(shards):
    count = len(shards)
    arrived = [shards[0]]
    for step in range(1, count):
        arrived.append(lax.ppermute(shards[step], "dim", [(i, (i + step) % count) for i in range(count)]))
    total = arrived[0]
    for part in arrived[1:]:
        total = total + part
    gathered = [total]
    for step in range(1, count):
        gathered.append(lax.ppermute(total, "dim", [(i, (i + step) % count) for i in range(count)]))
    return gathered


def own_distance_kernel(*refs):
    shard_refs, (distance_ref, sum_ref) = refs[:-2], refs[-2:]
    read_shards(shard_refs, distance_ref)
    rows = distance_ref.shape[0]
    down = lax.broadcasted_iota(jnp.int32, (rows, rows), 0)
    across = lax.broadcasted_iota(jnp.int32, (rows, rows), 1)
    distance = jnp.where(down == across, 0.0, distance_ref[...])
    distance_ref[...] = distance
    sum_ref[...] = jnp.broadcast_to(jnp.sum(distance), sum_ref.shape)


def own_distance(shards):
    rows = shards[0].shape[1]
    return pl.pallas_call(
        own_distance_kernel,
        out_shape=[f32(rows, rows), f32(8, 128)],
        compiler_params=params(),
        name="own_distance",
    )(*shards)


def weights_kernel(scale_base, *refs):
    own_ref, own_sum, other_sum = refs[:3]
    shard_refs = refs[3:-7]
    own_hi, own_lo, pair_hi, pair_lo, weight_ref, half_ref, pair_ref = refs[-7:]
    read_shards(shard_refs, pair_ref)
    pair = pair_ref[...]
    rows = pair.shape[0]
    spread = jnp.sum(pair) * 2.0 + jnp.sum(own_sum[0:1, 0:1] + other_sum[0:1, 0:1])
    width = jnp.full((1, 1), spread / scale_base, jnp.float32)
    inverse = -1.0 / width
    down = lax.broadcasted_iota(jnp.int32, (rows, rows), 0)
    across = lax.broadcasted_iota(jnp.int32, (rows, rows), 1)
    own_weights = jnp.where(down == across, 0.0, jnp.exp(own_ref[...] * inverse))
    pair_weights = jnp.exp(pair * inverse)
    own_hi[...], own_lo[...] = split(own_weights)
    pair_hi[...], pair_lo[...] = split(pair_weights)
    weight = jnp.sum(own_weights, axis=1, keepdims=True) + jnp.sum(pair_weights, axis=1, keepdims=True)
    weight_ref[...] = jnp.broadcast_to(weight, weight_ref.shape)
    half_ref[...] = jnp.broadcast_to(0.5 * width, half_ref.shape)


def weights_part(own, own_sum, other_sum, shards, scale_base):
    rows = own.shape[0]
    half = jax.ShapeDtypeStruct((rows, rows), jnp.bfloat16)
    return pl.pallas_call(
        functools.partial(weights_kernel, scale_base),
        out_shape=[half, half, half, half, f32(rows, 128), f32(8, 128)],
        scratch_shapes=[pltpu.VMEM((rows, rows), jnp.float32)],
        compiler_params=params(),
        name="kernel_weights",
    )(own, own_sum, other_sum, *shards)


def velocity_kernel(x_ref, s_ref, other_x, other_s, own_hi, own_lo, pair_hi, pair_lo, weight_ref, half_ref, *refs):
    out_ref = refs[-1]
    half = half_ref[0:1, 0:1]
    x = x_ref[...]
    driven = half * s_ref[...]
    hi, lo = split(driven - x)
    out = driven + weight_ref[:, 0:1] * x
    out = out + nn_dot(own_hi[...], hi) + nn_dot(own_hi[...], lo) + nn_dot(own_lo[...], hi)
    hi, lo = split(half * other_s[...] - other_x[...])
    out = out + nn_dot(pair_hi[...], hi) + nn_dot(pair_hi[...], lo) + nn_dot(pair_lo[...], hi)
    out_ref[...] = out


def velocity_part(particles, scores, visitor, visitor_scores, weights, earlier, chunk, chunks):
    rows, columns = particles.shape
    width = columns // chunks
    tile = min(TILE, width)
    tiles = width // tile
    offset = chunk * tiles
    mine = pl.BlockSpec((rows, tile), lambda i: (0, offset + i))
    other = pl.BlockSpec((rows, tile), lambda i: (0, i))
    before = [] if earlier is None else [earlier]
    operands = [particles, scores, visitor, visitor_scores, *weights, *before]
    return pl.pallas_call(
        velocity_kernel,
        grid=(tiles,),
        in_specs=[mine, mine, other, other] + [whole(w) for w in weights] + [pl.BlockSpec(memory_space=pl.ANY)] * len(before),
        out_specs=mine,
        out_shape=f32(rows, columns),
        input_output_aliases={len(operands) - 1: 0} if before else {},
        compiler_params=params(),
        cost_estimate=pl.CostEstimate(flops=12 * rows * rows * width, bytes_accessed=20 * rows * width, transcendentals=0),
        name="velocity",
    )(*operands)


def cut_kernel(width, *refs):
    source, outs, sems = refs[0], refs[1:-1], refs[-1]
    copies = [
        pltpu.make_async_copy(source.at[:, pl.ds(c * width, width)], out, sems.at[c]) for c, out in enumerate(outs)
    ]
    for copy in copies:
        copy.start()
    for copy in copies:
        copy.wait()


def cut(array, chunks):
    rows, columns = array.shape
    width = columns // chunks
    return pl.pallas_call(
        functools.partial(cut_kernel, width),
        in_specs=[pl.BlockSpec(memory_space=pl.ANY)],
        out_specs=[pl.BlockSpec(memory_space=pl.ANY)] * chunks,
        out_shape=[f32(rows, width)] * chunks,
        scratch_shapes=[pltpu.SemaphoreType.DMA((chunks,))],
        compiler_params=params(),
        cost_estimate=pl.CostEstimate(flops=0, bytes_accessed=8 * rows * columns, transcendentals=0),
        name="cut_scores",
    )(array)


def swap(array):
    return lax.ppermute(array, "blk", [(0, 1), (1, 0)])


def body(particles, scores):
    rows, columns = particles.shape
    count = lax.axis_size("dim")
    total_rows = rows * lax.axis_size("blk")
    scale_base = total_rows * total_rows * math.log(total_rows)

    visitors, carried = [], []
    for chunk in range(CHUNKS):
        copy, carried, shards = own_part(particles, carried, chunk, CHUNKS, count)
        visitors.append(swap(copy))
    own_squares = carried[2]
    visitor_scores = [swap(part) for part in cut(scores, CHUNKS)]

    own, own_sum = own_distance(exchange(shards))
    cross = [((d, b), ((d + 1) % count, 1 - b)) for d in range(count) for b in range(2)]
    other_sum = lax.ppermute(own_sum, ("dim", "blk"), [(d * 2 + b, e * 2 + f) for (d, b), (e, f) in cross])

    carried = []
    for chunk in range(CHUNKS):
        carried, shards = pair_part(particles, visitors[chunk], own_squares, carried, chunk, CHUNKS, count)
    weights = weights_part(own, own_sum, other_sum, exchange(shards), scale_base)

    velocity = None
    for chunk in range(CHUNKS):
        velocity = velocity_part(particles, scores, visitors[chunk], visitor_scores[chunk], weights, velocity, chunk, CHUNKS)
    return velocity


def solution(mesh):
    return jax.shard_map(
        body,
        mesh=mesh,
        in_specs=(P(("grp", "blk"), "dim"), P(("grp", "blk"), "dim")),
        out_specs=P(("grp", "blk"), "dim"),
        check_vma=False,
    )
```

```python
import math

import jax
import jax.numpy as jnp
from jax import lax
from jax.sharding import PartitionSpec as P


def dot3(left, right):
    return jnp.dot(left, right, precision=lax.Precision.HIGH, preferred_element_type=jnp.float32)


def total_over_dim(block):
    count = lax.axis_size("dim")
    rows, columns = block.shape
    parts = block.reshape(count, rows // count, columns)
    arrived = lax.all_to_all(parts, "dim", 0, 0)
    total = jnp.sum(arrived, axis=0)
    copies = jnp.broadcast_to(total[None], arrived.shape)
    return lax.all_to_all(copies, "dim", 0, 0).reshape(rows, columns)


def swap(array):
    return lax.ppermute(array, "blk", [(0, 1), (1, 0)])


def body(particles, scores):
    rows = particles.shape[0]
    count = lax.axis_size("dim")
    total_rows = rows * lax.axis_size("blk")
    scale_base = total_rows * total_rows * math.log(total_rows)

    visitor = swap(particles)
    visitor_scores = swap(scores)

    diagonal = lax.broadcasted_iota(jnp.int32, (rows, rows), 0) == lax.broadcasted_iota(jnp.int32, (rows, rows), 1)
    norms = jnp.sum(particles * particles, axis=1)
    own = norms[:, None] + norms[None, :] - 2.0 * dot3(particles, particles.T)
    own = total_over_dim(jnp.where(diagonal, norms[:, None], own))
    norms = jnp.sum(jnp.where(diagonal, own, 0.0), axis=1)
    own = jnp.where(diagonal, 0.0, own)
    summary = jnp.stack([norms, jnp.full((rows,), jnp.sum(own))])
    across = [(d * 2 + b, (d + 1) % count * 2 + 1 - b) for d in range(count) for b in range(2)]
    other = lax.ppermute(summary, ("dim", "blk"), across)

    visitor, other = lax.optimization_barrier((visitor, other))
    gram = total_over_dim(dot3(particles, visitor.T))
    pair = norms[:, None] + other[0][None, :] - 2.0 * gram

    width = (summary[1, 0] + other[1, 0] + 2.0 * jnp.sum(pair)) / scale_base
    own_weights = jnp.where(diagonal, 0.0, jnp.exp(-own / width))
    pair_weights = jnp.exp(-pair / width)
    weight = jnp.sum(own_weights, axis=1) + jnp.sum(pair_weights, axis=1)
    half = 0.5 * width
    weights = jnp.concatenate([own_weights, pair_weights], axis=1)
    moved = jnp.concatenate([half * scores - particles, half * visitor_scores - visitor], axis=0)
    return half * scores + particles * weight[:, None] + dot3(weights, moved)


def solution(mesh):
    return jax.shard_map(
        body,
        mesh=mesh,
        in_specs=(P(("grp", "blk"), "dim"), P(("grp", "blk"), "dim")),
        out_specs=P(("grp", "blk"), "dim"),
        check_vma=False,
    )
```

```python
import functools
import math

import jax
import jax.numpy as jnp
from jax import lax
from jax.experimental import pallas as pl
from jax.experimental.pallas import tpu as pltpu
from jax.sharding import PartitionSpec as P

GRAM_TILE = 2048
VELOCITY_TILE = 1024
MIB = 1024 * 1024


def params(limit):
    return pltpu.CompilerParams(vmem_limit_bytes=limit * MIB)


def split(x):
    hi = x.astype(jnp.bfloat16)
    lo = (x - hi.astype(jnp.float32)).astype(jnp.bfloat16)
    return hi, lo


def nt_dot(left, right):
    return lax.dot_general(left, right, (((1,), (1,)), ((), ())), preferred_element_type=jnp.float32)


def nn_dot(left, right):
    return jnp.dot(left, right, preferred_element_type=jnp.float32)


def lane_sums(values):
    total = values[:, :128]
    for start in range(128, values.shape[1], 128):
        total = total + values[:, start:start + 128]
    return total


def whole(array):
    return pl.BlockSpec(array.shape, lambda i: (0,) * len(array.shape))


def f32(*shape):
    return jax.ShapeDtypeStruct(shape, jnp.float32)


def on_diagonal(rows):
    return lax.broadcasted_iota(jnp.int32, (rows, rows), 0) == lax.broadcasted_iota(jnp.int32, (rows, rows), 1)


def own_kernel(x_ref, out_ref, gram_ref, squares_ref):
    @pl.when(pl.program_id(0) == 0)
    def _():
        gram_ref[...] = jnp.zeros_like(gram_ref)
        squares_ref[...] = jnp.zeros_like(squares_ref)

    x = x_ref[...]
    hi, lo = split(x)
    gram_ref[...] += nt_dot(jnp.concatenate([hi, lo], axis=0), hi)
    squares_ref[...] += lane_sums(x * x)

    @pl.when(pl.program_id(0) == pl.num_programs(0) - 1)
    def _():
        rows = out_ref.shape[0]
        mixed = gram_ref[rows:, :]
        gram = gram_ref[:rows, :] + mixed + mixed.T
        norms = jnp.sum(squares_ref[...], axis=1, keepdims=True)
        out_ref[...] = jnp.where(on_diagonal(rows), norms, norms + norms.T - 2.0 * gram)


def own_part(particles):
    rows, columns = particles.shape
    tile = min(GRAM_TILE, columns)
    out = f32(rows, rows)
    return pl.pallas_call(
        own_kernel,
        grid=(columns // tile,),
        in_specs=[pl.BlockSpec((rows, tile), lambda i: (0, i))],
        out_specs=whole(out),
        out_shape=out,
        scratch_shapes=[pltpu.VMEM((2 * rows, rows), jnp.float32), pltpu.VMEM((rows, 128), jnp.float32)],
        compiler_params=params(20),
        cost_estimate=pl.CostEstimate(flops=4 * rows * rows * columns, bytes_accessed=4 * rows * columns, transcendentals=0),
        name="own_gram",
    )(particles)


def pair_kernel(mine_ref, other_ref, gram_ref):
    @pl.when(pl.program_id(0) == 0)
    def _():
        gram_ref[...] = jnp.zeros_like(gram_ref)

    rows = gram_ref.shape[0]
    my_hi, my_lo = split(mine_ref[...])
    hi, lo = split(other_ref[...])
    both = nt_dot(jnp.concatenate([my_hi, my_lo], axis=0), hi)
    gram_ref[...] += both[:rows] + both[rows:] + nt_dot(my_hi, lo)


def pair_part(particles, visitor):
    rows, columns = particles.shape
    tile = min(GRAM_TILE, columns)
    out = f32(rows, rows)
    block = pl.BlockSpec((rows, tile), lambda i: (0, i))
    return pl.pallas_call(
        pair_kernel,
        grid=(columns // tile,),
        in_specs=[block, block],
        out_specs=whole(out),
        out_shape=out,
        compiler_params=params(24),
        cost_estimate=pl.CostEstimate(flops=6 * rows * rows * columns, bytes_accessed=8 * rows * columns, transcendentals=0),
        name="pair_gram",
    )(particles, visitor)


def sum_kernel(arrived_ref, out_ref):
    total = arrived_ref[0]
    for step in range(1, arrived_ref.shape[0]):
        total = total + arrived_ref[step]
    for step in range(out_ref.shape[0]):
        out_ref[step] = total


def summed_shards(block):
    count = lax.axis_size("dim")
    rows, columns = block.shape
    arrived = lax.all_to_all(block.reshape(count, rows // count, columns), "dim", 0, 0)
    return pl.pallas_call(sum_kernel, out_shape=f32(*arrived.shape), compiler_params=params(8), name="sum_shards")(arrived)


def gathered(copies):
    count, rows, columns = copies.shape
    return lax.all_to_all(copies, "dim", 0, 0).reshape(count * rows, columns)


def summary_kernel(own_ref, out_ref):
    own = own_ref[...]
    rows = own.shape[0]
    diagonal = on_diagonal(rows)
    norms = jnp.sum(jnp.where(diagonal, own, 0.0), axis=0, keepdims=True)
    total = jnp.sum(jnp.where(diagonal, 0.0, own))
    out_ref[...] = jnp.concatenate([norms, jnp.full((7, rows), total)], axis=0)


def summary_part(own):
    return pl.pallas_call(summary_kernel, out_shape=f32(8, own.shape[0]), compiler_params=params(8), name="summary")(own)


def weights_kernel(scale_base, own_ref, summary_ref, other_ref, gram_ref, hi_ref, lo_ref, weight_ref, half_ref):
    own = own_ref[...]
    rows = own.shape[0]
    diagonal = on_diagonal(rows)
    norms = jnp.sum(jnp.where(diagonal, own, 0.0), axis=1, keepdims=True)
    pair = norms + other_ref[0:1, :] - 2.0 * gram_ref[...]
    spread = summary_ref[1:2, 0:1] + other_ref[1:2, 0:1] + 2.0 * jnp.sum(pair)
    width = spread / scale_base
    inverse = -1.0 / width
    own_weights = jnp.where(diagonal, 0.0, jnp.exp(own * inverse))
    pair_weights = jnp.exp(pair * inverse)
    weights = jnp.concatenate([own_weights, pair_weights], axis=1)
    hi_ref[...], lo_ref[...] = split(weights)
    weight_ref[...] = jnp.broadcast_to(jnp.sum(weights, axis=1, keepdims=True), weight_ref.shape)
    half_ref[...] = jnp.broadcast_to(0.5 * width, half_ref.shape)


def weights_part(own, summary, other, gram, scale_base):
    rows = own.shape[0]
    half = jax.ShapeDtypeStruct((rows, 2 * rows), jnp.bfloat16)
    return pl.pallas_call(
        functools.partial(weights_kernel, scale_base),
        out_shape=[half, half, f32(rows, 128), f32(8, 128)],
        compiler_params=params(12),
        name="kernel_weights",
    )(own, summary, other, gram)


def velocity_kernel(x_ref, s_ref, other_x, other_s, hi_ref, lo_ref, weight_ref, half_ref, out_ref):
    half = half_ref[0:1, 0:1]
    x = x_ref[...]
    driven = half * s_ref[...]
    moved_hi, moved_lo = split(jnp.concatenate([driven - x, half * other_s[...] - other_x[...]], axis=0))
    hi = hi_ref[...]
    left = jnp.concatenate([hi, hi, lo_ref[...]], axis=1)
    right = jnp.concatenate([moved_hi, moved_lo, moved_hi], axis=0)
    out_ref[...] = driven + weight_ref[:, 0:1] * x + nn_dot(left, right)


def velocity_part(particles, scores, visitor, visitor_scores, weights):
    rows, columns = particles.shape
    tile = min(VELOCITY_TILE, columns)
    block = pl.BlockSpec((rows, tile), lambda i: (0, i))
    return pl.pallas_call(
        velocity_kernel,
        grid=(columns // tile,),
        in_specs=[block] * 4 + [whole(w) for w in weights],
        out_specs=block,
        out_shape=f32(rows, columns),
        compiler_params=params(28),
        cost_estimate=pl.CostEstimate(flops=12 * rows * rows * columns, bytes_accessed=20 * rows * columns, transcendentals=0),
        name="velocity",
    )(particles, scores, visitor, visitor_scores, *weights)


def swap(array):
    return lax.ppermute(array, "blk", [(0, 1), (1, 0)])


def body(particles, scores):
    count = lax.axis_size("dim")
    total_rows = particles.shape[0] * lax.axis_size("blk")
    scale_base = total_rows * total_rows * math.log(total_rows)

    visitor = swap(particles)
    visitor_scores = swap(scores)

    own_copies = summed_shards(own_part(particles))
    visitor, own_copies = lax.optimization_barrier((visitor, own_copies))
    own = gathered(own_copies)
    summary = summary_part(own)
    across = [(d * 2 + b, (d + 1) % count * 2 + 1 - b) for d in range(count) for b in range(2)]
    other = lax.ppermute(summary, ("dim", "blk"), across)

    gram = pair_part(particles, visitor)
    gram, summary = lax.optimization_barrier((gram, summary))
    gram = gathered(summed_shards(gram))
    weights = weights_part(own, summary, other, gram, scale_base)
    return velocity_part(particles, scores, visitor, visitor_scores, weights)


def solution(mesh):
    return jax.shard_map(
        body,
        mesh=mesh,
        in_specs=(P(("grp", "blk"), "dim"), P(("grp", "blk"), "dim")),
        out_specs=P(("grp", "blk"), "dim"),
        check_vma=False,
    )
```

```python
import functools
import math

import jax
import jax.numpy as jnp
from jax import lax
from jax.experimental import pallas as pl
from jax.experimental.pallas import tpu as pltpu
from jax.sharding import PartitionSpec as P

GRAM_TILE = 2048
VELOCITY_TILE = 1024
CHUNKS = 4
MIB = 1024 * 1024
BOTH = ("dim", "blk")


def params(limit):
    return pltpu.CompilerParams(vmem_limit_bytes=limit * MIB)


def small_cost():
    return pl.CostEstimate(flops=1024, bytes_accessed=1024, transcendentals=0)


def split(x):
    hi = x.astype(jnp.bfloat16)
    lo = (x - hi.astype(jnp.float32)).astype(jnp.bfloat16)
    return hi, lo


def nt_dot(left, right):
    return lax.dot_general(left, right, (((1,), (1,)), ((), ())), preferred_element_type=jnp.float32)


def nn_dot(left, right):
    return jnp.dot(left, right, preferred_element_type=jnp.float32)


def lane_sums(values):
    total = values[:, :128]
    for start in range(128, values.shape[1], 128):
        total = total + values[:, start:start + 128]
    return total


def whole(array):
    return pl.BlockSpec(array.shape, lambda i, core: (0,) * len(array.shape))


def f32(*shape):
    return jax.ShapeDtypeStruct(shape, jnp.float32)


def on_diagonal(rows):
    return lax.broadcasted_iota(jnp.int32, (rows, rows), 0) == lax.broadcasted_iota(jnp.int32, (rows, rows), 1)


def call(kernel, name, grid, in_specs, out_specs, out_shape, limit, scratch=(), aliases=None):
    return pl.pallas_call(
        kernel,
        grid_spec=pltpu.PrefetchScalarGridSpec(
            num_scalar_prefetch=1, grid=grid, in_specs=in_specs, out_specs=out_specs, scratch_shapes=list(scratch)
        ),
        out_shape=out_shape,
        input_output_aliases=aliases or {},
        compiler_params=params(limit),
        cost_estimate=small_cost(),
        name=name,
    )


def own_kernel(first, core_ref, *refs):
    refs = list(refs)
    x_ref = refs.pop(0)
    gram_in, squares_in = (None, None) if first else (refs.pop(0), refs.pop(0))
    if first:
        copy_ref, gram_ref, squares_ref = refs
    else:
        out_ref, gram_ref, squares_ref = refs

    @pl.when(pl.program_id(0) == 0)
    def _():
        gram_ref[...] = jnp.zeros_like(gram_ref) if first else gram_in[...]
        squares_ref[...] = jnp.zeros_like(squares_ref) if first else squares_in[...]

    x = x_ref[...]
    if first:
        copy_ref[...] = x
    hi, lo = split(x)
    gram_ref[...] += nt_dot(jnp.concatenate([hi, lo], axis=0), hi)
    squares_ref[...] += lane_sums(x * x)

    if not first:
        @pl.when(pl.program_id(0) == pl.num_programs(0) - 1)
        def _():
            rows = out_ref.shape[0]
            mixed = gram_ref[rows:, :]
            gram = gram_ref[:rows, :] + mixed + mixed.T
            norms = jnp.sum(squares_ref[...], axis=1, keepdims=True)
            out_ref[...] = jnp.where(on_diagonal(rows), norms, norms + norms.T - 2.0 * gram)


def own_sent(core, particles):
    rows, columns = particles.shape
    width = columns // 2
    tile = min(GRAM_TILE, width)
    tiles = width // tile
    outs = [f32(rows, width), f32(2 * rows, rows), f32(rows, 128)]
    return call(
        functools.partial(own_kernel, True),
        "own_gram_sent",
        (tiles,),
        [pl.BlockSpec((rows, tile), lambda i, core: (0, (1 - core[0]) * tiles + i))],
        [pl.BlockSpec((rows, tile), lambda i, core: (0, i)), whole(outs[1]), whole(outs[2])],
        outs,
        52,
    )(core, particles)


def own_kept(core, particles, gram, squares):
    rows, columns = particles.shape
    width = columns // 2
    tile = min(GRAM_TILE, width)
    tiles = width // tile
    out = f32(rows, rows)
    return call(
        functools.partial(own_kernel, False),
        "own_gram_kept",
        (tiles,),
        [pl.BlockSpec((rows, tile), lambda i, core: (0, core[0] * tiles + i)), whole(gram), whole(squares)],
        whole(out),
        out,
        52,
        scratch=[pltpu.VMEM((2 * rows, rows), jnp.float32), pltpu.VMEM((rows, 128), jnp.float32)],
    )(core, particles, gram, squares)


def copy_kernel(core_ref, source_ref, out_ref):
    out_ref[...] = source_ref[...]


def sent_half(core, array):
    rows, columns = array.shape
    width = columns // 2
    tile = min(GRAM_TILE, width)
    tiles = width // tile
    return call(
        copy_kernel,
        "sent_half",
        (tiles,),
        [pl.BlockSpec((rows, tile), lambda i, core: (0, (1 - core[0]) * tiles + i))],
        pl.BlockSpec((rows, tile), lambda i, core: (0, i)),
        f32(rows, width),
        52,
    )(core, array)


def pair_kernel(core_ref, mine_ref, other_ref, out_ref, gram_ref):
    @pl.when(pl.program_id(0) == 0)
    def _():
        gram_ref[...] = jnp.zeros_like(gram_ref)

    rows = gram_ref.shape[0]
    my_hi, my_lo = split(mine_ref[...])
    hi, lo = split(other_ref[...])
    both = nt_dot(jnp.concatenate([my_hi, my_lo], axis=0), hi)
    gram_ref[...] += both[:rows] + both[rows:] + nt_dot(my_hi, lo)

    @pl.when(pl.program_id(0) == pl.num_programs(0) - 1)
    def _():
        gram = gram_ref[...]
        out_ref[...] = jnp.where(core_ref[0] == 0, gram, gram.T)


def pair_part(core, particles, visitor):
    rows, width = visitor.shape
    tile = min(GRAM_TILE, width)
    tiles = width // tile
    out = f32(rows, rows)
    return call(
        pair_kernel,
        "pair_gram",
        (tiles,),
        [
            pl.BlockSpec((rows, tile), lambda i, core: (0, core[0] * tiles + i)),
            pl.BlockSpec((rows, tile), lambda i, core: (0, i)),
        ],
        whole(out),
        out,
        40,
        scratch=[pltpu.VMEM((rows, rows), jnp.float32)],
    )(core, particles, visitor)


def sum_kernel(arrived_ref, out_ref):
    total = arrived_ref[0]
    for step in range(1, arrived_ref.shape[0]):
        total = total + arrived_ref[step]
    for step in range(out_ref.shape[0]):
        out_ref[step] = total


def summed_shards(block, axes, copies):
    count = lax.axis_size(axes)
    rows, columns = block.shape
    arrived = lax.all_to_all(block.reshape(count, rows // count, columns), axes, 0, 0)
    return pl.pallas_call(
        sum_kernel,
        out_shape=f32(copies, rows // count, columns),
        compiler_params=params(8),
        cost_estimate=small_cost(),
        name="sum_shards",
    )(arrived)


def weights_kernel(scale_base, core_ref, blocks_ref, gram_ref, hi_ref, lo_ref, weight_ref, half_ref, own_ref, other_ref):
    core = core_ref[0]
    rows = gram_ref.shape[0]
    step = blocks_ref.shape[1]
    for d in range(blocks_ref.shape[0] // 2):
        own_ref[d * step:(d + 1) * step, :] = blocks_ref[2 * d + core]
        other_ref[d * step:(d + 1) * step, :] = blocks_ref[2 * d + 1 - core]
    own, other, gram = own_ref[...], other_ref[...], gram_ref[...]
    diagonal = on_diagonal(rows)
    gram = jnp.where(core == 0, gram, gram.T)
    norms = jnp.sum(jnp.where(diagonal, own, 0.0), axis=1, keepdims=True)
    others = jnp.sum(jnp.where(diagonal, other, 0.0), axis=0, keepdims=True)
    pair = norms + others - 2.0 * gram
    own = jnp.where(diagonal, 0.0, own)
    other = jnp.where(diagonal, 0.0, other)
    spread = jnp.sum(own) + jnp.sum(other) + 2.0 * jnp.sum(pair)
    width = jnp.full((1, 1), spread, jnp.float32) / scale_base
    inverse = -1.0 / width
    own = jnp.where(diagonal, 0.0, jnp.exp(own * inverse))
    other = jnp.where(diagonal, 0.0, jnp.exp(other * inverse))
    pair = jnp.exp(pair * inverse)
    weights = jnp.concatenate(
        [jnp.concatenate([own, pair], axis=1), jnp.concatenate([pair.T, other], axis=1)], axis=0
    )
    hi_ref[...], lo_ref[...] = split(weights)
    weight_ref[...] = jnp.broadcast_to(jnp.sum(weights, axis=1, keepdims=True), weight_ref.shape)
    half_ref[...] = jnp.broadcast_to(0.5 * width, half_ref.shape)


def weights_part(core, blocks, gram, scale_base):
    rows = gram.shape[0]
    half = jax.ShapeDtypeStruct((2 * rows, 2 * rows), jnp.bfloat16)
    outs = [half, half, f32(2 * rows, 128), f32(8, 128)]
    return call(
        functools.partial(weights_kernel, scale_base),
        "kernel_weights",
        (1,),
        [whole(blocks), whole(gram)],
        [whole(o) for o in outs],
        outs,
        48,
        scratch=[pltpu.VMEM((rows, rows), jnp.float32)] * 2,
    )(core, blocks, gram)


def velocity_kernel(core_ref, x_ref, s_ref, other_x, other_s, hi_ref, lo_ref, weight_ref, half_ref, *refs):
    out_ref, sent_ref = refs[-2:]
    rows = x_ref.shape[0]
    half = half_ref[0:1, 0:1]
    x = jnp.concatenate([x_ref[...], other_x[...]], axis=0)
    driven = half * jnp.concatenate([s_ref[...], other_s[...]], axis=0)
    moved_hi, moved_lo = split(driven - x)
    hi = hi_ref[...]
    both = nn_dot(jnp.concatenate([hi, lo_ref[...]], axis=0), moved_hi)
    out = driven + weight_ref[:, 0:1] * x + both[:2 * rows] + both[2 * rows:] + nn_dot(hi, moved_lo)
    out_ref[...] = out[:rows]
    sent_ref[...] = out[rows:]


def velocity_part(core, particles, scores, visitor, visitor_scores, weights, earlier, chunk):
    rows, columns = particles.shape
    half = columns // 2
    width = half // CHUNKS
    tile = min(VELOCITY_TILE, width)
    tiles = width // tile
    start = chunk * tiles
    mine = pl.BlockSpec((rows, tile), lambda i, core: (0, core[0] * (half // tile) + start + i))
    other = pl.BlockSpec((rows, tile), lambda i, core: (0, start + i))
    before = [] if earlier is None else [earlier]
    operands = [core, particles, scores, visitor, visitor_scores, *weights, *before]
    return call(
        velocity_kernel,
        "velocity",
        (tiles,),
        [mine, mine, other, other] + [whole(w) for w in weights] + [pl.BlockSpec(memory_space=pl.ANY)] * len(before),
        [mine, pl.BlockSpec((rows, tile), lambda i, core: (0, i))],
        [f32(rows, columns), f32(rows, width)],
        40,
        aliases={len(operands) - 1: 0} if before else None,
    )(*operands)


def place_kernel(core_ref, part_ref, earlier_ref, out_ref):
    out_ref[...] = part_ref[...]


def place(core, part, earlier, chunk):
    rows, columns = earlier.shape
    half = columns // 2
    width = part.shape[1]
    tile = min(VELOCITY_TILE, width)
    start = chunk * (width // tile)
    return call(
        place_kernel,
        "place",
        (width // tile,),
        [pl.BlockSpec((rows, tile), lambda i, core: (0, i)), pl.BlockSpec(memory_space=pl.ANY)],
        pl.BlockSpec((rows, tile), lambda i, core: (0, (1 - core[0]) * (half // tile) + start + i)),
        f32(rows, columns),
        40,
        aliases={2: 0},
    )(core, part, earlier)


def swap(array):
    return lax.ppermute(array, "blk", [(0, 1), (1, 0)])


def body(particles, scores):
    total_rows = particles.shape[0] * lax.axis_size("blk")
    scale_base = total_rows * total_rows * math.log(total_rows)
    devices = lax.axis_size(BOTH)
    core = lax.axis_index("blk").reshape(1)

    copy, gram, squares = own_sent(core, particles)
    visitor = swap(copy)
    own = own_kept(core, particles, gram, squares)
    scores_late, _ = lax.optimization_barrier((scores, own))
    visitor_scores = swap(sent_half(core, scores_late))

    own_copies = summed_shards(own, "dim", devices)
    visitor, own_copies = lax.optimization_barrier((visitor, own_copies))
    blocks = lax.all_to_all(own_copies, BOTH, 0, 0)

    gram, blocks = lax.optimization_barrier((pair_part(core, particles, visitor), blocks))
    gram_copies = summed_shards(gram, BOTH, devices)
    gram = lax.all_to_all(gram_copies, BOTH, 0, 0).reshape(own.shape)
    weights = weights_part(core, blocks, gram, scale_base)

    velocity, parts = None, []
    for chunk in range(CHUNKS):
        velocity, part = velocity_part(core, particles, scores, visitor, visitor_scores, weights, velocity, chunk)
        parts.append(swap(part))
    for chunk in range(CHUNKS):
        velocity = place(core, parts[chunk], velocity, chunk)
    return velocity


def solution(mesh):
    return jax.shard_map(
        body,
        mesh=mesh,
        in_specs=(P(("grp", "blk"), "dim"), P(("grp", "blk"), "dim")),
        out_specs=P(("grp", "blk"), "dim"),
        check_vma=False,
    )
```

```python
import functools
import math

import jax
import jax.numpy as jnp
from jax import lax
from jax.experimental import pallas as pl
from jax.experimental.pallas import tpu as pltpu
from jax.sharding import PartitionSpec as P

GRAM_TILE = 2048
VELOCITY_TILE = 1024
MIB = 1024 * 1024


def params(limit):
    return pltpu.CompilerParams(vmem_limit_bytes=limit * MIB)


def split(x):
    hi = x.astype(jnp.bfloat16)
    lo = (x - hi.astype(jnp.float32)).astype(jnp.bfloat16)
    return hi, lo


def nt_dot(left, right):
    return lax.dot_general(left, right, (((1,), (1,)), ((), ())), preferred_element_type=jnp.float32)


def nn_dot(left, right):
    return jnp.dot(left, right, preferred_element_type=jnp.float32)


def lane_sums(values):
    total = values[:, :128]
    for start in range(128, values.shape[1], 128):
        total = total + values[:, start:start + 128]
    return total


def whole(array):
    return pl.BlockSpec(array.shape, lambda i: (0,) * len(array.shape))


def f32(*shape):
    return jax.ShapeDtypeStruct(shape, jnp.float32)


def on_diagonal(rows):
    return lax.broadcasted_iota(jnp.int32, (rows, rows), 0) == lax.broadcasted_iota(jnp.int32, (rows, rows), 1)


def strips(rows, columns):
    for column in range(0, columns, 256):
        for row in range(0, rows, 32):
            yield slice(row, row + 32), slice(column, column + 256)


def below(where, rows):
    return slice(where.start + rows, where.stop + rows)


def own_kernel(x_ref, out_ref, halves_ref, gram_ref, squares_ref):
    rows, columns = x_ref.shape

    @pl.when(pl.program_id(0) == 0)
    def _():
        gram_ref[...] = jnp.zeros_like(gram_ref)
        squares_ref[...] = jnp.zeros_like(squares_ref)

    for row, column in strips(rows, columns):
        x = x_ref[row, column]
        hi, lo = split(x)
        halves_ref[row, column] = hi
        halves_ref[below(row, rows), column] = lo
        squares_ref[row, :] += lane_sums(x * x)
    gram_ref[...] += nt_dot(halves_ref[...], halves_ref[:rows, :])

    @pl.when(pl.program_id(0) == pl.num_programs(0) - 1)
    def _():
        mixed = gram_ref[rows:, :]
        gram = gram_ref[:rows, :] + mixed + mixed.T
        norms = jnp.sum(squares_ref[...], axis=1, keepdims=True)
        out_ref[...] = jnp.where(on_diagonal(rows), norms, norms + norms.T - 2.0 * gram)


def own_part(particles):
    rows, columns = particles.shape
    tile = min(GRAM_TILE, columns)
    out = f32(rows, rows)
    return pl.pallas_call(
        own_kernel,
        grid=(columns // tile,),
        in_specs=[pl.BlockSpec((rows, tile), lambda i: (0, i))],
        out_specs=whole(out),
        out_shape=out,
        scratch_shapes=[
            pltpu.VMEM((2 * rows, tile), jnp.bfloat16),
            pltpu.VMEM((2 * rows, rows), jnp.float32),
            pltpu.VMEM((rows, 128), jnp.float32),
        ],
        compiler_params=params(52),
        cost_estimate=pl.CostEstimate(flops=4 * rows * rows * columns, bytes_accessed=4 * rows * columns, transcendentals=0),
        name="own_gram",
    )(particles)


def pair_kernel(mine_ref, other_ref, gram_ref, mine_halves, other_halves):
    rows, columns = mine_ref.shape

    @pl.when(pl.program_id(0) == 0)
    def _():
        gram_ref[...] = jnp.zeros_like(gram_ref)

    for source, halves_ref in ((mine_ref, mine_halves), (other_ref, other_halves)):
        for row, column in strips(rows, columns):
            hi, lo = split(source[row, column])
            halves_ref[row, column] = hi
            halves_ref[below(row, rows), column] = lo
    both = nt_dot(mine_halves[...], other_halves[:rows, :])
    gram_ref[...] += both[:rows] + both[rows:] + nt_dot(mine_halves[:rows, :], other_halves[rows:, :])


def pair_part(particles, visitor):
    rows, columns = particles.shape
    tile = min(GRAM_TILE, columns)
    out = f32(rows, rows)
    block = pl.BlockSpec((rows, tile), lambda i: (0, i))
    return pl.pallas_call(
        pair_kernel,
        grid=(columns // tile,),
        in_specs=[block, block],
        out_specs=whole(out),
        out_shape=out,
        scratch_shapes=[
            pltpu.VMEM((2 * rows, tile), jnp.bfloat16),
            pltpu.VMEM((2 * rows, tile), jnp.bfloat16),
        ],
        compiler_params=params(52),
        cost_estimate=pl.CostEstimate(flops=6 * rows * rows * columns, bytes_accessed=8 * rows * columns, transcendentals=0),
        name="pair_gram",
    )(particles, visitor)


def sum_kernel(arrived_ref, out_ref):
    total = arrived_ref[0]
    for step in range(1, arrived_ref.shape[0]):
        total = total + arrived_ref[step]
    for step in range(out_ref.shape[0]):
        out_ref[step] = total


def summed_shards(block):
    count = lax.axis_size("dim")
    rows, columns = block.shape
    arrived = lax.all_to_all(block.reshape(count, rows // count, columns), "dim", 0, 0)
    return pl.pallas_call(sum_kernel, out_shape=f32(*arrived.shape), compiler_params=params(8), name="sum_shards")(arrived)


def gathered(copies):
    count, rows, columns = copies.shape
    return lax.all_to_all(copies, "dim", 0, 0).reshape(count * rows, columns)


def summary_kernel(own_ref, out_ref):
    own = own_ref[...]
    rows = own.shape[0]
    diagonal = on_diagonal(rows)
    norms = jnp.sum(jnp.where(diagonal, own, 0.0), axis=0, keepdims=True)
    total = jnp.sum(jnp.where(diagonal, 0.0, own))
    out_ref[...] = jnp.concatenate([norms, jnp.full((7, rows), total)], axis=0)


def summary_part(own):
    return pl.pallas_call(summary_kernel, out_shape=f32(8, own.shape[0]), compiler_params=params(8), name="summary")(own)


def weights_kernel(scale_base, own_ref, summary_ref, other_ref, gram_ref, weights_ref, weight_ref, half_ref):
    own = own_ref[...]
    rows = own.shape[0]
    diagonal = on_diagonal(rows)
    norms = jnp.sum(jnp.where(diagonal, own, 0.0), axis=1, keepdims=True)
    pair = norms + other_ref[0:1, :] - 2.0 * gram_ref[...]
    spread = summary_ref[1:2, 0:1] + other_ref[1:2, 0:1] + 2.0 * jnp.sum(pair)
    width = spread / scale_base
    inverse = -1.0 / width
    own_weights = jnp.where(diagonal, 0.0, jnp.exp(own * inverse))
    pair_weights = jnp.exp(pair * inverse)
    weights = jnp.concatenate([own_weights, pair_weights], axis=1)
    hi, lo = split(weights)
    weights_ref[...] = jnp.concatenate([hi, hi, lo], axis=1)
    weight_ref[...] = jnp.broadcast_to(jnp.sum(weights, axis=1, keepdims=True), weight_ref.shape)
    half_ref[...] = jnp.broadcast_to(0.5 * width, half_ref.shape)


def weights_part(own, summary, other, gram, scale_base):
    rows = own.shape[0]
    return pl.pallas_call(
        functools.partial(weights_kernel, scale_base),
        out_shape=[jax.ShapeDtypeStruct((rows, 6 * rows), jnp.bfloat16), f32(rows, 128), f32(32, 256)],
        compiler_params=params(12),
        name="kernel_weights",
    )(own, summary, other, gram)


def velocity_kernel(x_ref, s_ref, other_x, other_s, weights_ref, weight_ref, half_ref, out_ref, moved_ref):
    rows, columns = x_ref.shape
    half = half_ref[...]
    for column in range(0, columns, 256):
        column = slice(column, column + 256)
        for offset, sources in ((0, (x_ref, s_ref)), (rows, (other_x, other_s))):
            for row in range(0, rows, 32):
                row = slice(row, row + 32)
                hi, lo = split(half * sources[1][row, column] - sources[0][row, column])
                moved_ref[below(row, offset), column] = hi
                moved_ref[below(row, offset + 2 * rows), column] = lo
                moved_ref[below(row, offset + 4 * rows), column] = hi
        out_ref[:, column] = nn_dot(weights_ref[...], moved_ref[:, column])
        for row in range(0, rows, 32):
            row = slice(row, row + 32)
            weight = weight_ref[row, :]
            weight = jnp.concatenate([weight, weight], axis=1)
            out_ref[row, column] += half * s_ref[row, column] + weight * x_ref[row, column]


def velocity_part(particles, scores, visitor, visitor_scores, weights):
    rows, columns = particles.shape
    tile = min(VELOCITY_TILE, columns)
    block = pl.BlockSpec((rows, tile), lambda i: (0, i))
    return pl.pallas_call(
        velocity_kernel,
        grid=(columns // tile,),
        in_specs=[block] * 4 + [whole(w) for w in weights],
        out_specs=block,
        out_shape=f32(rows, columns),
        scratch_shapes=[pltpu.VMEM((6 * rows, tile), jnp.bfloat16)],
        compiler_params=params(52),
        cost_estimate=pl.CostEstimate(flops=12 * rows * rows * columns, bytes_accessed=20 * rows * columns, transcendentals=0),
        name="velocity",
    )(particles, scores, visitor, visitor_scores, *weights)


def swap(array):
    return lax.ppermute(array, "blk", [(0, 1), (1, 0)])


def body(particles, scores):
    count = lax.axis_size("dim")
    total_rows = particles.shape[0] * lax.axis_size("blk")
    scale_base = total_rows * total_rows * math.log(total_rows)

    visitor = swap(particles)
    visitor_scores = swap(scores)

    own_copies = summed_shards(own_part(particles))
    visitor, own_copies = lax.optimization_barrier((visitor, own_copies))
    own = gathered(own_copies)
    summary = summary_part(own)
    across = [(d * 2 + b, (d + 1) % count * 2 + 1 - b) for d in range(count) for b in range(2)]
    other = lax.ppermute(summary, ("dim", "blk"), across)

    gram = pair_part(particles, visitor)
    gram, summary = lax.optimization_barrier((gram, summary))
    gram = gathered(summed_shards(gram))
    weights = weights_part(own, summary, other, gram, scale_base)
    return velocity_part(particles, scores, visitor, visitor_scores, weights)


def solution(mesh):
    return jax.shard_map(
        body,
        mesh=mesh,
        in_specs=(P(("grp", "blk"), "dim"), P(("grp", "blk"), "dim")),
        out_specs=P(("grp", "blk"), "dim"),
        check_vma=False,
    )
```

```python
import functools
import math

import jax
import jax.numpy as jnp
from jax import lax
from jax.experimental import pallas as pl
from jax.experimental.pallas import tpu as pltpu
from jax.sharding import PartitionSpec as P

GRAM_TILE = 2048
VELOCITY_TILE = 1024
MIB = 1024 * 1024


def params(limit):
    return pltpu.CompilerParams(vmem_limit_bytes=limit * MIB)


def split(x):
    hi = x.astype(jnp.bfloat16)
    lo = (x - hi.astype(jnp.float32)).astype(jnp.bfloat16)
    return hi, lo


def nt_dot(left, right):
    return lax.dot_general(left, right, (((1,), (1,)), ((), ())), preferred_element_type=jnp.float32)


def nn_dot(left, right):
    return jnp.dot(left, right, preferred_element_type=jnp.float32)


def lane_sums(values):
    total = values[:, :128]
    for start in range(128, values.shape[1], 128):
        total = total + values[:, start:start + 128]
    return total


def whole(array):
    return pl.BlockSpec(array.shape, lambda i: (0,) * len(array.shape))


def f32(*shape):
    return jax.ShapeDtypeStruct(shape, jnp.float32)


def on_diagonal(rows):
    return lax.broadcasted_iota(jnp.int32, (rows, rows), 0) == lax.broadcasted_iota(jnp.int32, (rows, rows), 1)


def own_kernel(x_ref, out_ref, gram_ref, squares_ref):
    @pl.when(pl.program_id(0) == 0)
    def _():
        gram_ref[...] = jnp.zeros_like(gram_ref)
        squares_ref[...] = jnp.zeros_like(squares_ref)

    x = x_ref[...]
    hi, lo = split(x)
    gram_ref[...] += nt_dot(jnp.concatenate([hi, lo], axis=0), hi)
    squares_ref[...] += lane_sums(x * x)

    @pl.when(pl.program_id(0) == pl.num_programs(0) - 1)
    def _():
        rows = out_ref.shape[0]
        mixed = gram_ref[rows:, :]
        gram = gram_ref[:rows, :] + mixed + mixed.T
        norms = jnp.sum(squares_ref[...], axis=1, keepdims=True)
        out_ref[...] = jnp.where(on_diagonal(rows), norms, norms + norms.T - 2.0 * gram)


def own_part(particles):
    rows, columns = particles.shape
    tile = min(GRAM_TILE, columns)
    out = f32(rows, rows)
    return pl.pallas_call(
        own_kernel,
        grid=(columns // tile,),
        in_specs=[pl.BlockSpec((rows, tile), lambda i: (0, i))],
        out_specs=whole(out),
        out_shape=out,
        scratch_shapes=[pltpu.VMEM((2 * rows, rows), jnp.float32), pltpu.VMEM((rows, 128), jnp.float32)],
        compiler_params=params(52),
        cost_estimate=pl.CostEstimate(flops=4 * rows * rows * columns, bytes_accessed=4 * rows * columns, transcendentals=0),
        name="own_gram",
    )(particles)


def pair_kernel(mine_ref, other_ref, gram_ref):
    @pl.when(pl.program_id(0) == 0)
    def _():
        gram_ref[...] = jnp.zeros_like(gram_ref)

    rows = gram_ref.shape[0]
    my_hi, my_lo = split(mine_ref[...])
    hi, lo = split(other_ref[...])
    both = nt_dot(jnp.concatenate([my_hi, my_lo], axis=0), hi)
    gram_ref[...] += both[:rows] + both[rows:] + nt_dot(my_hi, lo)


def pair_part(particles, visitor):
    rows, columns = particles.shape
    tile = min(GRAM_TILE, columns)
    out = f32(rows, rows)
    block = pl.BlockSpec((rows, tile), lambda i: (0, i))
    return pl.pallas_call(
        pair_kernel,
        grid=(columns // tile,),
        in_specs=[block, block],
        out_specs=whole(out),
        out_shape=out,
        compiler_params=params(52),
        cost_estimate=pl.CostEstimate(flops=6 * rows * rows * columns, bytes_accessed=8 * rows * columns, transcendentals=0),
        name="pair_gram",
    )(particles, visitor)


def sum_kernel(arrived_ref, out_ref):
    total = arrived_ref[0]
    for step in range(1, arrived_ref.shape[0]):
        total = total + arrived_ref[step]
    for step in range(out_ref.shape[0]):
        out_ref[step] = total


def summed_shards(block, beside=None):
    count = lax.axis_size("dim")
    rows, columns = block.shape
    arrived = lax.all_to_all(block.reshape(count, rows // count, columns), "dim", 0, 0)
    if beside is not None:
        arrived, _ = lax.optimization_barrier((arrived, beside))
    return pl.pallas_call(sum_kernel, out_shape=f32(*arrived.shape), compiler_params=params(8), name="sum_shards")(arrived)


def gathered(copies):
    count, rows, columns = copies.shape
    return lax.all_to_all(copies, "dim", 0, 0).reshape(count * rows, columns)


def summary_kernel(own_ref, out_ref):
    own = own_ref[...]
    rows = own.shape[0]
    diagonal = on_diagonal(rows)
    norms = jnp.sum(jnp.where(diagonal, own, 0.0), axis=0, keepdims=True)
    total = jnp.sum(jnp.where(diagonal, 0.0, own))
    out_ref[...] = jnp.concatenate([norms, jnp.full((7, rows), total)], axis=0)


def summary_part(own):
    return pl.pallas_call(summary_kernel, out_shape=f32(8, own.shape[0]), compiler_params=params(8), name="summary")(own)


def weights_kernel(scale_base, own_ref, summary_ref, other_ref, gram_ref, hi_ref, lo_ref, weight_ref, half_ref):
    own = own_ref[...]
    rows = own.shape[0]
    diagonal = on_diagonal(rows)
    norms = jnp.sum(jnp.where(diagonal, own, 0.0), axis=1, keepdims=True)
    pair = norms + other_ref[0:1, :] - 2.0 * gram_ref[...]
    spread = summary_ref[1:2, 0:1] + other_ref[1:2, 0:1] + 2.0 * jnp.sum(pair)
    width = spread / scale_base
    inverse = -1.0 / width
    own_weights = jnp.where(diagonal, 0.0, jnp.exp(own * inverse))
    pair_weights = jnp.exp(pair * inverse)
    weights = jnp.concatenate([own_weights, pair_weights], axis=1)
    hi_ref[...], lo_ref[...] = split(weights)
    weight_ref[...] = jnp.broadcast_to(jnp.sum(weights, axis=1, keepdims=True), weight_ref.shape)
    half_ref[...] = jnp.broadcast_to(0.5 * width, half_ref.shape)


def weights_part(own, summary, other, gram, scale_base):
    rows = own.shape[0]
    half = jax.ShapeDtypeStruct((rows, 2 * rows), jnp.bfloat16)
    return pl.pallas_call(
        functools.partial(weights_kernel, scale_base),
        out_shape=[half, half, f32(rows, 128), f32(8, 128)],
        compiler_params=params(12),
        name="kernel_weights",
    )(own, summary, other, gram)


def velocity_kernel(x_ref, s_ref, other_x, other_s, hi_ref, lo_ref, weight_ref, half_ref, out_ref):
    rows = out_ref.shape[0]
    half = half_ref[0:1, 0:1]
    x = x_ref[...]
    driven = half * s_ref[...]
    moved_hi, moved_lo = split(jnp.concatenate([driven - x, half * other_s[...] - other_x[...]], axis=0))
    hi = hi_ref[...]
    both = nn_dot(jnp.concatenate([hi, lo_ref[...]], axis=0), moved_hi)
    out_ref[...] = driven + weight_ref[:, 0:1] * x + both[:rows] + both[rows:] + nn_dot(hi, moved_lo)


def velocity_part(particles, scores, visitor, visitor_scores, weights):
    rows, columns = particles.shape
    tile = min(VELOCITY_TILE, columns)
    block = pl.BlockSpec((rows, tile), lambda i: (0, i))
    return pl.pallas_call(
        velocity_kernel,
        grid=(columns // tile,),
        in_specs=[block] * 4 + [whole(w) for w in weights],
        out_specs=block,
        out_shape=f32(rows, columns),
        compiler_params=params(52),
        cost_estimate=pl.CostEstimate(flops=12 * rows * rows * columns, bytes_accessed=20 * rows * columns, transcendentals=0),
        name="velocity",
    )(particles, scores, visitor, visitor_scores, *weights)


def swap(array):
    return lax.ppermute(array, "blk", [(0, 1), (1, 0)])


def body(particles, scores):
    count = lax.axis_size("dim")
    total_rows = particles.shape[0] * lax.axis_size("blk")
    scale_base = total_rows * total_rows * math.log(total_rows)

    visitor = swap(particles)
    visitor_scores = swap(scores)

    own = gathered(summed_shards(own_part(particles)))
    summary = summary_part(own)
    across = [(d * 2 + b, (d + 1) % count * 2 + 1 - b) for d in range(count) for b in range(2)]
    other = lax.ppermute(summary, ("dim", "blk"), across)

    gram = gathered(summed_shards(pair_part(particles, visitor), other))
    weights = weights_part(own, summary, other, gram, scale_base)
    return velocity_part(particles, scores, visitor, visitor_scores, weights)


def solution(mesh):
    return jax.shard_map(
        body,
        mesh=mesh,
        in_specs=(P(("grp", "blk"), "dim"), P(("grp", "blk"), "dim")),
        out_specs=P(("grp", "blk"), "dim"),
        check_vma=False,
    )
```

```python
import functools
import math

import jax
import jax.numpy as jnp
from jax import lax
from jax.experimental import pallas as pl
from jax.experimental.pallas import tpu as pltpu
from jax.sharding import PartitionSpec as P

GRAM_TILE = 2048
VELOCITY_TILE = 2048
MIB = 1024 * 1024
BOTH = ("dim", "blk")


def params(limit):
    return pltpu.CompilerParams(vmem_limit_bytes=limit * MIB)


def split(x):
    hi = x.astype(jnp.bfloat16)
    lo = (x - hi.astype(jnp.float32)).astype(jnp.bfloat16)
    return hi, lo


def nt_dot(left, right):
    return lax.dot_general(left, right, (((1,), (1,)), ((), ())), preferred_element_type=jnp.float32)


def nn_dot(left, right):
    return jnp.dot(left, right, preferred_element_type=jnp.float32)


def lane_sums(values):
    total = values[:, :128]
    for start in range(128, values.shape[1], 128):
        total = total + values[:, start:start + 128]
    return total


def whole(array):
    return pl.BlockSpec(array.shape, lambda i: (0,) * len(array.shape))


def f32(*shape):
    return jax.ShapeDtypeStruct(shape, jnp.float32)


def on_diagonal(rows):
    return lax.broadcasted_iota(jnp.int32, (rows, rows), 0) == lax.broadcasted_iota(jnp.int32, (rows, rows), 1)


def own_kernel(x_ref, out_ref, gram_ref, squares_ref):
    @pl.when(pl.program_id(0) == 0)
    def _():
        gram_ref[...] = jnp.zeros_like(gram_ref)
        squares_ref[...] = jnp.zeros_like(squares_ref)

    x = x_ref[...]
    hi, lo = split(x)
    gram_ref[...] += nt_dot(jnp.concatenate([hi, lo], axis=0), hi)
    squares_ref[...] += lane_sums(x * x)

    @pl.when(pl.program_id(0) == pl.num_programs(0) - 1)
    def _():
        rows = out_ref.shape[0]
        mixed = gram_ref[rows:, :]
        gram = gram_ref[:rows, :] + mixed + mixed.T
        norms = jnp.sum(squares_ref[...], axis=1, keepdims=True)
        out_ref[...] = jnp.where(on_diagonal(rows), norms, norms + norms.T - 2.0 * gram)


def own_part(particles):
    rows, columns = particles.shape
    tile = min(GRAM_TILE, columns)
    out = f32(rows, rows)
    return pl.pallas_call(
        own_kernel,
        grid=(columns // tile,),
        in_specs=[pl.BlockSpec((rows, tile), lambda i: (0, i))],
        out_specs=whole(out),
        out_shape=out,
        scratch_shapes=[pltpu.VMEM((2 * rows, rows), jnp.float32), pltpu.VMEM((rows, 128), jnp.float32)],
        compiler_params=params(52),
        cost_estimate=pl.CostEstimate(flops=4 * rows * rows * columns, bytes_accessed=4 * rows * columns, transcendentals=0),
        name="own_gram",
    )(particles)


def pair_kernel(core_ref, mine_ref, other_ref, out_ref, gram_ref):
    @pl.when(pl.program_id(0) == 0)
    def _():
        gram_ref[...] = jnp.zeros_like(gram_ref)

    rows = gram_ref.shape[0]
    my_hi, my_lo = split(mine_ref[...])
    hi, lo = split(other_ref[...])
    both = nt_dot(jnp.concatenate([my_hi, my_lo], axis=0), hi)
    gram_ref[...] += both[:rows] + both[rows:] + nt_dot(my_hi, lo)

    @pl.when(pl.program_id(0) == pl.num_programs(0) - 1)
    def _():
        gram = gram_ref[...]
        out_ref[...] = jnp.where(core_ref[0] == 0, gram, gram.T)


def pair_part(core, particles, visitor):
    rows, columns = particles.shape
    width = columns // 2
    tile = min(GRAM_TILE, width)
    tiles = width // tile
    out = f32(rows, rows)
    block = pl.BlockSpec((rows, tile), lambda i, core: (0, core[0] * tiles + i))
    return pl.pallas_call(
        pair_kernel,
        grid_spec=pltpu.PrefetchScalarGridSpec(
            num_scalar_prefetch=1,
            grid=(tiles,),
            in_specs=[block, block],
            out_specs=pl.BlockSpec(out.shape, lambda i, core: (0, 0)),
            scratch_shapes=[pltpu.VMEM((rows, rows), jnp.float32)],
        ),
        out_shape=out,
        compiler_params=params(52),
        cost_estimate=pl.CostEstimate(flops=6 * rows * rows * width, bytes_accessed=8 * rows * width, transcendentals=0),
        name="pair_gram",
    )(core, particles, visitor)


def sum_kernel(arrived_ref, out_ref):
    total = arrived_ref[0]
    for step in range(1, arrived_ref.shape[0]):
        total = total + arrived_ref[step]
    for step in range(out_ref.shape[0]):
        out_ref[step] = total


def summed_shards(block, axes, beside=None):
    count = lax.axis_size(axes)
    rows, columns = block.shape
    arrived = lax.all_to_all(block.reshape(count, rows // count, columns), axes, 0, 0)
    if beside is not None:
        arrived, _ = lax.optimization_barrier((arrived, beside))
    return pl.pallas_call(sum_kernel, out_shape=f32(*arrived.shape), compiler_params=params(8), name="sum_shards")(arrived)


def gathered(copies, axes):
    count, rows, columns = copies.shape
    return lax.all_to_all(copies, axes, 0, 0).reshape(count * rows, columns)


def summary_kernel(own_ref, out_ref):
    own = own_ref[...]
    rows = own.shape[0]
    diagonal = on_diagonal(rows)
    norms = jnp.sum(jnp.where(diagonal, own, 0.0), axis=0, keepdims=True)
    total = jnp.sum(jnp.where(diagonal, 0.0, own))
    out_ref[...] = jnp.concatenate([norms, jnp.full((7, rows), total)], axis=0)


def summary_part(own):
    return pl.pallas_call(summary_kernel, out_shape=f32(8, own.shape[0]), compiler_params=params(8), name="summary")(own)


def weights_kernel(scale_base, core_ref, own_ref, summary_ref, other_ref, gram_ref, hi_ref, lo_ref, weight_ref, half_ref):
    own = own_ref[...]
    rows = own.shape[0]
    diagonal = on_diagonal(rows)
    norms = jnp.sum(jnp.where(diagonal, own, 0.0), axis=1, keepdims=True)
    gram = gram_ref[...]
    pair = norms + other_ref[0:1, :] - 2.0 * jnp.where(core_ref[0] == 0, gram, gram.T)
    spread = summary_ref[1:2, 0:1] + other_ref[1:2, 0:1] + 2.0 * jnp.sum(pair)
    width = spread / scale_base
    inverse = -1.0 / width
    own_weights = jnp.where(diagonal, 0.0, jnp.exp(own * inverse))
    pair_weights = jnp.exp(pair * inverse)
    weights = jnp.concatenate([own_weights, pair_weights], axis=1)
    hi_ref[...], lo_ref[...] = split(weights)
    weight_ref[...] = jnp.broadcast_to(jnp.sum(weights, axis=1, keepdims=True), weight_ref.shape)
    half_ref[...] = jnp.broadcast_to(0.5 * width, half_ref.shape)


def weights_part(core, own, summary, other, gram, scale_base):
    rows = own.shape[0]
    half = jax.ShapeDtypeStruct((rows, 2 * rows), jnp.bfloat16)
    return pl.pallas_call(
        functools.partial(weights_kernel, scale_base),
        in_specs=[pl.BlockSpec(memory_space=pltpu.SMEM)] + [pl.BlockSpec(memory_space=pltpu.VMEM)] * 4,
        out_shape=[half, half, f32(rows, 128), f32(8, 128)],
        compiler_params=params(12),
        name="kernel_weights",
    )(core, own, summary, other, gram)


def velocity_kernel(x_ref, s_ref, other_x, other_s, hi_ref, lo_ref, weight_ref, half_ref, out_ref):
    rows = out_ref.shape[0]
    half = half_ref[0:1, 0:1]
    x = x_ref[...]
    driven = half * s_ref[...]
    moved_hi, moved_lo = split(jnp.concatenate([driven - x, half * other_s[...] - other_x[...]], axis=0))
    hi = hi_ref[...]
    both = nn_dot(jnp.concatenate([hi, lo_ref[...]], axis=0), moved_hi)
    out_ref[...] = driven + weight_ref[:, 0:1] * x + both[:rows] + both[rows:] + nn_dot(hi, moved_lo)


def velocity_part(particles, scores, visitor, visitor_scores, weights):
    rows, columns = particles.shape
    tile = min(VELOCITY_TILE, columns)
    block = pl.BlockSpec((rows, tile), lambda i: (0, i))
    return pl.pallas_call(
        velocity_kernel,
        grid=(columns // tile,),
        in_specs=[block] * 4 + [whole(w) for w in weights],
        out_specs=block,
        out_shape=f32(rows, columns),
        compiler_params=params(52),
        cost_estimate=pl.CostEstimate(flops=12 * rows * rows * columns, bytes_accessed=20 * rows * columns, transcendentals=0),
        name="velocity",
    )(particles, scores, visitor, visitor_scores, *weights)


def swap(array):
    return lax.ppermute(array, "blk", [(0, 1), (1, 0)])


def body(particles, scores):
    count = lax.axis_size("dim")
    total_rows = particles.shape[0] * lax.axis_size("blk")
    scale_base = total_rows * total_rows * math.log(total_rows)

    core = lax.axis_index("blk").reshape(1)
    visitor = swap(particles)

    own_copies = summed_shards(own_part(particles), "dim")
    own = gathered(own_copies, "dim")
    summary = summary_part(own)
    across = [(d * 2 + b, (d + 1) % count * 2 + 1 - b) for d in range(count) for b in range(2)]
    other = lax.ppermute(summary, BOTH, across)

    visitor, _ = lax.optimization_barrier((visitor, own_copies))
    gram = pair_part(core, particles, visitor)
    scores_late, gram = lax.optimization_barrier((scores, gram))
    visitor_scores = swap(scores_late)
    gram = gathered(summed_shards(gram, BOTH, other), BOTH)
    weights = weights_part(core, own, summary, other, gram, scale_base)
    return velocity_part(particles, scores, visitor, visitor_scores, weights)


def solution(mesh):
    return jax.shard_map(
        body,
        mesh=mesh,
        in_specs=(P(("grp", "blk"), "dim"), P(("grp", "blk"), "dim")),
        out_specs=P(("grp", "blk"), "dim"),
        check_vma=False,
    )
```

```python
import functools
import math

import jax
import jax.numpy as jnp
from jax import lax
from jax.experimental import pallas as pl
from jax.experimental.pallas import tpu as pltpu
from jax.sharding import PartitionSpec as P

GRAM_TILE = 2048
VELOCITY_TILE = 2048
MIB = 1024 * 1024
BOTH = ("dim", "blk")


def params(limit):
    return pltpu.CompilerParams(vmem_limit_bytes=limit * MIB)


def split(x):
    hi = x.astype(jnp.bfloat16)
    lo = (x - hi.astype(jnp.float32)).astype(jnp.bfloat16)
    return hi, lo


def nt_dot(left, right):
    return lax.dot_general(left, right, (((1,), (1,)), ((), ())), preferred_element_type=jnp.float32)


def nn_dot(left, right):
    return jnp.dot(left, right, preferred_element_type=jnp.float32)


def lane_sums(values):
    total = values[:, :128]
    for start in range(128, values.shape[1], 128):
        total = total + values[:, start:start + 128]
    return total


def whole(array):
    return pl.BlockSpec(array.shape, lambda i: (0,) * len(array.shape))


def f32(*shape):
    return jax.ShapeDtypeStruct(shape, jnp.float32)


def on_diagonal(rows):
    return lax.broadcasted_iota(jnp.int32, (rows, rows), 0) == lax.broadcasted_iota(jnp.int32, (rows, rows), 1)


def own_kernel(x_ref, out_ref, gram_ref, squares_ref):
    @pl.when(pl.program_id(0) == 0)
    def _():
        gram_ref[...] = jnp.zeros_like(gram_ref)
        squares_ref[...] = jnp.zeros_like(squares_ref)

    x = x_ref[...]
    hi, lo = split(x)
    gram_ref[...] += nt_dot(jnp.concatenate([hi, lo], axis=0), hi)
    squares_ref[...] += lane_sums(x * x)

    @pl.when(pl.program_id(0) == pl.num_programs(0) - 1)
    def _():
        rows = out_ref.shape[0]
        mixed = gram_ref[rows:, :]
        gram = gram_ref[:rows, :] + mixed + mixed.T
        norms = jnp.sum(squares_ref[...], axis=1, keepdims=True)
        out_ref[...] = jnp.where(on_diagonal(rows), norms, norms + norms.T - 2.0 * gram)


def own_part(particles):
    rows, columns = particles.shape
    tile = min(GRAM_TILE, columns)
    out = f32(rows, rows)
    return pl.pallas_call(
        own_kernel,
        grid=(columns // tile,),
        in_specs=[pl.BlockSpec((rows, tile), lambda i: (0, i))],
        out_specs=whole(out),
        out_shape=out,
        scratch_shapes=[pltpu.VMEM((2 * rows, rows), jnp.float32), pltpu.VMEM((rows, 128), jnp.float32)],
        compiler_params=params(52),
        cost_estimate=pl.CostEstimate(flops=4 * rows * rows * columns, bytes_accessed=4 * rows * columns, transcendentals=0),
        name="own_gram",
    )(particles)


def pair_kernel(core_ref, mine_ref, other_ref, out_ref, gram_ref):
    @pl.when(pl.program_id(0) == 0)
    def _():
        gram_ref[...] = jnp.zeros_like(gram_ref)

    rows = gram_ref.shape[0]
    my_hi, my_lo = split(mine_ref[...])
    hi, lo = split(other_ref[...])
    both = nt_dot(jnp.concatenate([my_hi, my_lo], axis=0), hi)
    gram_ref[...] += both[:rows] + both[rows:] + nt_dot(my_hi, lo)

    @pl.when(pl.program_id(0) == pl.num_programs(0) - 1)
    def _():
        gram = gram_ref[...]
        out_ref[...] = jnp.where(core_ref[0] == 0, gram, gram.T)


def pair_part(core, particles, visitor):
    rows, columns = particles.shape
    width = columns // 2
    tile = min(GRAM_TILE, width)
    tiles = width // tile
    out = f32(rows, rows)
    block = pl.BlockSpec((rows, tile), lambda i, core: (0, core[0] * tiles + i))
    return pl.pallas_call(
        pair_kernel,
        grid_spec=pltpu.PrefetchScalarGridSpec(
            num_scalar_prefetch=1,
            grid=(tiles,),
            in_specs=[block, block],
            out_specs=pl.BlockSpec(out.shape, lambda i, core: (0, 0)),
            scratch_shapes=[pltpu.VMEM((rows, rows), jnp.float32)],
        ),
        out_shape=out,
        compiler_params=params(52),
        cost_estimate=pl.CostEstimate(flops=6 * rows * rows * width, bytes_accessed=8 * rows * width, transcendentals=0),
        name="pair_gram",
    )(core, particles, visitor)


def sum_kernel(arrived_ref, out_ref):
    total = arrived_ref[0]
    for step in range(1, arrived_ref.shape[0]):
        total = total + arrived_ref[step]
    for step in range(out_ref.shape[0]):
        out_ref[step] = total


def summed_shards(block, axes, beside=None):
    count = lax.axis_size(axes)
    rows, columns = block.shape
    arrived = lax.all_to_all(block.reshape(count, rows // count, columns), axes, 0, 0)
    if beside is not None:
        arrived, _ = lax.optimization_barrier((arrived, beside))
    return pl.pallas_call(sum_kernel, out_shape=f32(*arrived.shape), compiler_params=params(8), name="sum_shards")(arrived)


def gathered(copies, axes):
    count, rows, columns = copies.shape
    return lax.all_to_all(copies, axes, 0, 0).reshape(count * rows, columns)


def summary_kernel(own_ref, out_ref):
    own = own_ref[...]
    rows = own.shape[0]
    diagonal = on_diagonal(rows)
    norms = jnp.sum(jnp.where(diagonal, own, 0.0), axis=0, keepdims=True)
    total = jnp.sum(jnp.where(diagonal, 0.0, own))
    out_ref[...] = jnp.concatenate([norms, jnp.full((7, rows), total)], axis=0)


def summary_part(own):
    return pl.pallas_call(summary_kernel, out_shape=f32(8, own.shape[0]), compiler_params=params(8), name="summary")(own)


def weights_kernel(scale_base, core_ref, own_ref, summary_ref, other_ref, gram_ref, hi_ref, lo_ref, weight_ref, half_ref):
    own = own_ref[...]
    rows = own.shape[0]
    diagonal = on_diagonal(rows)
    norms = jnp.sum(jnp.where(diagonal, own, 0.0), axis=1, keepdims=True)
    gram = gram_ref[...]
    pair = norms + other_ref[0:1, :] - 2.0 * jnp.where(core_ref[0] == 0, gram, gram.T)
    spread = summary_ref[1:2, 0:1] + other_ref[1:2, 0:1] + 2.0 * jnp.sum(pair)
    width = spread / scale_base
    inverse = -1.0 / width
    own_weights = jnp.where(diagonal, 0.0, jnp.exp(own * inverse))
    pair_weights = jnp.exp(pair * inverse)
    weights = jnp.concatenate([own_weights, pair_weights], axis=1)
    hi_ref[...], lo_ref[...] = split(weights)
    weight_ref[...] = jnp.broadcast_to(jnp.sum(weights, axis=1, keepdims=True), weight_ref.shape)
    half_ref[...] = jnp.broadcast_to(0.5 * width, half_ref.shape)


def weights_part(core, own, summary, other, gram, scale_base):
    rows = own.shape[0]
    half = jax.ShapeDtypeStruct((rows, 2 * rows), jnp.bfloat16)
    return pl.pallas_call(
        functools.partial(weights_kernel, scale_base),
        in_specs=[pl.BlockSpec(memory_space=pltpu.SMEM)] + [pl.BlockSpec(memory_space=pltpu.VMEM)] * 4,
        out_shape=[half, half, f32(rows, 128), f32(8, 128)],
        compiler_params=params(12),
        name="kernel_weights",
    )(core, own, summary, other, gram)


def velocity_kernel(x_ref, s_ref, other_x, other_s, hi_ref, lo_ref, weight_ref, half_ref, out_ref):
    rows = out_ref.shape[0]
    half = half_ref[0:1, 0:1]
    x = x_ref[...]
    driven = half * s_ref[...]
    moved_hi, moved_lo = split(jnp.concatenate([driven - x, half * other_s[...] - other_x[...]], axis=0))
    hi = hi_ref[...]
    both = nn_dot(jnp.concatenate([hi, lo_ref[...]], axis=0), moved_hi)
    out_ref[...] = driven + weight_ref[:, 0:1] * x + both[:rows] + both[rows:] + nn_dot(hi, moved_lo)


def velocity_part(particles, scores, visitor, visitor_scores, weights):
    rows, columns = particles.shape
    tile = min(VELOCITY_TILE, columns)
    block = pl.BlockSpec((rows, tile), lambda i: (0, i))
    return pl.pallas_call(
        velocity_kernel,
        grid=(columns // tile,),
        in_specs=[block] * 4 + [whole(w) for w in weights],
        out_specs=block,
        out_shape=f32(rows, columns),
        compiler_params=params(52),
        cost_estimate=pl.CostEstimate(flops=12 * rows * rows * columns, bytes_accessed=20 * rows * columns, transcendentals=0),
        name="velocity",
    )(particles, scores, visitor, visitor_scores, *weights)


def swap(array):
    return lax.ppermute(array, "blk", [(0, 1), (1, 0)])


def body(particles, scores):
    count = lax.axis_size("dim")
    total_rows = particles.shape[0] * lax.axis_size("blk")
    scale_base = total_rows * total_rows * math.log(total_rows)

    core = lax.axis_index("blk").reshape(1)
    visitor = swap(particles)
    visitor_scores = swap(scores)

    own = gathered(summed_shards(own_part(particles), "dim"), "dim")
    summary = summary_part(own)
    across = [(d * 2 + b, (d + 1) % count * 2 + 1 - b) for d in range(count) for b in range(2)]
    other = lax.ppermute(summary, BOTH, across)

    gram = summed_shards(pair_part(core, particles, visitor), BOTH, other)
    gram = gathered(gram, BOTH)
    weights = weights_part(core, own, summary, other, gram, scale_base)
    return velocity_part(particles, scores, visitor, visitor_scores, weights)


def solution(mesh):
    return jax.shard_map(
        body,
        mesh=mesh,
        in_specs=(P(("grp", "blk"), "dim"), P(("grp", "blk"), "dim")),
        out_specs=P(("grp", "blk"), "dim"),
        check_vma=False,
    )
```

```python
import functools
import math

import jax
import jax.numpy as jnp
from jax import lax
from jax.experimental import pallas as pl
from jax.experimental.pallas import tpu as pltpu
from jax.sharding import PartitionSpec as P

GRAM_TILE = 1024
VELOCITY_TILE = 1024
DEPTH = 4
MIB = 1024 * 1024
BOTH = ("dim", "blk")


def params(limit):
    return pltpu.CompilerParams(vmem_limit_bytes=limit * MIB)


def split(x):
    hi = x.astype(jnp.bfloat16)
    lo = (x - hi.astype(jnp.float32)).astype(jnp.bfloat16)
    return hi, lo


def nt_dot(left, right):
    return lax.dot_general(left, right, (((1,), (1,)), ((), ())), preferred_element_type=jnp.float32)


def nn_dot(left, right):
    return jnp.dot(left, right, preferred_element_type=jnp.float32)


def lane_sums(values):
    total = values[:, :128]
    for start in range(128, values.shape[1], 128):
        total = total + values[:, start:start + 128]
    return total


def fetch(sources, buffers, sems, first=0):
    step, steps = pl.program_id(0), pl.num_programs(0)
    depth, _, tile = buffers[0].shape

    def copies(at):
        columns = pl.ds(pl.multiple_of((first + at) * tile, tile), tile)
        slot = lax.rem(at, depth)
        return [
            pltpu.make_async_copy(source.at[:, columns], buffer.at[slot], sems.at[n, slot])
            for n, (source, buffer) in enumerate(zip(sources, buffers))
        ]

    def start(at):
        @pl.when(at < steps)
        def _():
            for copy in copies(at):
                copy.start()

    @pl.when(step == 0)
    def _():
        for ahead in range(depth - 1):
            start(ahead)

    start(step + depth - 1)
    for copy in copies(step):
        copy.wait()
    return [buffer[lax.rem(step, depth)] for buffer in buffers]


def slots(count, rows, tile):
    return [pltpu.VMEM((DEPTH, rows, tile), jnp.float32)] * count + [pltpu.SemaphoreType.DMA((count, DEPTH))]


def in_hbm():
    return pl.BlockSpec(memory_space=pl.ANY)


def whole(array):
    return pl.BlockSpec(array.shape, lambda i: (0,) * len(array.shape))


def f32(*shape):
    return jax.ShapeDtypeStruct(shape, jnp.float32)


def on_diagonal(rows):
    return lax.broadcasted_iota(jnp.int32, (rows, rows), 0) == lax.broadcasted_iota(jnp.int32, (rows, rows), 1)


def own_kernel(x_ref, out_ref, gram_ref, squares_ref, buffer, sems):
    @pl.when(pl.program_id(0) == 0)
    def _():
        gram_ref[...] = jnp.zeros_like(gram_ref)
        squares_ref[...] = jnp.zeros_like(squares_ref)

    (x,) = fetch([x_ref], [buffer], sems)
    hi, lo = split(x)
    gram_ref[...] += nt_dot(jnp.concatenate([hi, lo], axis=0), hi)
    squares_ref[...] += lane_sums(x * x)

    @pl.when(pl.program_id(0) == pl.num_programs(0) - 1)
    def _():
        rows = out_ref.shape[0]
        mixed = gram_ref[rows:, :]
        gram = gram_ref[:rows, :] + mixed + mixed.T
        norms = jnp.sum(squares_ref[...], axis=1, keepdims=True)
        out_ref[...] = jnp.where(on_diagonal(rows), norms, norms + norms.T - 2.0 * gram)


def own_part(particles):
    rows, columns = particles.shape
    tile = min(GRAM_TILE, columns)
    out = f32(rows, rows)
    return pl.pallas_call(
        own_kernel,
        grid=(columns // tile,),
        in_specs=[in_hbm()],
        out_specs=whole(out),
        out_shape=out,
        scratch_shapes=[
            pltpu.VMEM((2 * rows, rows), jnp.float32),
            pltpu.VMEM((rows, 128), jnp.float32),
            *slots(1, rows, tile),
        ],
        compiler_params=params(52),
        cost_estimate=pl.CostEstimate(flops=4 * rows * rows * columns, bytes_accessed=4 * rows * columns, transcendentals=0),
        name="own_gram",
    )(particles)


def pair_kernel(core_ref, mine_ref, other_ref, out_ref, gram_ref, my_buffer, buffer, sems):
    @pl.when(pl.program_id(0) == 0)
    def _():
        gram_ref[...] = jnp.zeros_like(gram_ref)

    rows = gram_ref.shape[0]
    mine, other = fetch([mine_ref, other_ref], [my_buffer, buffer], sems, core_ref[0] * pl.num_programs(0))
    my_hi, my_lo = split(mine)
    hi, lo = split(other)
    both = nt_dot(jnp.concatenate([my_hi, my_lo], axis=0), hi)
    gram_ref[...] += both[:rows] + both[rows:] + nt_dot(my_hi, lo)

    @pl.when(pl.program_id(0) == pl.num_programs(0) - 1)
    def _():
        gram = gram_ref[...]
        out_ref[...] = jnp.where(core_ref[0] == 0, gram, gram.T)


def pair_part(core, particles, visitor):
    rows, columns = particles.shape
    width = columns // 2
    tile = min(GRAM_TILE, width)
    tiles = width // tile
    out = f32(rows, rows)
    return pl.pallas_call(
        pair_kernel,
        grid_spec=pltpu.PrefetchScalarGridSpec(
            num_scalar_prefetch=1,
            grid=(tiles,),
            in_specs=[in_hbm(), in_hbm()],
            out_specs=pl.BlockSpec(out.shape, lambda i, core: (0, 0)),
            scratch_shapes=[pltpu.VMEM((rows, rows), jnp.float32), *slots(2, rows, tile)],
        ),
        out_shape=out,
        compiler_params=params(52),
        cost_estimate=pl.CostEstimate(flops=6 * rows * rows * width, bytes_accessed=8 * rows * width, transcendentals=0),
        name="pair_gram",
    )(core, particles, visitor)


def sum_kernel(arrived_ref, out_ref):
    total = arrived_ref[0]
    for step in range(1, arrived_ref.shape[0]):
        total = total + arrived_ref[step]
    for step in range(out_ref.shape[0]):
        out_ref[step] = total


def summed_shards(block, axes, beside=None):
    count = lax.axis_size(axes)
    rows, columns = block.shape
    arrived = lax.all_to_all(block.reshape(count, rows // count, columns), axes, 0, 0)
    if beside is not None:
        arrived, _ = lax.optimization_barrier((arrived, beside))
    return pl.pallas_call(sum_kernel, out_shape=f32(*arrived.shape), compiler_params=params(8), name="sum_shards")(arrived)


def gathered(copies, axes):
    count, rows, columns = copies.shape
    return lax.all_to_all(copies, axes, 0, 0).reshape(count * rows, columns)


def summary_kernel(own_ref, out_ref):
    own = own_ref[...]
    rows = own.shape[0]
    diagonal = on_diagonal(rows)
    norms = jnp.sum(jnp.where(diagonal, own, 0.0), axis=0, keepdims=True)
    total = jnp.sum(jnp.where(diagonal, 0.0, own))
    out_ref[...] = jnp.concatenate([norms, jnp.full((7, rows), total)], axis=0)


def summary_part(own):
    return pl.pallas_call(summary_kernel, out_shape=f32(8, own.shape[0]), compiler_params=params(8), name="summary")(own)


def weights_kernel(scale_base, core_ref, own_ref, summary_ref, other_ref, gram_ref, hi_ref, lo_ref, weight_ref, half_ref):
    own = own_ref[...]
    rows = own.shape[0]
    diagonal = on_diagonal(rows)
    norms = jnp.sum(jnp.where(diagonal, own, 0.0), axis=1, keepdims=True)
    gram = gram_ref[...]
    pair = norms + other_ref[0:1, :] - 2.0 * jnp.where(core_ref[0] == 0, gram, gram.T)
    spread = summary_ref[1:2, 0:1] + other_ref[1:2, 0:1] + 2.0 * jnp.sum(pair)
    width = spread / scale_base
    inverse = -1.0 / width
    own_weights = jnp.where(diagonal, 0.0, jnp.exp(own * inverse))
    pair_weights = jnp.exp(pair * inverse)
    weights = jnp.concatenate([own_weights, pair_weights], axis=1)
    hi_ref[...], lo_ref[...] = split(weights)
    weight_ref[...] = jnp.broadcast_to(jnp.sum(weights, axis=1, keepdims=True), weight_ref.shape)
    half_ref[...] = jnp.broadcast_to(0.5 * width, half_ref.shape)


def weights_part(core, own, summary, other, gram, scale_base):
    rows = own.shape[0]
    half = jax.ShapeDtypeStruct((rows, 2 * rows), jnp.bfloat16)
    return pl.pallas_call(
        functools.partial(weights_kernel, scale_base),
        in_specs=[pl.BlockSpec(memory_space=pltpu.SMEM)] + [pl.BlockSpec(memory_space=pltpu.VMEM)] * 4,
        out_shape=[half, half, f32(rows, 128), f32(8, 128)],
        compiler_params=params(12),
        name="kernel_weights",
    )(core, own, summary, other, gram)


def velocity_kernel(
    x_ref, s_ref, other_x_ref, other_s_ref, hi_ref, lo_ref, weight_ref, half_ref, out_ref, *scratch
):
    rows = out_ref.shape[0]
    half = half_ref[0:1, 0:1]
    x, s, other_x, other_s = fetch([x_ref, s_ref, other_x_ref, other_s_ref], scratch[:4], scratch[4])
    driven = half * s
    moved_hi, moved_lo = split(jnp.concatenate([driven - x, half * other_s - other_x], axis=0))
    hi = hi_ref[...]
    both = nn_dot(jnp.concatenate([hi, lo_ref[...]], axis=0), moved_hi)
    out_ref[...] = driven + weight_ref[:, 0:1] * x + both[:rows] + both[rows:] + nn_dot(hi, moved_lo)


def velocity_part(particles, scores, visitor, visitor_scores, weights):
    rows, columns = particles.shape
    tile = min(VELOCITY_TILE, columns)
    block = pl.BlockSpec((rows, tile), lambda i: (0, i))
    return pl.pallas_call(
        velocity_kernel,
        grid=(columns // tile,),
        in_specs=[in_hbm()] * 4 + [whole(w) for w in weights],
        out_specs=block,
        out_shape=f32(rows, columns),
        scratch_shapes=slots(4, rows, tile),
        compiler_params=params(52),
        cost_estimate=pl.CostEstimate(flops=12 * rows * rows * columns, bytes_accessed=20 * rows * columns, transcendentals=0),
        name="velocity",
    )(particles, scores, visitor, visitor_scores, *weights)


def swap(array):
    return lax.ppermute(array, "blk", [(0, 1), (1, 0)])


def body(particles, scores):
    count = lax.axis_size("dim")
    total_rows = particles.shape[0] * lax.axis_size("blk")
    scale_base = total_rows * total_rows * math.log(total_rows)

    core = lax.axis_index("blk").reshape(1)
    visitor = swap(particles)
    visitor_scores = swap(scores)

    own = gathered(summed_shards(own_part(particles), "dim"), "dim")
    summary = summary_part(own)
    across = [(d * 2 + b, (d + 1) % count * 2 + 1 - b) for d in range(count) for b in range(2)]
    other = lax.ppermute(summary, BOTH, across)

    gram = summed_shards(pair_part(core, particles, visitor), BOTH, other)
    gram = gathered(gram, BOTH)
    weights = weights_part(core, own, summary, other, gram, scale_base)
    return velocity_part(particles, scores, visitor, visitor_scores, weights)


def solution(mesh):
    return jax.shard_map(
        body,
        mesh=mesh,
        in_specs=(P(("grp", "blk"), "dim"), P(("grp", "blk"), "dim")),
        out_specs=P(("grp", "blk"), "dim"),
        check_vma=False,
    )
```

```python
import functools
import math

import jax
import jax.numpy as jnp
from jax import lax
from jax.experimental import pallas as pl
from jax.experimental.pallas import tpu as pltpu
from jax.sharding import PartitionSpec as P

GRAM_TILE = 1024
VELOCITY_TILE = 1024
DEPTH = 4
MIB = 1024 * 1024
BOTH = ("dim", "blk")


def params(limit):
    return pltpu.CompilerParams(vmem_limit_bytes=limit * MIB)


def split(x):
    hi = x.astype(jnp.bfloat16)
    lo = (x - hi.astype(jnp.float32)).astype(jnp.bfloat16)
    return hi, lo


def nt_dot(left, right):
    return lax.dot_general(left, right, (((1,), (1,)), ((), ())), preferred_element_type=jnp.float32)


def nn_dot(left, right):
    return jnp.dot(left, right, preferred_element_type=jnp.float32)


def lane_sums(values):
    total = values[:, :128]
    for start in range(128, values.shape[1], 128):
        total = total + values[:, start:start + 128]
    return total


def fetch(sources, buffers, sems, first=0, meanwhile=None):
    step, steps = pl.program_id(0), pl.num_programs(0)
    depth, _, tile = buffers[0].shape

    def copies(at):
        columns = pl.ds(pl.multiple_of((first + at) * tile, tile), tile)
        slot = lax.rem(at, depth)
        return [
            pltpu.make_async_copy(source.at[:, columns], buffer.at[slot], sems.at[n, slot])
            for n, (source, buffer) in enumerate(zip(sources, buffers))
        ]

    def start(at):
        @pl.when(at < steps)
        def _():
            for copy in copies(at):
                copy.start()

    @pl.when(step == 0)
    def _():
        for ahead in range(depth - 1):
            start(ahead)
        if meanwhile is not None:
            meanwhile()

    start(step + depth - 1)
    for copy in copies(step):
        copy.wait()
    return [buffer[lax.rem(step, depth)] for buffer in buffers]


def slots(count, rows, tile):
    return [pltpu.VMEM((DEPTH, rows, tile), jnp.float32)] * count + [pltpu.SemaphoreType.DMA((count, DEPTH))]


def in_hbm():
    return pl.BlockSpec(memory_space=pl.ANY)


def whole(array):
    return pl.BlockSpec(array.shape, lambda i: (0,) * len(array.shape))


def f32(*shape):
    return jax.ShapeDtypeStruct(shape, jnp.float32)


def on_diagonal(rows):
    return lax.broadcasted_iota(jnp.int32, (rows, rows), 0) == lax.broadcasted_iota(jnp.int32, (rows, rows), 1)


def own_kernel(x_ref, out_ref, gram_ref, squares_ref, buffer, sems):
    @pl.when(pl.program_id(0) == 0)
    def _():
        gram_ref[...] = jnp.zeros_like(gram_ref)
        squares_ref[...] = jnp.zeros_like(squares_ref)

    (x,) = fetch([x_ref], [buffer], sems)
    hi, lo = split(x)
    gram_ref[...] += nt_dot(jnp.concatenate([hi, lo], axis=0), hi)
    squares_ref[...] += lane_sums(x * x)

    @pl.when(pl.program_id(0) == pl.num_programs(0) - 1)
    def _():
        rows = out_ref.shape[0]
        mixed = gram_ref[rows:, :]
        gram = gram_ref[:rows, :] + mixed + mixed.T
        norms = jnp.sum(squares_ref[...], axis=1, keepdims=True)
        out_ref[...] = jnp.where(on_diagonal(rows), norms, norms + norms.T - 2.0 * gram)


def own_part(particles):
    rows, columns = particles.shape
    tile = min(GRAM_TILE, columns)
    out = f32(rows, rows)
    return pl.pallas_call(
        own_kernel,
        grid=(columns // tile,),
        in_specs=[in_hbm()],
        out_specs=whole(out),
        out_shape=out,
        scratch_shapes=[
            pltpu.VMEM((2 * rows, rows), jnp.float32),
            pltpu.VMEM((rows, 128), jnp.float32),
            *slots(1, rows, tile),
        ],
        compiler_params=params(52),
        cost_estimate=pl.CostEstimate(flops=4 * rows * rows * columns, bytes_accessed=4 * rows * columns, transcendentals=0),
        name="own_gram",
    )(particles)


def pair_kernel(core_ref, mine_ref, other_ref, out_ref, gram_ref, my_buffer, buffer, sems):
    @pl.when(pl.program_id(0) == 0)
    def _():
        gram_ref[...] = jnp.zeros_like(gram_ref)

    rows = gram_ref.shape[0]
    mine, other = fetch([mine_ref, other_ref], [my_buffer, buffer], sems, core_ref[0] * pl.num_programs(0))
    my_hi, my_lo = split(mine)
    hi, lo = split(other)
    both = nt_dot(jnp.concatenate([my_hi, my_lo], axis=0), hi)
    gram_ref[...] += both[:rows] + both[rows:] + nt_dot(my_hi, lo)

    @pl.when(pl.program_id(0) == pl.num_programs(0) - 1)
    def _():
        gram = gram_ref[...]
        out_ref[...] = jnp.where(core_ref[0] == 0, gram, gram.T)


def pair_part(core, particles, visitor):
    rows, columns = particles.shape
    width = columns // 2
    tile = min(GRAM_TILE, width)
    tiles = width // tile
    out = f32(rows, rows)
    return pl.pallas_call(
        pair_kernel,
        grid_spec=pltpu.PrefetchScalarGridSpec(
            num_scalar_prefetch=1,
            grid=(tiles,),
            in_specs=[in_hbm(), in_hbm()],
            out_specs=pl.BlockSpec(out.shape, lambda i, core: (0, 0)),
            scratch_shapes=[pltpu.VMEM((rows, rows), jnp.float32), *slots(2, rows, tile)],
        ),
        out_shape=out,
        compiler_params=params(52),
        cost_estimate=pl.CostEstimate(flops=6 * rows * rows * width, bytes_accessed=8 * rows * width, transcendentals=0),
        name="pair_gram",
    )(core, particles, visitor)


def sum_kernel(arrived_ref, out_ref):
    total = arrived_ref[0]
    for step in range(1, arrived_ref.shape[0]):
        total = total + arrived_ref[step]
    for step in range(out_ref.shape[0]):
        out_ref[step] = total


def summed_shards(block, axes, beside=None):
    count = lax.axis_size(axes)
    rows, columns = block.shape
    arrived = lax.all_to_all(block.reshape(count, rows // count, columns), axes, 0, 0)
    if beside is not None:
        arrived, _ = lax.optimization_barrier((arrived, beside))
    return pl.pallas_call(sum_kernel, out_shape=f32(*arrived.shape), compiler_params=params(8), name="sum_shards")(arrived)


def gathered(copies, axes):
    count, rows, columns = copies.shape
    return lax.all_to_all(copies, axes, 0, 0).reshape(count * rows, columns)


def summary_kernel(own_ref, out_ref):
    own = own_ref[...]
    rows = own.shape[0]
    diagonal = on_diagonal(rows)
    norms = jnp.sum(jnp.where(diagonal, own, 0.0), axis=0, keepdims=True)
    total = jnp.sum(jnp.where(diagonal, 0.0, own))
    out_ref[...] = jnp.concatenate([norms, jnp.full((7, rows), total)], axis=0)


def summary_part(own):
    return pl.pallas_call(summary_kernel, out_shape=f32(8, own.shape[0]), compiler_params=params(8), name="summary")(own)


def form_weights(scale_base, core, own_ref, summary_ref, other_ref, gram_ref, weights_ref, weight_ref, half_ref):
    own = own_ref[...]
    rows = own.shape[0]
    diagonal = on_diagonal(rows)
    norms = jnp.sum(jnp.where(diagonal, own, 0.0), axis=1, keepdims=True)
    gram = gram_ref[...]
    pair = norms + other_ref[0:1, :] - 2.0 * jnp.where(core == 0, gram, gram.T)
    spread = summary_ref[1:2, 0:1] + other_ref[1:2, 0:1] + 2.0 * jnp.sum(pair)
    width = spread / scale_base
    inverse = -1.0 / width
    own_weights = jnp.where(diagonal, 0.0, jnp.exp(own * inverse))
    pair_weights = jnp.exp(pair * inverse)
    weights = jnp.concatenate([own_weights, pair_weights], axis=1)
    weights_ref[:rows, :], weights_ref[rows:, :] = split(weights)
    weight_ref[...] = jnp.broadcast_to(jnp.sum(weights, axis=1, keepdims=True), weight_ref.shape)
    half_ref[...] = jnp.broadcast_to(0.5 * width, half_ref.shape)


def velocity_kernel(
    scale_base, core_ref, x_ref, s_ref, other_x_ref, other_s_ref, own_ref, summary_ref, other_ref, gram_ref, out_ref, *scratch
):
    rows = out_ref.shape[0]
    weights_ref, weight_ref, half_ref = scratch[5:]

    def meanwhile():
        form_weights(
            scale_base, core_ref[0], own_ref, summary_ref, other_ref, gram_ref, weights_ref, weight_ref, half_ref
        )

    x, s, other_x, other_s = fetch(
        [x_ref, s_ref, other_x_ref, other_s_ref], scratch[:4], scratch[4], meanwhile=meanwhile
    )
    half = half_ref[0:1, 0:1]
    driven = half * s
    moved_hi, moved_lo = split(jnp.concatenate([driven - x, half * other_s - other_x], axis=0))
    both = nn_dot(weights_ref[...], moved_hi)
    out_ref[...] = driven + weight_ref[:, 0:1] * x + both[:rows] + both[rows:] + nn_dot(weights_ref[:rows, :], moved_lo)


def velocity_part(core, particles, scores, visitor, visitor_scores, own, summary, other, gram, scale_base):
    rows, columns = particles.shape
    tile = min(VELOCITY_TILE, columns)
    small = [own, summary, other, gram]
    return pl.pallas_call(
        functools.partial(velocity_kernel, scale_base),
        grid_spec=pltpu.PrefetchScalarGridSpec(
            num_scalar_prefetch=1,
            grid=(columns // tile,),
            in_specs=[in_hbm()] * 4 + [pl.BlockSpec(a.shape, lambda i, core: (0, 0)) for a in small],
            out_specs=pl.BlockSpec((rows, tile), lambda i, core: (0, i)),
            scratch_shapes=[
                *slots(4, rows, tile),
                pltpu.VMEM((2 * rows, 2 * rows), jnp.bfloat16),
                pltpu.VMEM((rows, 128), jnp.float32),
                pltpu.VMEM((8, 128), jnp.float32),
            ],
        ),
        out_shape=f32(rows, columns),
        compiler_params=params(52),
        cost_estimate=pl.CostEstimate(flops=12 * rows * rows * columns, bytes_accessed=20 * rows * columns, transcendentals=0),
        name="velocity",
    )(core, particles, scores, visitor, visitor_scores, *small)


def swap(array):
    return lax.ppermute(array, "blk", [(0, 1), (1, 0)])


def body(particles, scores):
    count = lax.axis_size("dim")
    total_rows = particles.shape[0] * lax.axis_size("blk")
    scale_base = total_rows * total_rows * math.log(total_rows)

    core = lax.axis_index("blk").reshape(1)
    visitor = swap(particles)
    visitor_scores = swap(scores)

    own = gathered(summed_shards(own_part(particles), "dim"), "dim")
    summary = summary_part(own)
    across = [(d * 2 + b, (d + 1) % count * 2 + 1 - b) for d in range(count) for b in range(2)]
    other = lax.ppermute(summary, BOTH, across)

    gram = summed_shards(pair_part(core, particles, visitor), BOTH, other)
    gram = gathered(gram, BOTH)
    return velocity_part(core, particles, scores, visitor, visitor_scores, own, summary, other, gram, scale_base)


def solution(mesh):
    return jax.shard_map(
        body,
        mesh=mesh,
        in_specs=(P(("grp", "blk"), "dim"), P(("grp", "blk"), "dim")),
        out_specs=P(("grp", "blk"), "dim"),
        check_vma=False,
    )
```

```python
import functools
import math

import jax
import jax.numpy as jnp
from jax import lax
from jax.experimental import pallas as pl
from jax.experimental.pallas import tpu as pltpu
from jax.sharding import PartitionSpec as P

GRAM_TILE = 1024
VELOCITY_TILE = 2048
GRAM_DEPTH = 4
VELOCITY_DEPTH = 3
MIB = 1024 * 1024
BOTH = ("dim", "blk")


def params(limit):
    return pltpu.CompilerParams(vmem_limit_bytes=limit * MIB)


def split(x):
    hi = x.astype(jnp.bfloat16)
    lo = (x - hi.astype(jnp.float32)).astype(jnp.bfloat16)
    return hi, lo


def nt_dot(left, right):
    return lax.dot_general(left, right, (((1,), (1,)), ((), ())), preferred_element_type=jnp.float32)


def nn_dot(left, right):
    return jnp.dot(left, right, preferred_element_type=jnp.float32)


def lane_sums(values):
    total = values[:, :128]
    for start in range(128, values.shape[1], 128):
        total = total + values[:, start:start + 128]
    return total


def fetch(sources, buffers, sems, first=0):
    step, steps = pl.program_id(0), pl.num_programs(0)
    depth, _, tile = buffers[0].shape

    def copies(at):
        columns = pl.ds(pl.multiple_of((first + at) * tile, tile), tile)
        slot = lax.rem(at, depth)
        return [
            pltpu.make_async_copy(source.at[:, columns], buffer.at[slot], sems.at[n, slot])
            for n, (source, buffer) in enumerate(zip(sources, buffers))
        ]

    def start(at):
        @pl.when(at < steps)
        def _():
            for copy in copies(at):
                copy.start()

    @pl.when(step == 0)
    def _():
        for ahead in range(depth - 1):
            start(ahead)

    start(step + depth - 1)
    for copy in copies(step):
        copy.wait()
    return [buffer[lax.rem(step, depth)] for buffer in buffers]


def slots(depth, count, rows, tile):
    return [pltpu.VMEM((depth, rows, tile), jnp.float32)] * count + [pltpu.SemaphoreType.DMA((count, depth))]


def in_hbm():
    return pl.BlockSpec(memory_space=pl.ANY)


def whole(array):
    return pl.BlockSpec(array.shape, lambda i: (0,) * len(array.shape))


def f32(*shape):
    return jax.ShapeDtypeStruct(shape, jnp.float32)


def on_diagonal(rows):
    return lax.broadcasted_iota(jnp.int32, (rows, rows), 0) == lax.broadcasted_iota(jnp.int32, (rows, rows), 1)


def own_kernel(x_ref, out_ref, gram_ref, squares_ref, buffer, sems):
    @pl.when(pl.program_id(0) == 0)
    def _():
        gram_ref[...] = jnp.zeros_like(gram_ref)
        squares_ref[...] = jnp.zeros_like(squares_ref)

    (x,) = fetch([x_ref], [buffer], sems)
    hi, lo = split(x)
    gram_ref[...] += nt_dot(jnp.concatenate([hi, lo], axis=0), hi)
    squares_ref[...] += lane_sums(x * x)

    @pl.when(pl.program_id(0) == pl.num_programs(0) - 1)
    def _():
        rows = out_ref.shape[0]
        mixed = gram_ref[rows:, :]
        gram = gram_ref[:rows, :] + mixed + mixed.T
        norms = jnp.sum(squares_ref[...], axis=1, keepdims=True)
        out_ref[...] = jnp.where(on_diagonal(rows), norms, norms + norms.T - 2.0 * gram)


def own_part(particles):
    rows, columns = particles.shape
    tile = min(GRAM_TILE, columns)
    out = f32(rows, rows)
    return pl.pallas_call(
        own_kernel,
        grid=(columns // tile,),
        in_specs=[in_hbm()],
        out_specs=whole(out),
        out_shape=out,
        scratch_shapes=[
            pltpu.VMEM((2 * rows, rows), jnp.float32),
            pltpu.VMEM((rows, 128), jnp.float32),
            *slots(GRAM_DEPTH, 1, rows, tile),
        ],
        compiler_params=params(52),
        cost_estimate=pl.CostEstimate(flops=4 * rows * rows * columns, bytes_accessed=4 * rows * columns, transcendentals=0),
        name="own_gram",
    )(particles)


def pair_kernel(core_ref, mine_ref, other_ref, out_ref, gram_ref, my_buffer, buffer, sems):
    @pl.when(pl.program_id(0) == 0)
    def _():
        gram_ref[...] = jnp.zeros_like(gram_ref)

    rows = gram_ref.shape[0]
    mine, other = fetch([mine_ref, other_ref], [my_buffer, buffer], sems, core_ref[0] * pl.num_programs(0))
    my_hi, my_lo = split(mine)
    hi, lo = split(other)
    both = nt_dot(jnp.concatenate([my_hi, my_lo], axis=0), hi)
    gram_ref[...] += both[:rows] + both[rows:] + nt_dot(my_hi, lo)

    @pl.when(pl.program_id(0) == pl.num_programs(0) - 1)
    def _():
        gram = gram_ref[...]
        out_ref[...] = jnp.where(core_ref[0] == 0, gram, gram.T)


def pair_part(core, particles, visitor):
    rows, columns = particles.shape
    width = columns // 2
    tile = min(GRAM_TILE, width)
    tiles = width // tile
    out = f32(rows, rows)
    return pl.pallas_call(
        pair_kernel,
        grid_spec=pltpu.PrefetchScalarGridSpec(
            num_scalar_prefetch=1,
            grid=(tiles,),
            in_specs=[in_hbm(), in_hbm()],
            out_specs=pl.BlockSpec(out.shape, lambda i, core: (0, 0)),
            scratch_shapes=[pltpu.VMEM((rows, rows), jnp.float32), *slots(GRAM_DEPTH, 2, rows, tile)],
        ),
        out_shape=out,
        compiler_params=params(52),
        cost_estimate=pl.CostEstimate(flops=6 * rows * rows * width, bytes_accessed=8 * rows * width, transcendentals=0),
        name="pair_gram",
    )(core, particles, visitor)


def sum_kernel(arrived_ref, out_ref):
    total = arrived_ref[0]
    for step in range(1, arrived_ref.shape[0]):
        total = total + arrived_ref[step]
    for step in range(out_ref.shape[0]):
        out_ref[step] = total


def summed_shards(block, axes, beside=None):
    count = lax.axis_size(axes)
    rows, columns = block.shape
    arrived = lax.all_to_all(block.reshape(count, rows // count, columns), axes, 0, 0)
    if beside is not None:
        arrived, _ = lax.optimization_barrier((arrived, beside))
    return pl.pallas_call(sum_kernel, out_shape=f32(*arrived.shape), compiler_params=params(8), name="sum_shards")(arrived)


def gathered(copies, axes):
    count, rows, columns = copies.shape
    return lax.all_to_all(copies, axes, 0, 0).reshape(count * rows, columns)


def summary_kernel(own_ref, out_ref):
    own = own_ref[...]
    rows = own.shape[0]
    diagonal = on_diagonal(rows)
    norms = jnp.sum(jnp.where(diagonal, own, 0.0), axis=0, keepdims=True)
    total = jnp.sum(jnp.where(diagonal, 0.0, own))
    out_ref[...] = jnp.concatenate([norms, jnp.full((7, rows), total)], axis=0)


def summary_part(own):
    return pl.pallas_call(summary_kernel, out_shape=f32(8, own.shape[0]), compiler_params=params(8), name="summary")(own)


def weights_kernel(scale_base, core_ref, own_ref, summary_ref, other_ref, gram_ref, hi_ref, lo_ref, weight_ref, half_ref):
    own = own_ref[...]
    rows = own.shape[0]
    diagonal = on_diagonal(rows)
    norms = jnp.sum(jnp.where(diagonal, own, 0.0), axis=1, keepdims=True)
    gram = gram_ref[...]
    pair = norms + other_ref[0:1, :] - 2.0 * jnp.where(core_ref[0] == 0, gram, gram.T)
    spread = summary_ref[1:2, 0:1] + other_ref[1:2, 0:1] + 2.0 * jnp.sum(pair)
    width = spread / scale_base
    inverse = -1.0 / width
    own_weights = jnp.where(diagonal, 0.0, jnp.exp(own * inverse))
    pair_weights = jnp.exp(pair * inverse)
    weights = jnp.concatenate([own_weights, pair_weights], axis=1)
    hi_ref[...], lo_ref[...] = split(weights)
    weight_ref[...] = jnp.broadcast_to(jnp.sum(weights, axis=1, keepdims=True), weight_ref.shape)
    half_ref[...] = jnp.broadcast_to(0.5 * width, half_ref.shape)


def weights_part(core, own, summary, other, gram, scale_base):
    rows = own.shape[0]
    half = jax.ShapeDtypeStruct((rows, 2 * rows), jnp.bfloat16)
    return pl.pallas_call(
        functools.partial(weights_kernel, scale_base),
        in_specs=[pl.BlockSpec(memory_space=pltpu.SMEM)] + [pl.BlockSpec(memory_space=pltpu.VMEM)] * 4,
        out_shape=[half, half, f32(rows, 128), f32(8, 128)],
        compiler_params=params(12),
        name="kernel_weights",
    )(core, own, summary, other, gram)


def velocity_kernel(
    x_ref, s_ref, other_x_ref, other_s_ref, hi_ref, lo_ref, weight_ref, half_ref, out_ref, *scratch
):
    rows = out_ref.shape[0]
    half = half_ref[0:1, 0:1]
    x, s, other_x, other_s = fetch([x_ref, s_ref, other_x_ref, other_s_ref], scratch[:4], scratch[4])
    driven = half * s
    moved_hi, moved_lo = split(jnp.concatenate([driven - x, half * other_s - other_x], axis=0))
    hi = hi_ref[...]
    both = nn_dot(jnp.concatenate([hi, lo_ref[...]], axis=0), moved_hi)
    out_ref[...] = driven + weight_ref[:, 0:1] * x + both[:rows] + both[rows:] + nn_dot(hi, moved_lo)


def velocity_part(particles, scores, visitor, visitor_scores, weights):
    rows, columns = particles.shape
    tile = min(VELOCITY_TILE, columns)
    block = pl.BlockSpec((rows, tile), lambda i: (0, i))
    return pl.pallas_call(
        velocity_kernel,
        grid=(columns // tile,),
        in_specs=[in_hbm()] * 4 + [whole(w) for w in weights],
        out_specs=block,
        out_shape=f32(rows, columns),
        scratch_shapes=slots(VELOCITY_DEPTH, 4, rows, tile),
        compiler_params=params(52),
        cost_estimate=pl.CostEstimate(flops=12 * rows * rows * columns, bytes_accessed=20 * rows * columns, transcendentals=0),
        name="velocity",
    )(particles, scores, visitor, visitor_scores, *weights)


def swap(array):
    return lax.ppermute(array, "blk", [(0, 1), (1, 0)])


def body(particles, scores):
    count = lax.axis_size("dim")
    total_rows = particles.shape[0] * lax.axis_size("blk")
    scale_base = total_rows * total_rows * math.log(total_rows)

    core = lax.axis_index("blk").reshape(1)
    visitor = swap(particles)
    visitor_scores = swap(scores)

    own = gathered(summed_shards(own_part(particles), "dim"), "dim")
    summary = summary_part(own)
    across = [(d * 2 + b, (d + 1) % count * 2 + 1 - b) for d in range(count) for b in range(2)]
    other = lax.ppermute(summary, BOTH, across)

    gram = summed_shards(pair_part(core, particles, visitor), BOTH, other)
    gram = gathered(gram, BOTH)
    weights = weights_part(core, own, summary, other, gram, scale_base)
    return velocity_part(particles, scores, visitor, visitor_scores, weights)


def solution(mesh):
    return jax.shard_map(
        body,
        mesh=mesh,
        in_specs=(P(("grp", "blk"), "dim"), P(("grp", "blk"), "dim")),
        out_specs=P(("grp", "blk"), "dim"),
        check_vma=False,
    )
```

```python
import functools
import math

import jax
import jax.numpy as jnp
from jax import lax
from jax.experimental import pallas as pl
from jax.experimental.pallas import tpu as pltpu
from jax.sharding import PartitionSpec as P

GRAM_TILE = 1024
VELOCITY_TILE = 1024
DEPTH = 4
MIB = 1024 * 1024
BOTH = ("dim", "blk")


def params(limit):
    return pltpu.CompilerParams(vmem_limit_bytes=limit * MIB)


def split(x):
    hi = x.astype(jnp.bfloat16)
    lo = (x - hi.astype(jnp.float32)).astype(jnp.bfloat16)
    return hi, lo


def nt_dot(left, right):
    return lax.dot_general(left, right, (((1,), (1,)), ((), ())), preferred_element_type=jnp.float32)


def nn_dot(left, right):
    return jnp.dot(left, right, preferred_element_type=jnp.float32)


def lane_sums(values):
    total = values[:, :128]
    for start in range(128, values.shape[1], 128):
        total = total + values[:, start:start + 128]
    return total


def fetch(sources, buffers, sems, first=0):
    step, steps = pl.program_id(0), pl.num_programs(0)
    depth, _, tile = buffers[0].shape

    def copies(at):
        columns = pl.ds(pl.multiple_of((first + at) * tile, tile), tile)
        slot = lax.rem(at, depth)
        return [
            pltpu.make_async_copy(source.at[:, columns], buffer.at[slot], sems.at[n, slot])
            for n, (source, buffer) in enumerate(zip(sources, buffers))
        ]

    def start(at):
        @pl.when(at < steps)
        def _():
            for copy in copies(at):
                copy.start()

    @pl.when(step == 0)
    def _():
        for ahead in range(depth - 1):
            start(ahead)

    start(step + depth - 1)
    for copy in copies(step):
        copy.wait()
    return [buffer.at[lax.rem(step, depth)] for buffer in buffers]


def slots(count, rows, tile):
    return [pltpu.VMEM((DEPTH, rows, tile), jnp.float32)] * count + [pltpu.SemaphoreType.DMA((count, DEPTH))]


def in_hbm():
    return pl.BlockSpec(memory_space=pl.ANY)


def whole(array):
    return pl.BlockSpec(array.shape, lambda i: (0,) * len(array.shape))


def f32(*shape):
    return jax.ShapeDtypeStruct(shape, jnp.float32)


def on_diagonal(rows):
    return lax.broadcasted_iota(jnp.int32, (rows, rows), 0) == lax.broadcasted_iota(jnp.int32, (rows, rows), 1)


def strips(rows, columns):
    for column in range(0, columns, 256):
        for row in range(0, rows, 32):
            yield slice(row, row + 32), slice(column, column + 256)


def below(where, rows):
    return slice(where.start + rows, where.stop + rows)


def own_kernel(x_ref, out_ref, gram_ref, squares_ref, halves_ref, buffer, sems):
    @pl.when(pl.program_id(0) == 0)
    def _():
        gram_ref[...] = jnp.zeros_like(gram_ref)
        squares_ref[...] = jnp.zeros_like(squares_ref)

    (x,) = fetch([x_ref], [buffer], sems)
    rows = x.shape[0]
    for row, column in strips(*x.shape):
        part = x[row, column]
        hi, lo = split(part)
        halves_ref[row, column] = hi
        halves_ref[below(row, rows), column] = lo
        squares_ref[row, :] += lane_sums(part * part)
    gram_ref[...] += nt_dot(halves_ref[...], halves_ref[:rows, :])

    @pl.when(pl.program_id(0) == pl.num_programs(0) - 1)
    def _():
        mixed = gram_ref[rows:, :]
        gram = gram_ref[:rows, :] + mixed + mixed.T
        norms = jnp.sum(squares_ref[...], axis=1, keepdims=True)
        distance = jnp.where(on_diagonal(rows), norms, norms + norms.T - 2.0 * gram)
        half, quarter = rows // 2, rows // 4
        out_ref[:half, :] = distance[:half, :]
        out_ref[half:, :half] = distance[half:half + quarter, half:]
        out_ref[half:, half:] = distance[half + quarter:, half:]


def own_part(particles):
    rows, columns = particles.shape
    tile = min(GRAM_TILE, columns)
    out = f32(rows * 3 // 4, rows)
    return pl.pallas_call(
        own_kernel,
        grid=(columns // tile,),
        in_specs=[in_hbm()],
        out_specs=whole(out),
        out_shape=out,
        scratch_shapes=[
            pltpu.VMEM((2 * rows, rows), jnp.float32),
            pltpu.VMEM((rows, 128), jnp.float32),
            pltpu.VMEM((2 * rows, tile), jnp.bfloat16),
            *slots(1, rows, tile),
        ],
        compiler_params=params(52),
        cost_estimate=pl.CostEstimate(flops=4 * rows * rows * columns, bytes_accessed=4 * rows * columns, transcendentals=0),
        name="own_gram",
    )(particles)


def pair_kernel(core_ref, mine_ref, other_ref, out_ref, gram_ref, my_halves, halves, my_buffer, buffer, sems):
    @pl.when(pl.program_id(0) == 0)
    def _():
        gram_ref[...] = jnp.zeros_like(gram_ref)

    rows = gram_ref.shape[0]
    mine, other = fetch([mine_ref, other_ref], [my_buffer, buffer], sems, core_ref[0] * pl.num_programs(0))
    for source, halves_ref in ((mine, my_halves), (other, halves)):
        for row, column in strips(*source.shape):
            hi, lo = split(source[row, column])
            halves_ref[row, column] = hi
            halves_ref[below(row, rows), column] = lo
    both = nt_dot(my_halves[...], halves[:rows, :])
    gram_ref[...] += both[:rows] + both[rows:] + nt_dot(my_halves[:rows, :], halves[rows:, :])

    @pl.when(pl.program_id(0) == pl.num_programs(0) - 1)
    def _():
        gram = gram_ref[...]
        out_ref[...] = jnp.where(core_ref[0] == 0, gram, gram.T)


def pair_part(core, particles, visitor):
    rows, columns = particles.shape
    width = columns // 2
    tile = min(GRAM_TILE, width)
    tiles = width // tile
    out = f32(rows, rows)
    return pl.pallas_call(
        pair_kernel,
        grid_spec=pltpu.PrefetchScalarGridSpec(
            num_scalar_prefetch=1,
            grid=(tiles,),
            in_specs=[in_hbm(), in_hbm()],
            out_specs=pl.BlockSpec(out.shape, lambda i, core: (0, 0)),
            scratch_shapes=[
                pltpu.VMEM((rows, rows), jnp.float32),
                pltpu.VMEM((2 * rows, tile), jnp.bfloat16),
                pltpu.VMEM((2 * rows, tile), jnp.bfloat16),
                *slots(2, rows, tile),
            ],
        ),
        out_shape=out,
        compiler_params=params(52),
        cost_estimate=pl.CostEstimate(flops=6 * rows * rows * width, bytes_accessed=8 * rows * width, transcendentals=0),
        name="pair_gram",
    )(core, particles, visitor)


def sum_kernel(arrived_ref, out_ref):
    total = arrived_ref[0]
    for step in range(1, arrived_ref.shape[0]):
        total = total + arrived_ref[step]
    for step in range(out_ref.shape[0]):
        out_ref[step] = total


def summed_shards(block, axes, beside=None):
    count = lax.axis_size(axes)
    rows, columns = block.shape
    arrived = lax.all_to_all(block.reshape(count, rows // count, columns), axes, 0, 0)
    if beside is not None:
        arrived, _ = lax.optimization_barrier((arrived, beside))
    return pl.pallas_call(sum_kernel, out_shape=f32(*arrived.shape), compiler_params=params(8), name="sum_shards")(arrived)


def gathered(copies, axes):
    count, rows, columns = copies.shape
    return lax.all_to_all(copies, axes, 0, 0).reshape(count * rows, columns)


def summary_kernel(packed_ref, own_ref, out_ref):
    rows = own_ref.shape[0]
    half = rows // 2
    upper = packed_ref[:half, :]
    own_ref[:half, :] = upper
    own_ref[half:, :half] = upper[:, half:].T
    own_ref[half:half + half // 2, half:] = packed_ref[half:, :half]
    own_ref[half + half // 2:, half:] = packed_ref[half:, half:]
    own = own_ref[...]
    diagonal = on_diagonal(rows)
    norms = jnp.sum(jnp.where(diagonal, own, 0.0), axis=0, keepdims=True)
    total = jnp.sum(jnp.where(diagonal, 0.0, own))
    out_ref[...] = jnp.concatenate([norms, jnp.full((7, rows), total)], axis=0)


def summary_part(packed):
    rows = packed.shape[1]
    return pl.pallas_call(
        summary_kernel, out_shape=[f32(rows, rows), f32(8, rows)], compiler_params=params(8), name="summary"
    )(packed)


def weights_kernel(scale_base, core_ref, own_ref, summary_ref, other_ref, gram_ref, hi_ref, lo_ref, weight_ref, half_ref):
    own = own_ref[...]
    rows = own.shape[0]
    diagonal = on_diagonal(rows)
    norms = jnp.sum(jnp.where(diagonal, own, 0.0), axis=1, keepdims=True)
    gram = gram_ref[...]
    pair = norms + other_ref[0:1, :] - 2.0 * jnp.where(core_ref[0] == 0, gram, gram.T)
    spread = summary_ref[1:2, 0:1] + other_ref[1:2, 0:1] + 2.0 * jnp.sum(pair)
    width = spread / scale_base
    inverse = -1.0 / width
    own_weights = jnp.where(diagonal, 0.0, jnp.exp(own * inverse))
    pair_weights = jnp.exp(pair * inverse)
    weights = jnp.concatenate([own_weights, pair_weights], axis=1)
    hi_ref[...], lo_ref[...] = split(weights)
    weight_ref[...] = jnp.broadcast_to(jnp.sum(weights, axis=1, keepdims=True), weight_ref.shape)
    half_ref[...] = jnp.broadcast_to(0.5 * width, half_ref.shape)


def weights_part(core, own, summary, other, gram, scale_base):
    rows = own.shape[0]
    half = jax.ShapeDtypeStruct((rows, 2 * rows), jnp.bfloat16)
    return pl.pallas_call(
        functools.partial(weights_kernel, scale_base),
        in_specs=[pl.BlockSpec(memory_space=pltpu.SMEM)] + [pl.BlockSpec(memory_space=pltpu.VMEM)] * 4,
        out_shape=[half, half, f32(rows, 128), f32(32, 256)],
        compiler_params=params(12),
        name="kernel_weights",
    )(core, own, summary, other, gram)


def velocity_kernel(
    x_ref, s_ref, other_x_ref, other_s_ref, hi_ref, lo_ref, weight_ref, half_ref, out_ref, moved_ref, *scratch
):
    rows, columns = out_ref.shape
    half = half_ref[...]
    weights = jnp.concatenate([hi_ref[...], lo_ref[...]], axis=0)
    x, s, other_x, other_s = fetch([x_ref, s_ref, other_x_ref, other_s_ref], scratch[:4], scratch[4])
    for start in range(0, columns, 256):
        column = slice(start, start + 256)
        for offset, points, slopes in ((0, x, s), (rows, other_x, other_s)):
            for start_row in range(0, rows, 32):
                row = slice(start_row, start_row + 32)
                hi, lo = split(half * slopes[row, column] - points[row, column])
                moved_ref[below(row, offset), column] = hi
                moved_ref[below(row, offset + 2 * rows), column] = lo
        both = nn_dot(weights, moved_ref[:2 * rows, column])
        rest = nn_dot(hi_ref[...], moved_ref[2 * rows:, column])
        for start_row in range(0, rows, 32):
            row = slice(start_row, start_row + 32)
            weight = weight_ref[row, :]
            weight = jnp.concatenate([weight, weight], axis=1)
            out_ref[row, column] = (
                half * s[row, column] + weight * x[row, column] + both[row] + both[below(row, rows)] + rest[row]
            )


def velocity_part(particles, scores, visitor, visitor_scores, weights):
    rows, columns = particles.shape
    tile = min(VELOCITY_TILE, columns)
    block = pl.BlockSpec((rows, tile), lambda i: (0, i))
    return pl.pallas_call(
        velocity_kernel,
        grid=(columns // tile,),
        in_specs=[in_hbm()] * 4 + [whole(w) for w in weights],
        out_specs=block,
        out_shape=f32(rows, columns),
        scratch_shapes=[pltpu.VMEM((4 * rows, tile), jnp.bfloat16), *slots(4, rows, tile)],
        compiler_params=params(52),
        cost_estimate=pl.CostEstimate(flops=12 * rows * rows * columns, bytes_accessed=20 * rows * columns, transcendentals=0),
        name="velocity",
    )(particles, scores, visitor, visitor_scores, *weights)


def swap(array):
    return lax.ppermute(array, "blk", [(0, 1), (1, 0)])


def body(particles, scores):
    count = lax.axis_size("dim")
    total_rows = particles.shape[0] * lax.axis_size("blk")
    scale_base = total_rows * total_rows * math.log(total_rows)

    core = lax.axis_index("blk").reshape(1)
    visitor = swap(particles)
    visitor_scores = swap(scores)

    own = gathered(summed_shards(own_part(particles), "dim"), "dim")
    own, summary = summary_part(own)
    across = [(d * 2 + b, (d + 1) % count * 2 + 1 - b) for d in range(count) for b in range(2)]
    other = lax.ppermute(summary, BOTH, across)

    gram = summed_shards(pair_part(core, particles, visitor), BOTH, other)
    gram = gathered(gram, BOTH)
    weights = weights_part(core, own, summary, other, gram, scale_base)
    return velocity_part(particles, scores, visitor, visitor_scores, weights)


def solution(mesh):
    return jax.shard_map(
        body,
        mesh=mesh,
        in_specs=(P(("grp", "blk"), "dim"), P(("grp", "blk"), "dim")),
        out_specs=P(("grp", "blk"), "dim"),
        check_vma=False,
    )
```

```python
import functools
import math

import jax
import jax.numpy as jnp
from jax import lax
from jax.experimental import pallas as pl
from jax.experimental.pallas import tpu as pltpu
from jax.sharding import PartitionSpec as P

GRAM_TILE = 1024
VELOCITY_TILE = 1024
GRAM_DEPTH = 4
VELOCITY_DEPTH = 4
MIB = 1024 * 1024
BOTH = ("dim", "blk")


def params(limit):
    return pltpu.CompilerParams(vmem_limit_bytes=limit * MIB)


def split(x):
    hi = x.astype(jnp.bfloat16)
    lo = (x - hi.astype(jnp.float32)).astype(jnp.bfloat16)
    return hi, lo


def nt_dot(left, right):
    return lax.dot_general(left, right, (((1,), (1,)), ((), ())), preferred_element_type=jnp.float32)


def nn_dot(left, right):
    return jnp.dot(left, right, preferred_element_type=jnp.float32)


def lane_sums(values):
    total = values[:, :128]
    for start in range(128, values.shape[1], 128):
        total = total + values[:, start:start + 128]
    return total


def fetch(sources, buffers, sems, first=0):
    step, steps = pl.program_id(0), pl.num_programs(0)
    depth, _, tile = buffers[0].shape

    def each(at, act):
        slot = lax.rem(at, depth)
        for n, (source, buffer) in enumerate(zip(sources, buffers)):

            def one(source, block):
                columns = pl.ds(pl.multiple_of(block * tile, tile), tile)
                act(pltpu.make_async_copy(source.at[:, columns], buffer.at[slot], sems.at[n, slot]))

            if isinstance(source, tuple):
                pl.when(at < steps // 2)(functools.partial(one, source[0], at))
                pl.when(at >= steps // 2)(functools.partial(one, source[1], at - steps // 2))
            else:
                one(source, lax.rem(first + at, source.shape[1] // tile))

    def start(at):
        @pl.when(at < steps)
        def _():
            each(at, lambda copy: copy.start())

    @pl.when(step == 0)
    def _():
        for ahead in range(depth - 1):
            start(ahead)

    start(step + depth - 1)
    each(step, lambda copy: copy.wait())
    return [buffer.at[lax.rem(step, depth)] for buffer in buffers]


def slots(depth, count, rows, tile):
    return [pltpu.VMEM((depth, rows, tile), jnp.float32)] * count + [pltpu.SemaphoreType.DMA((count, depth))]


def in_hbm():
    return pl.BlockSpec(memory_space=pl.ANY)


def whole(array):
    return pl.BlockSpec(array.shape, lambda i, core: (0,) * len(array.shape))


def f32(*shape):
    return jax.ShapeDtypeStruct(shape, jnp.float32)


def on_diagonal(rows):
    return lax.broadcasted_iota(jnp.int32, (rows, rows), 0) == lax.broadcasted_iota(jnp.int32, (rows, rows), 1)


def strips(rows, columns):
    for column in range(0, columns, 256):
        for row in range(0, rows, 32):
            yield slice(row, row + 32), slice(column, column + 256)


def below(where, rows):
    return slice(where.start + rows, where.stop + rows)


def call(kernel, name, steps, in_specs, out_specs, out_shape, scratch, limit):
    return pl.pallas_call(
        kernel,
        grid_spec=pltpu.PrefetchScalarGridSpec(
            num_scalar_prefetch=1, grid=(steps,), in_specs=in_specs, out_specs=out_specs, scratch_shapes=scratch
        ),
        out_shape=out_shape,
        compiler_params=params(limit),
        cost_estimate=pl.CostEstimate(flops=1024, bytes_accessed=1024, transcendentals=0),
        name=name,
    )


def add_own(x, halves_ref, gram_ref, squares_ref):
    rows = x.shape[0]
    for row, column in strips(*x.shape):
        part = x[row, column]
        hi, lo = split(part)
        halves_ref[row, column] = hi
        halves_ref[below(row, rows), column] = lo
        squares_ref[row, :] += lane_sums(part * part)
    gram_ref[...] += nt_dot(halves_ref[...], halves_ref[:rows, :])


def sent_kernel(core_ref, x_ref, copy_ref, gram_ref, squares_ref, halves_ref, buffer, sems):
    steps = pl.num_programs(0)

    @pl.when(pl.program_id(0) == 0)
    def _():
        gram_ref[...] = jnp.zeros_like(gram_ref)
        squares_ref[...] = jnp.zeros_like(squares_ref)

    (x,) = fetch([x_ref], [buffer], sems, (1 - core_ref[0]) * steps)
    copy_ref[...] = x[...]
    add_own(x, halves_ref, gram_ref, squares_ref)


def kept_kernel(core_ref, x_ref, gram_in, squares_in, copy_ref, out_ref, gram_ref, squares_ref, halves_ref, buffer, sems):
    steps = pl.num_programs(0)

    @pl.when(pl.program_id(0) == 0)
    def _():
        gram_ref[...] = gram_in[...]
        squares_ref[...] = squares_in[...]

    (x,) = fetch([x_ref], [buffer], sems, core_ref[0] * steps)
    copy_ref[...] = x[...]
    add_own(x, halves_ref, gram_ref, squares_ref)

    @pl.when(pl.program_id(0) == steps - 1)
    def _():
        rows = x.shape[0]
        half = rows // 2
        mixed = gram_ref[rows:, :]
        gram = gram_ref[:rows, :] + mixed + mixed.T
        norms = jnp.sum(squares_ref[...], axis=1, keepdims=True)
        distance = norms + norms.T - 2.0 * gram
        down = lax.broadcasted_iota(jnp.int32, (half, half), 0)
        across = lax.broadcasted_iota(jnp.int32, (half, half), 1)
        square = jnp.where(across > down, distance[:half, :half], distance[half:, half:])
        out_ref[:, :half] = jnp.where(across == down, 0.0, square)
        out_ref[:, half:] = distance[:half, half:]


def own_parts(core, particles):
    rows, columns = particles.shape
    width = columns // 2
    tile = min(GRAM_TILE, width)
    block = pl.BlockSpec((rows, tile), lambda i, core: (0, i))
    sums = [f32(2 * rows, rows), f32(rows, 128)]
    scratch = [pltpu.VMEM((2 * rows, tile), jnp.bfloat16), *slots(GRAM_DEPTH, 1, rows, tile)]
    sent, *partial = call(
        sent_kernel, "own_gram_sent", width // tile, [in_hbm()], [block] + [whole(o) for o in sums],
        [f32(rows, width)] + sums, scratch, 56,
    )(core, particles)
    packed = f32(rows // 2, rows)
    kept, packed = call(
        kept_kernel, "own_gram_kept", width // tile, [in_hbm()] + [whole(o) for o in sums], [block, whole(packed)],
        [f32(rows, width), packed], [pltpu.VMEM(o.shape, jnp.float32) for o in sums] + scratch, 56,
    )(core, particles, *partial)
    return sent, kept, packed


def pair_kernel(core_ref, mine_ref, other_ref, packed_ref, out_ref, gram_ref, squares_ref, my_halves, halves, *scratch):
    my_buffer, buffer, sems = scratch
    steps = pl.num_programs(0)
    rows = gram_ref.shape[0]

    @pl.when(pl.program_id(0) == 0)
    def _():
        gram_ref[...] = jnp.zeros_like(gram_ref)
        squares_ref[...] = jnp.zeros_like(squares_ref)

    mine, other = fetch([mine_ref, other_ref], [my_buffer, buffer], sems, core_ref[0] * steps)
    for offset, source, halves_ref in ((0, mine, my_halves), (rows, other, halves)):
        for row, column in strips(*source.shape):
            part = source[row, column]
            hi, lo = split(part)
            halves_ref[row, column] = hi
            halves_ref[below(row, rows), column] = lo
            squares_ref[below(row, offset), :] += lane_sums(part * part)
    both = nt_dot(my_halves[...], halves[:rows, :])
    gram_ref[...] += both[:rows] + both[rows:] + nt_dot(my_halves[:rows, :], halves[rows:, :])

    @pl.when(pl.program_id(0) == steps - 1)
    def _():
        norms = jnp.sum(squares_ref[:rows, :], axis=1, keepdims=True)
        others = jnp.sum(squares_ref[rows:, :], axis=1, keepdims=True)
        pair = norms + others.T - 2.0 * gram_ref[...]
        gram_ref[...] = jnp.where(core_ref[0] == 0, pair, pair.T)
        count = out_ref.shape[0]
        depth, few = rows // count, rows // 2 // count
        for shard in range(count):
            out_ref[shard, :depth, :] = gram_ref[shard * depth:(shard + 1) * depth, :]
            out_ref[shard, depth:, :] = packed_ref[shard * few:(shard + 1) * few, :]


def pair_part(core, particles, visitor, packed, count):
    rows, width = visitor.shape
    tile = min(GRAM_TILE, width)
    out = f32(count, rows * 3 // 2 // count, rows)
    return call(
        pair_kernel, "pair_gram", width // tile, [in_hbm(), in_hbm(), whole(packed)], whole(out), out,
        [
            pltpu.VMEM((rows, rows), jnp.float32),
            pltpu.VMEM((2 * rows, 128), jnp.float32),
            pltpu.VMEM((2 * rows, tile), jnp.bfloat16),
            pltpu.VMEM((2 * rows, tile), jnp.bfloat16),
            *slots(GRAM_DEPTH, 2, rows, tile),
        ],
        56,
    )(core, particles, visitor, packed)


def sum_kernel(place_ref, arrived_ref, out_ref):
    count, height, rows = arrived_ref.shape
    depth = rows // count
    few = height - depth
    pair = arrived_ref[0, :depth, :]
    for source in range(1, count):
        pair = pair + arrived_ref[source, :depth, :]
    own = []
    for core in range(2):
        total = arrived_ref[core, depth:, :]
        for source in range(core + 2, count, 2):
            total = total + arrived_ref[source, depth:, :]
        own.append(total)
    down = lax.broadcasted_iota(jnp.int32, (few, rows), 0) + place_ref[0] * few
    free = down == lax.broadcasted_iota(jnp.int32, (few, rows), 1)
    for core in range(2):
        elsewhere = jnp.sum(jnp.where(free, 0.0, own[1 - core]), keepdims=True)
        shard = jnp.where(free, elsewhere * (2.0 / few), own[core])
        for target in range(core, count, 2):
            out_ref[target, :depth, :] = pair
            out_ref[target, depth:, :] = shard


def summed_shards(place, arrived):
    return pl.pallas_call(
        sum_kernel,
        in_specs=[pl.BlockSpec(memory_space=pltpu.SMEM), pl.BlockSpec(memory_space=pltpu.VMEM)],
        out_shape=f32(*arrived.shape),
        compiler_params=params(12),
        name="sum_shards",
    )(place, arrived)


def weights_kernel(scale_base, core_ref, shards_ref, hi_ref, lo_ref, weight_ref, half_ref, pair_ref, packed_ref):
    count, height, rows = shards_ref.shape
    depth, half = rows // count, rows // 2
    few = height - depth
    for shard in range(count):
        pair_ref[shard * depth:(shard + 1) * depth, :] = shards_ref[shard, :depth, :]
        packed_ref[shard * few:(shard + 1) * few, :] = shards_ref[shard, depth:, :]
    pair = pair_ref[...]
    pair = jnp.where(core_ref[0] == 0, pair, pair.T)
    square, corner = packed_ref[:, :half], packed_ref[:, half:]
    down = lax.broadcasted_iota(jnp.int32, (half, half), 0)
    across = lax.broadcasted_iota(jnp.int32, (half, half), 1)
    elsewhere = jnp.sum(jnp.where(across == down, square, 0.0), keepdims=True)
    upper = jnp.where(across == down, 0.0, jnp.where(across > down, square, square.T))
    lower = jnp.where(across == down, 0.0, jnp.where(across < down, square, square.T))
    own = jnp.concatenate(
        [jnp.concatenate([upper, corner], axis=1), jnp.concatenate([corner.T, lower], axis=1)], axis=0
    )
    spread = elsewhere + jnp.sum(own, keepdims=True) + 2.0 * jnp.sum(pair, keepdims=True)
    width = spread / scale_base
    inverse = -1.0 / width
    own_weights = jnp.where(on_diagonal(rows), 0.0, jnp.exp(own * inverse))
    pair_weights = jnp.exp(pair * inverse)
    weights = jnp.concatenate([own_weights, pair_weights], axis=1)
    hi_ref[...], lo_ref[...] = split(weights)
    weight_ref[...] = jnp.broadcast_to(jnp.sum(weights, axis=1, keepdims=True), weight_ref.shape)
    half_ref[...] = jnp.broadcast_to(0.5 * width, half_ref.shape)


def weights_part(core, shards, scale_base):
    rows = shards.shape[2]
    bf16 = jax.ShapeDtypeStruct((rows, 2 * rows), jnp.bfloat16)
    return pl.pallas_call(
        functools.partial(weights_kernel, scale_base),
        in_specs=[pl.BlockSpec(memory_space=pltpu.SMEM), pl.BlockSpec(memory_space=pltpu.VMEM)],
        out_shape=[bf16, bf16, f32(rows, 128), f32(32, 256)],
        scratch_shapes=[pltpu.VMEM((rows, rows), jnp.float32), pltpu.VMEM((rows // 2, rows), jnp.float32)],
        compiler_params=params(16),
        name="kernel_weights",
    )(core, shards)


def velocity_kernel(
    core_ref, x_ref, s_ref, first_x_ref, second_x_ref, other_s_ref, hi_ref, lo_ref, weight_ref, half_ref, out_ref, moved_ref, *scratch
):
    rows, columns = out_ref.shape
    half = half_ref[...]
    weights = jnp.concatenate([hi_ref[...], lo_ref[...]], axis=0)
    x, s, other_x, other_s = fetch(
        [x_ref, s_ref, (first_x_ref, second_x_ref), other_s_ref],
        scratch[:4],
        scratch[4],
        core_ref[0] * (pl.num_programs(0) // 2),
    )
    for start in range(0, columns, 256):
        column = slice(start, start + 256)
        for offset, points, slopes in ((0, x, s), (rows, other_x, other_s)):
            for start_row in range(0, rows, 32):
                row = slice(start_row, start_row + 32)
                hi, lo = split(half * slopes[row, column] - points[row, column])
                moved_ref[below(row, offset), column] = hi
                moved_ref[below(row, offset + 2 * rows), column] = lo
        both = nn_dot(weights, moved_ref[:2 * rows, column])
        rest = nn_dot(hi_ref[...], moved_ref[2 * rows:, column])
        for start_row in range(0, rows, 32):
            row = slice(start_row, start_row + 32)
            weight = weight_ref[row, :]
            weight = jnp.concatenate([weight, weight], axis=1)
            out_ref[row, column] = (
                half * s[row, column] + weight * x[row, column] + both[row] + both[below(row, rows)] + rest[row]
            )


def velocity_part(core, particles, scores, visitors, visitor_scores, weights):
    rows, columns = particles.shape
    tile = min(VELOCITY_TILE, columns // 2)
    steps = columns // tile
    return call(
        velocity_kernel, "velocity", steps, [in_hbm()] * 5 + [whole(w) for w in weights],
        pl.BlockSpec((rows, tile), lambda i, core: (0, lax.rem(core[0] * (steps // 2) + i, steps))),
        f32(rows, columns), [pltpu.VMEM((4 * rows, tile), jnp.bfloat16), *slots(VELOCITY_DEPTH, 4, rows, tile)],
        52,
    )(core, particles, scores, *visitors, visitor_scores, *weights)


def swap(array):
    return lax.ppermute(array, "blk", [(0, 1), (1, 0)])


def body(particles, scores):
    total_rows = particles.shape[0] * lax.axis_size("blk")
    scale_base = total_rows * total_rows * math.log(total_rows)
    core = lax.axis_index("blk").reshape(1)
    place = lax.axis_index("dim").reshape(1) * 2 + core

    sent, kept, packed = own_parts(core, particles)
    visitor = swap(sent)
    kept, scores_late, _ = lax.optimization_barrier((kept, scores, visitor))
    visitors = [visitor, swap(kept)]
    visitor_scores = swap(scores_late)

    shards = pair_part(core, particles, visitor, packed, lax.axis_size(BOTH))
    shards = summed_shards(place, lax.all_to_all(shards, BOTH, 0, 0))
    weights = weights_part(core, lax.all_to_all(shards, BOTH, 0, 0), scale_base)
    return velocity_part(core, particles, scores, visitors, visitor_scores, weights)


def solution(mesh):
    return jax.shard_map(
        body,
        mesh=mesh,
        in_specs=(P(("grp", "blk"), "dim"), P(("grp", "blk"), "dim")),
        out_specs=P(("grp", "blk"), "dim"),
        check_vma=False,
    )
```

```python
import functools
import math

import jax
import jax.numpy as jnp
from jax import lax
from jax.experimental import pallas as pl
from jax.experimental.pallas import tpu as pltpu
from jax.sharding import PartitionSpec as P

GRAM_TILE = 1024
VELOCITY_TILE = 1024
GRAM_DEPTH = 4
VELOCITY_DEPTH = 4
MIB = 1024 * 1024
BOTH = ("dim", "blk")


def params(limit):
    return pltpu.CompilerParams(vmem_limit_bytes=limit * MIB)


def split(x):
    hi = x.astype(jnp.bfloat16)
    lo = (x - hi.astype(jnp.float32)).astype(jnp.bfloat16)
    return hi, lo


def nt_dot(left, right):
    return lax.dot_general(left, right, (((1,), (1,)), ((), ())), preferred_element_type=jnp.float32)


def nn_dot(left, right):
    return jnp.dot(left, right, preferred_element_type=jnp.float32)


def lane_sums(values):
    total = values[:, :128]
    for start in range(128, values.shape[1], 128):
        total = total + values[:, start:start + 128]
    return total


def fetch(sources, buffers, sems, first=0):
    step, steps = pl.program_id(0), pl.num_programs(0)
    depth, _, tile = buffers[0].shape

    def each(at, act):
        slot = lax.rem(at, depth)
        for n, (source, buffer) in enumerate(zip(sources, buffers)):

            def one(source, block):
                columns = pl.ds(pl.multiple_of(block * tile, tile), tile)
                act(pltpu.make_async_copy(source.at[:, columns], buffer.at[slot], sems.at[n, slot]))

            if isinstance(source, tuple):
                begin = 0
                for piece in source:
                    end = begin + piece.shape[1] // tile
                    pl.when((at >= begin) & (at < end))(functools.partial(one, piece, at - begin))
                    begin = end
            else:
                one(source, lax.rem(first + at, source.shape[1] // tile))

    def start(at):
        @pl.when(at < steps)
        def _():
            each(at, lambda copy: copy.start())

    @pl.when(step == 0)
    def _():
        for ahead in range(depth - 1):
            start(ahead)

    start(step + depth - 1)
    each(step, lambda copy: copy.wait())
    return [buffer.at[lax.rem(step, depth)] for buffer in buffers]


def slots(depth, count, rows, tile):
    return [pltpu.VMEM((depth, rows, tile), jnp.float32)] * count + [pltpu.SemaphoreType.DMA((count, depth))]


def in_hbm():
    return pl.BlockSpec(memory_space=pl.ANY)


def whole(array):
    return pl.BlockSpec(array.shape, lambda i, core: (0,) * len(array.shape))


def f32(*shape):
    return jax.ShapeDtypeStruct(shape, jnp.float32)


def on_diagonal(rows):
    return lax.broadcasted_iota(jnp.int32, (rows, rows), 0) == lax.broadcasted_iota(jnp.int32, (rows, rows), 1)


def strips(rows, columns):
    for column in range(0, columns, 256):
        for row in range(0, rows, 32):
            yield slice(row, row + 32), slice(column, column + 256)


def below(where, rows):
    return slice(where.start + rows, where.stop + rows)


def call(kernel, name, steps, in_specs, out_specs, out_shape, scratch, limit):
    return pl.pallas_call(
        kernel,
        grid_spec=pltpu.PrefetchScalarGridSpec(
            num_scalar_prefetch=1, grid=(steps,), in_specs=in_specs, out_specs=out_specs, scratch_shapes=scratch
        ),
        out_shape=out_shape,
        compiler_params=params(limit),
        cost_estimate=pl.CostEstimate(flops=1024, bytes_accessed=1024, transcendentals=0),
        name=name,
    )


def add_own(x, halves_ref, gram_ref, squares_ref):
    rows = x.shape[0]
    for row, column in strips(*x.shape):
        part = x[row, column]
        hi, lo = split(part)
        halves_ref[row, column] = hi
        halves_ref[below(row, rows), column] = lo
        squares_ref[row, :] += lane_sums(part * part)
    gram_ref[...] += nt_dot(halves_ref[...], halves_ref[:rows, :])


def cut_kernel(begin, of_other, core_ref, x_ref, out_ref, buffer, in_sems, out_sems):
    columns = out_ref.shape[1]
    half = x_ref.shape[1] // 2
    side = 1 - core_ref[0] if of_other else core_ref[0]
    step = columns // in_sems.shape[0]
    start = pl.multiple_of(side * half + begin, step)
    ins, outs = [], []
    for n in range(in_sems.shape[0]):
        there = pl.ds(n * step, step)
        here = pl.ds(pl.multiple_of(start + n * step, step), step)
        ins.append(pltpu.make_async_copy(x_ref.at[:, here], buffer.at[:, there], in_sems.at[n]))
        outs.append(pltpu.make_async_copy(buffer.at[:, there], out_ref.at[:, there], out_sems.at[n]))
    for copy in ins:
        copy.start()
    for arriving, leaving in zip(ins, outs):
        arriving.wait()
        leaving.start()
    for copy in outs:
        copy.wait()


def cut(core, array, begin, width, of_other):
    rows = array.shape[0]
    pieces = max(1, width // 512)
    return pl.pallas_call(
        functools.partial(cut_kernel, begin, of_other),
        in_specs=[pl.BlockSpec(memory_space=pltpu.SMEM), in_hbm()],
        out_specs=in_hbm(),
        out_shape=f32(rows, width),
        scratch_shapes=[
            pltpu.VMEM((rows, width), jnp.float32),
            pltpu.SemaphoreType.DMA((pieces,)),
            pltpu.SemaphoreType.DMA((pieces,)),
        ],
        compiler_params=params(56),
        cost_estimate=pl.CostEstimate(
            flops=0, bytes_accessed=1024 if of_other else 8 * rows * width, transcendentals=0
        ),
        name="cut_positions",
    )(core, array)


def own_kernel(core_ref, x_ref, out_ref, gram_ref, squares_ref, halves_ref, buffer, sems):
    steps = pl.num_programs(0)

    @pl.when(pl.program_id(0) == 0)
    def _():
        gram_ref[...] = jnp.zeros_like(gram_ref)
        squares_ref[...] = jnp.zeros_like(squares_ref)

    (x,) = fetch([x_ref], [buffer], sems)
    add_own(x, halves_ref, gram_ref, squares_ref)

    @pl.when(pl.program_id(0) == steps - 1)
    def _():
        rows = x.shape[0]
        half = rows // 2
        mixed = gram_ref[rows:, :]
        gram = gram_ref[:rows, :] + mixed + mixed.T
        norms = jnp.sum(squares_ref[...], axis=1, keepdims=True)
        distance = norms + norms.T - 2.0 * gram
        down = lax.broadcasted_iota(jnp.int32, (half, half), 0)
        across = lax.broadcasted_iota(jnp.int32, (half, half), 1)
        square = jnp.where(across > down, distance[:half, :half], distance[half:, half:])
        out_ref[:, :half] = jnp.where(across == down, 0.0, square)
        out_ref[:, half:] = distance[:half, half:]


def own_part(core, particles):
    rows, columns = particles.shape
    tile = min(GRAM_TILE, columns)
    packed = f32(rows // 2, rows)
    return call(
        own_kernel, "own_gram", columns // tile, [in_hbm()], whole(packed), packed,
        [
            pltpu.VMEM((2 * rows, rows), jnp.float32),
            pltpu.VMEM((rows, 128), jnp.float32),
            pltpu.VMEM((2 * rows, tile), jnp.bfloat16),
            *slots(GRAM_DEPTH, 1, rows, tile),
        ],
        56,
    )(core, particles)


def pair_kernel(
    core_ref, mine_ref, other_ref, packed_ref, out_ref, gram_ref, squares_ref, my_halves, halves, *scratch
):
    my_buffer, buffer, sems = scratch
    steps = pl.num_programs(0)
    rows = gram_ref.shape[0]

    @pl.when(pl.program_id(0) == 0)
    def _():
        gram_ref[...] = jnp.zeros_like(gram_ref)
        squares_ref[...] = jnp.zeros_like(squares_ref)

    mine, other = fetch([mine_ref, other_ref], [my_buffer, buffer], sems, core_ref[0] * steps)
    for offset, source, halves_ref in ((0, mine, my_halves), (rows, other, halves)):
        for row, column in strips(*source.shape):
            part = source[row, column]
            hi, lo = split(part)
            halves_ref[row, column] = hi
            halves_ref[below(row, rows), column] = lo
            squares_ref[below(row, offset), :] += lane_sums(part * part)
    both = nt_dot(my_halves[...], halves[:rows, :])
    gram_ref[...] += both[:rows] + both[rows:] + nt_dot(my_halves[:rows, :], halves[rows:, :])

    @pl.when(pl.program_id(0) == steps - 1)
    def _():
        norms = jnp.sum(squares_ref[:rows, :], axis=1, keepdims=True)
        others = jnp.sum(squares_ref[rows:, :], axis=1, keepdims=True)
        pair = norms + others.T - 2.0 * gram_ref[...]
        gram_ref[...] = jnp.where(core_ref[0] == 0, pair, pair.T)
        count = out_ref.shape[0]
        depth, few = rows // count, rows // 2 // count
        for shard in range(count):
            out_ref[shard, :depth, :] = gram_ref[shard * depth:(shard + 1) * depth, :]
            out_ref[shard, depth:, :] = packed_ref[shard * few:(shard + 1) * few, :]


def pair_part(core, particles, visitors, packed, count):
    rows, width = particles.shape[0], particles.shape[1] // 2
    tile = min(GRAM_TILE, width)
    out = f32(count, rows * 3 // 2 // count, rows)
    return call(
        pair_kernel, "pair_gram", width // tile, [in_hbm()] * 2 + [whole(packed)], whole(out), out,
        [
            pltpu.VMEM((rows, rows), jnp.float32),
            pltpu.VMEM((2 * rows, 128), jnp.float32),
            pltpu.VMEM((2 * rows, tile), jnp.bfloat16),
            pltpu.VMEM((2 * rows, tile), jnp.bfloat16),
            *slots(GRAM_DEPTH, 2, rows, tile),
        ],
        56,
    )(core, particles, *visitors, packed)


def sum_kernel(place_ref, arrived_ref, out_ref):
    count, height, rows = arrived_ref.shape
    depth = rows // count
    few = height - depth
    pair = arrived_ref[0, :depth, :]
    for source in range(1, count):
        pair = pair + arrived_ref[source, :depth, :]
    own = []
    for core in range(2):
        total = arrived_ref[core, depth:, :]
        for source in range(core + 2, count, 2):
            total = total + arrived_ref[source, depth:, :]
        own.append(total)
    down = lax.broadcasted_iota(jnp.int32, (few, rows), 0) + place_ref[0] * few
    free = down == lax.broadcasted_iota(jnp.int32, (few, rows), 1)
    for core in range(2):
        elsewhere = jnp.sum(jnp.where(free, 0.0, own[1 - core]), keepdims=True)
        shard = jnp.where(free, elsewhere * (2.0 / few), own[core])
        for target in range(core, count, 2):
            out_ref[target, :depth, :] = pair
            out_ref[target, depth:, :] = shard


def summed_shards(place, arrived):
    return pl.pallas_call(
        sum_kernel,
        in_specs=[pl.BlockSpec(memory_space=pltpu.SMEM), pl.BlockSpec(memory_space=pltpu.VMEM)],
        out_shape=f32(*arrived.shape),
        compiler_params=params(58),
        name="sum_shards",
    )(place, arrived)


def weights_kernel(scale_base, core_ref, shards_ref, hi_ref, lo_ref, weight_ref, half_ref, pair_ref, packed_ref):
    count, height, rows = shards_ref.shape
    depth, half = rows // count, rows // 2
    few = height - depth
    for shard in range(count):
        pair_ref[shard * depth:(shard + 1) * depth, :] = shards_ref[shard, :depth, :]
        packed_ref[shard * few:(shard + 1) * few, :] = shards_ref[shard, depth:, :]
    pair = pair_ref[...]
    pair = jnp.where(core_ref[0] == 0, pair, pair.T)
    square, corner = packed_ref[:, :half], packed_ref[:, half:]
    down = lax.broadcasted_iota(jnp.int32, (half, half), 0)
    across = lax.broadcasted_iota(jnp.int32, (half, half), 1)
    elsewhere = jnp.sum(jnp.where(across == down, square, 0.0), keepdims=True)
    upper = jnp.where(across == down, 0.0, jnp.where(across > down, square, square.T))
    lower = jnp.where(across == down, 0.0, jnp.where(across < down, square, square.T))
    own = jnp.concatenate(
        [jnp.concatenate([upper, corner], axis=1), jnp.concatenate([corner.T, lower], axis=1)], axis=0
    )
    spread = elsewhere + jnp.sum(own, keepdims=True) + 2.0 * jnp.sum(pair, keepdims=True)
    width = spread / scale_base
    inverse = -1.0 / width
    own_weights = jnp.where(on_diagonal(rows), 0.0, jnp.exp(own * inverse))
    pair_weights = jnp.exp(pair * inverse)
    weights = jnp.concatenate([own_weights, pair_weights], axis=1)
    hi_ref[...], lo_ref[...] = split(weights)
    weight_ref[...] = jnp.broadcast_to(jnp.sum(weights, axis=1, keepdims=True), weight_ref.shape)
    half_ref[...] = jnp.broadcast_to(0.5 * width, half_ref.shape)


def weights_part(core, shards, scale_base):
    rows = shards.shape[2]
    bf16 = jax.ShapeDtypeStruct((rows, 2 * rows), jnp.bfloat16)
    return pl.pallas_call(
        functools.partial(weights_kernel, scale_base),
        in_specs=[pl.BlockSpec(memory_space=pltpu.SMEM), pl.BlockSpec(memory_space=pltpu.VMEM)],
        out_shape=[bf16, bf16, f32(rows, 128), f32(32, 256)],
        scratch_shapes=[pltpu.VMEM((rows, rows), jnp.float32), pltpu.VMEM((rows // 2, rows), jnp.float32)],
        compiler_params=params(16),
        name="kernel_weights",
    )(core, shards)


def velocity_kernel(
    core_ref, x_ref, s_ref, first_x_ref, last_x_ref, other_s_ref, hi_ref, lo_ref, weight_ref, half_ref, out_ref, moved_ref, *scratch
):
    rows, columns = out_ref.shape
    half = half_ref[...]
    weights = jnp.concatenate([hi_ref[...], lo_ref[...]], axis=0)
    x, s, other_x, other_s = fetch(
        [x_ref, s_ref, (first_x_ref, last_x_ref), other_s_ref],
        scratch[:4],
        scratch[4],
        core_ref[0] * (pl.num_programs(0) // 2),
    )
    for start in range(0, columns, 256):
        column = slice(start, start + 256)
        for offset, points, slopes in ((0, x, s), (rows, other_x, other_s)):
            for start_row in range(0, rows, 32):
                row = slice(start_row, start_row + 32)
                hi, lo = split(half * slopes[row, column] - points[row, column])
                moved_ref[below(row, offset), column] = hi
                moved_ref[below(row, offset + 2 * rows), column] = lo
        both = nn_dot(weights, moved_ref[:2 * rows, column])
        rest = nn_dot(hi_ref[...], moved_ref[2 * rows:, column])
        for start_row in range(0, rows, 32):
            row = slice(start_row, start_row + 32)
            weight = weight_ref[row, :]
            weight = jnp.concatenate([weight, weight], axis=1)
            out_ref[row, column] = (
                half * s[row, column] + weight * x[row, column] + both[row] + both[below(row, rows)] + rest[row]
            )


def velocity_part(core, particles, scores, visitors, visitor_scores, weights):
    rows, columns = particles.shape
    tile = min(VELOCITY_TILE, columns // 2)
    steps = columns // tile
    return call(
        velocity_kernel, "velocity", steps, [in_hbm()] * 5 + [whole(w) for w in weights],
        pl.BlockSpec((rows, tile), lambda i, core: (0, lax.rem(core[0] * (steps // 2) + i, steps))),
        f32(rows, columns), [pltpu.VMEM((4 * rows, tile), jnp.bfloat16), *slots(VELOCITY_DEPTH, 4, rows, tile)],
        52,
    )(core, particles, scores, *visitors, visitor_scores, *weights)


def swap(array):
    return lax.ppermute(array, "blk", [(0, 1), (1, 0)])


def body(particles, scores):
    total_rows = particles.shape[0] * lax.axis_size("blk")
    scale_base = total_rows * total_rows * math.log(total_rows)
    core = lax.axis_index("blk").reshape(1)
    place = lax.axis_index("dim").reshape(1) * 2 + core

    width = particles.shape[1] // 2
    sent = cut(core, particles, 0, width, True)
    visitors = [swap(sent)]
    particles_next, _ = lax.optimization_barrier((particles, sent))
    packed = own_part(core, particles_next)
    scores_late, *_ = lax.optimization_barrier((scores, visitors[0], packed))
    visitor_scores = swap(scores_late)

    shards = pair_part(core, particles, visitors, packed, lax.axis_size(BOTH))
    particles_next, _ = lax.optimization_barrier((particles, shards))
    visitors.append(swap(cut(core, particles_next, 0, width, False)))
    shards = summed_shards(place, lax.all_to_all(shards, BOTH, 0, 0))
    weights = weights_part(core, lax.all_to_all(shards, BOTH, 0, 0), scale_base)
    return velocity_part(core, particles, scores, visitors, visitor_scores, weights)


def solution(mesh):
    return jax.shard_map(
        body,
        mesh=mesh,
        in_specs=(P(("grp", "blk"), "dim"), P(("grp", "blk"), "dim")),
        out_specs=P(("grp", "blk"), "dim"),
        check_vma=False,
    )
```

```python
import functools
import math

import jax
import jax.numpy as jnp
from jax import lax
from jax.experimental import pallas as pl
from jax.experimental.pallas import tpu as pltpu
from jax.sharding import PartitionSpec as P

GRAM_TILE = 1024
VELOCITY_TILE = 1024
GRAM_DEPTH = 4
VELOCITY_DEPTH = 4
MIB = 1024 * 1024
BOTH = ("dim", "blk")


def params(limit):
    return pltpu.CompilerParams(vmem_limit_bytes=limit * MIB)


def split(x):
    hi = x.astype(jnp.bfloat16)
    lo = (x - hi.astype(jnp.float32)).astype(jnp.bfloat16)
    return hi, lo


def nt_dot(left, right):
    return lax.dot_general(left, right, (((1,), (1,)), ((), ())), preferred_element_type=jnp.float32)


def nn_dot(left, right):
    return jnp.dot(left, right, preferred_element_type=jnp.float32)


def lane_sums(values):
    total = values[:, :128]
    for start in range(128, values.shape[1], 128):
        total = total + values[:, start:start + 128]
    return total


def fetch(sources, buffers, sems, first=0):
    step, steps = pl.program_id(0), pl.num_programs(0)
    depth, _, tile = buffers[0].shape

    def each(at, act):
        slot = lax.rem(at, depth)
        for n, (source, buffer) in enumerate(zip(sources, buffers)):

            def one(source, block):
                columns = pl.ds(pl.multiple_of(block * tile, tile), tile)
                act(pltpu.make_async_copy(source.at[:, columns], buffer.at[slot], sems.at[n, slot]))

            if isinstance(source, tuple):
                pl.when(at < steps // 2)(functools.partial(one, source[0], at))
                pl.when(at >= steps // 2)(functools.partial(one, source[1], at - steps // 2))
            else:
                one(source, lax.rem(first + at, source.shape[1] // tile))

    def start(at):
        @pl.when(at < steps)
        def _():
            each(at, lambda copy: copy.start())

    @pl.when(step == 0)
    def _():
        for ahead in range(depth - 1):
            start(ahead)

    start(step + depth - 1)
    each(step, lambda copy: copy.wait())
    return [buffer.at[lax.rem(step, depth)] for buffer in buffers]


def slots(depth, count, rows, tile):
    return [pltpu.VMEM((depth, rows, tile), jnp.float32)] * count + [pltpu.SemaphoreType.DMA((count, depth))]


def in_hbm():
    return pl.BlockSpec(memory_space=pl.ANY)


def whole(array):
    return pl.BlockSpec(array.shape, lambda i, core: (0,) * len(array.shape))


def f32(*shape):
    return jax.ShapeDtypeStruct(shape, jnp.float32)


def on_diagonal(rows):
    return lax.broadcasted_iota(jnp.int32, (rows, rows), 0) == lax.broadcasted_iota(jnp.int32, (rows, rows), 1)


def strips(rows, columns):
    for column in range(0, columns, 256):
        for row in range(0, rows, 32):
            yield slice(row, row + 32), slice(column, column + 256)


def below(where, rows):
    return slice(where.start + rows, where.stop + rows)


def call(kernel, name, steps, in_specs, out_specs, out_shape, scratch, limit):
    return pl.pallas_call(
        kernel,
        grid_spec=pltpu.PrefetchScalarGridSpec(
            num_scalar_prefetch=1, grid=(steps,), in_specs=in_specs, out_specs=out_specs, scratch_shapes=scratch
        ),
        out_shape=out_shape,
        compiler_params=params(limit),
        cost_estimate=pl.CostEstimate(flops=1024, bytes_accessed=1024, transcendentals=0),
        name=name,
    )


def add_own(x, halves_ref, gram_ref, squares_ref):
    rows = x.shape[0]
    for row, column in strips(*x.shape):
        part = x[row, column]
        hi, lo = split(part)
        halves_ref[row, column] = hi
        halves_ref[below(row, rows), column] = lo
        squares_ref[row, :] += lane_sums(part * part)
    gram_ref[...] += nt_dot(halves_ref[...], halves_ref[:rows, :])


def cut_kernel(core_ref, x_ref, out_ref, buffer, in_sems, out_sems):
    columns = out_ref.shape[1]
    step = columns // in_sems.shape[0]
    start = pl.multiple_of((1 - core_ref[0]) * columns, step)
    ins, outs = [], []
    for n in range(in_sems.shape[0]):
        there = pl.ds(n * step, step)
        here = pl.ds(pl.multiple_of(start + n * step, step), step)
        ins.append(pltpu.make_async_copy(x_ref.at[:, here], buffer.at[:, there], in_sems.at[n]))
        outs.append(pltpu.make_async_copy(buffer.at[:, there], out_ref.at[:, there], out_sems.at[n]))
    for copy in ins:
        copy.start()
    for arriving, leaving in zip(ins, outs):
        arriving.wait()
        leaving.start()
    for copy in outs:
        copy.wait()


def cut(core, array):
    rows, width = array.shape[0], array.shape[1] // 2
    pieces = max(1, width // 512)
    return pl.pallas_call(
        cut_kernel,
        in_specs=[pl.BlockSpec(memory_space=pltpu.SMEM), in_hbm()],
        out_specs=in_hbm(),
        out_shape=f32(rows, width),
        scratch_shapes=[
            pltpu.VMEM((rows, width), jnp.float32),
            pltpu.SemaphoreType.DMA((pieces,)),
            pltpu.SemaphoreType.DMA((pieces,)),
        ],
        compiler_params=params(56),
        cost_estimate=pl.CostEstimate(flops=1024, bytes_accessed=1024, transcendentals=0),
        name="cut_positions",
    )(core, array)


def own_kernel(core_ref, x_ref, copy_ref, out_ref, gram_ref, squares_ref, halves_ref, buffer, sems):
    steps = pl.num_programs(0)

    @pl.when(pl.program_id(0) == 0)
    def _():
        gram_ref[...] = jnp.zeros_like(gram_ref)
        squares_ref[...] = jnp.zeros_like(squares_ref)

    (x,) = fetch([x_ref], [buffer], sems, core_ref[0] * (steps // 2))

    @pl.when(pl.program_id(0) < steps // 2)
    def _():
        copy_ref[...] = x[...]

    add_own(x, halves_ref, gram_ref, squares_ref)

    @pl.when(pl.program_id(0) == steps - 1)
    def _():
        rows = x.shape[0]
        half = rows // 2
        mixed = gram_ref[rows:, :]
        gram = gram_ref[:rows, :] + mixed + mixed.T
        norms = jnp.sum(squares_ref[...], axis=1, keepdims=True)
        distance = norms + norms.T - 2.0 * gram
        down = lax.broadcasted_iota(jnp.int32, (half, half), 0)
        across = lax.broadcasted_iota(jnp.int32, (half, half), 1)
        square = jnp.where(across > down, distance[:half, :half], distance[half:, half:])
        out_ref[:, :half] = jnp.where(across == down, 0.0, square)
        out_ref[:, half:] = distance[:half, half:]


def own_part(core, particles):
    rows, columns = particles.shape
    tile = min(GRAM_TILE, columns // 2)
    steps = columns // tile
    packed = f32(rows // 2, rows)
    return call(
        own_kernel, "own_gram", steps, [in_hbm()],
        [pl.BlockSpec((rows, tile), lambda i, core: (0, jnp.minimum(i, steps // 2 - 1))), whole(packed)],
        [f32(rows, columns // 2), packed],
        [
            pltpu.VMEM((2 * rows, rows), jnp.float32),
            pltpu.VMEM((rows, 128), jnp.float32),
            pltpu.VMEM((2 * rows, tile), jnp.bfloat16),
            *slots(GRAM_DEPTH, 1, rows, tile),
        ],
        56,
    )(core, particles)


def pair_kernel(core_ref, mine_ref, other_ref, packed_ref, out_ref, gram_ref, squares_ref, my_halves, halves, *scratch):
    my_buffer, buffer, sems = scratch
    steps = pl.num_programs(0)
    rows = gram_ref.shape[0]

    @pl.when(pl.program_id(0) == 0)
    def _():
        gram_ref[...] = jnp.zeros_like(gram_ref)
        squares_ref[...] = jnp.zeros_like(squares_ref)

    mine, other = fetch([mine_ref, other_ref], [my_buffer, buffer], sems, core_ref[0] * steps)
    for offset, source, halves_ref in ((0, mine, my_halves), (rows, other, halves)):
        for row, column in strips(*source.shape):
            part = source[row, column]
            hi, lo = split(part)
            halves_ref[row, column] = hi
            halves_ref[below(row, rows), column] = lo
            squares_ref[below(row, offset), :] += lane_sums(part * part)
    both = nt_dot(my_halves[...], halves[:rows, :])
    gram_ref[...] += both[:rows] + both[rows:] + nt_dot(my_halves[:rows, :], halves[rows:, :])

    @pl.when(pl.program_id(0) == steps - 1)
    def _():
        norms = jnp.sum(squares_ref[:rows, :], axis=1, keepdims=True)
        others = jnp.sum(squares_ref[rows:, :], axis=1, keepdims=True)
        pair = norms + others.T - 2.0 * gram_ref[...]
        gram_ref[...] = jnp.where(core_ref[0] == 0, pair, pair.T)
        count = out_ref.shape[0]
        depth, few = rows // count, rows // 2 // count
        for shard in range(count):
            out_ref[shard, :depth, :] = gram_ref[shard * depth:(shard + 1) * depth, :]
            out_ref[shard, depth:, :] = packed_ref[shard * few:(shard + 1) * few, :]


def pair_part(core, particles, visitor, packed, count):
    rows, width = visitor.shape
    tile = min(GRAM_TILE, width)
    out = f32(count, rows * 3 // 2 // count, rows)
    return call(
        pair_kernel, "pair_gram", width // tile, [in_hbm(), in_hbm(), whole(packed)], whole(out), out,
        [
            pltpu.VMEM((rows, rows), jnp.float32),
            pltpu.VMEM((2 * rows, 128), jnp.float32),
            pltpu.VMEM((2 * rows, tile), jnp.bfloat16),
            pltpu.VMEM((2 * rows, tile), jnp.bfloat16),
            *slots(GRAM_DEPTH, 2, rows, tile),
        ],
        56,
    )(core, particles, visitor, packed)


def sum_kernel(place_ref, arrived_ref, out_ref):
    count, height, rows = arrived_ref.shape
    depth = rows // count
    few = height - depth
    pair = arrived_ref[0, :depth, :]
    for source in range(1, count):
        pair = pair + arrived_ref[source, :depth, :]
    own = []
    for core in range(2):
        total = arrived_ref[core, depth:, :]
        for source in range(core + 2, count, 2):
            total = total + arrived_ref[source, depth:, :]
        own.append(total)
    down = lax.broadcasted_iota(jnp.int32, (few, rows), 0) + place_ref[0] * few
    free = down == lax.broadcasted_iota(jnp.int32, (few, rows), 1)
    for core in range(2):
        elsewhere = jnp.sum(jnp.where(free, 0.0, own[1 - core]), keepdims=True)
        shard = jnp.where(free, elsewhere * (2.0 / few), own[core])
        for target in range(core, count, 2):
            out_ref[target, :depth, :] = pair
            out_ref[target, depth:, :] = shard


def summed_shards(place, arrived):
    return pl.pallas_call(
        sum_kernel,
        in_specs=[pl.BlockSpec(memory_space=pltpu.SMEM), pl.BlockSpec(memory_space=pltpu.VMEM)],
        out_shape=f32(*arrived.shape),
        compiler_params=params(12),
        name="sum_shards",
    )(place, arrived)


def weights_kernel(scale_base, core_ref, shards_ref, hi_ref, lo_ref, weight_ref, half_ref, pair_ref, packed_ref):
    count, height, rows = shards_ref.shape
    depth, half = rows // count, rows // 2
    few = height - depth
    for shard in range(count):
        pair_ref[shard * depth:(shard + 1) * depth, :] = shards_ref[shard, :depth, :]
        packed_ref[shard * few:(shard + 1) * few, :] = shards_ref[shard, depth:, :]
    pair = pair_ref[...]
    pair = jnp.where(core_ref[0] == 0, pair, pair.T)
    square, corner = packed_ref[:, :half], packed_ref[:, half:]
    down = lax.broadcasted_iota(jnp.int32, (half, half), 0)
    across = lax.broadcasted_iota(jnp.int32, (half, half), 1)
    elsewhere = jnp.sum(jnp.where(across == down, square, 0.0), keepdims=True)
    upper = jnp.where(across == down, 0.0, jnp.where(across > down, square, square.T))
    lower = jnp.where(across == down, 0.0, jnp.where(across < down, square, square.T))
    own = jnp.concatenate(
        [jnp.concatenate([upper, corner], axis=1), jnp.concatenate([corner.T, lower], axis=1)], axis=0
    )
    spread = elsewhere + jnp.sum(own, keepdims=True) + 2.0 * jnp.sum(pair, keepdims=True)
    width = spread / scale_base
    inverse = -1.0 / width
    own_weights = jnp.where(on_diagonal(rows), 0.0, jnp.exp(own * inverse))
    pair_weights = jnp.exp(pair * inverse)
    weights = jnp.concatenate([own_weights, pair_weights], axis=1)
    hi_ref[...], lo_ref[...] = split(weights)
    weight_ref[...] = jnp.broadcast_to(jnp.sum(weights, axis=1, keepdims=True), weight_ref.shape)
    half_ref[...] = jnp.broadcast_to(0.5 * width, half_ref.shape)


def weights_part(core, shards, scale_base):
    rows = shards.shape[2]
    bf16 = jax.ShapeDtypeStruct((rows, 2 * rows), jnp.bfloat16)
    return pl.pallas_call(
        functools.partial(weights_kernel, scale_base),
        in_specs=[pl.BlockSpec(memory_space=pltpu.SMEM), pl.BlockSpec(memory_space=pltpu.VMEM)],
        out_shape=[bf16, bf16, f32(rows, 128), f32(32, 256)],
        scratch_shapes=[pltpu.VMEM((rows, rows), jnp.float32), pltpu.VMEM((rows // 2, rows), jnp.float32)],
        compiler_params=params(16),
        name="kernel_weights",
    )(core, shards)


def velocity_kernel(
    core_ref, x_ref, s_ref, first_x_ref, second_x_ref, other_s_ref, hi_ref, lo_ref, weight_ref, half_ref, out_ref, moved_ref, *scratch
):
    rows, columns = out_ref.shape
    half = half_ref[...]
    weights = jnp.concatenate([hi_ref[...], lo_ref[...]], axis=0)
    x, s, other_x, other_s = fetch(
        [x_ref, s_ref, (first_x_ref, second_x_ref), other_s_ref],
        scratch[:4],
        scratch[4],
        core_ref[0] * (pl.num_programs(0) // 2),
    )
    for start in range(0, columns, 256):
        column = slice(start, start + 256)
        for offset, points, slopes in ((0, x, s), (rows, other_x, other_s)):
            for start_row in range(0, rows, 32):
                row = slice(start_row, start_row + 32)
                hi, lo = split(half * slopes[row, column] - points[row, column])
                moved_ref[below(row, offset), column] = hi
                moved_ref[below(row, offset + 2 * rows), column] = lo
        both = nn_dot(weights, moved_ref[:2 * rows, column])
        rest = nn_dot(hi_ref[...], moved_ref[2 * rows:, column])
        for start_row in range(0, rows, 32):
            row = slice(start_row, start_row + 32)
            weight = weight_ref[row, :]
            weight = jnp.concatenate([weight, weight], axis=1)
            out_ref[row, column] = (
                half * s[row, column] + weight * x[row, column] + both[row] + both[below(row, rows)] + rest[row]
            )


def velocity_part(core, particles, scores, visitors, visitor_scores, weights):
    rows, columns = particles.shape
    tile = min(VELOCITY_TILE, columns // 2)
    steps = columns // tile
    return call(
        velocity_kernel, "velocity", steps, [in_hbm()] * 5 + [whole(w) for w in weights],
        pl.BlockSpec((rows, tile), lambda i, core: (0, lax.rem(core[0] * (steps // 2) + i, steps))),
        f32(rows, columns), [pltpu.VMEM((4 * rows, tile), jnp.bfloat16), *slots(VELOCITY_DEPTH, 4, rows, tile)],
        52,
    )(core, particles, scores, *visitors, visitor_scores, *weights)


def swap(array):
    return lax.ppermute(array, "blk", [(0, 1), (1, 0)])


def body(particles, scores):
    total_rows = particles.shape[0] * lax.axis_size("blk")
    scale_base = total_rows * total_rows * math.log(total_rows)
    core = lax.axis_index("blk").reshape(1)
    place = lax.axis_index("dim").reshape(1) * 2 + core

    core, place = lax.optimization_barrier((core, place))

    sent = cut(core, particles)
    visitor = swap(sent)
    particles_next, _ = lax.optimization_barrier((particles, sent))
    kept, packed = own_part(core, particles_next)
    kept, scores_late, _ = lax.optimization_barrier((kept, scores, visitor))
    visitors = [visitor, swap(kept)]
    visitor_scores = swap(scores_late)

    shards = pair_part(core, particles, visitor, packed, lax.axis_size(BOTH))
    shards = summed_shards(place, lax.all_to_all(shards, BOTH, 0, 0))
    weights = weights_part(core, lax.all_to_all(shards, BOTH, 0, 0), scale_base)
    return velocity_part(core, particles, scores, visitors, visitor_scores, weights)


def solution(mesh):
    return jax.shard_map(
        body,
        mesh=mesh,
        in_specs=(P(("grp", "blk"), "dim"), P(("grp", "blk"), "dim")),
        out_specs=P(("grp", "blk"), "dim"),
        check_vma=False,
    )
```

```python
import functools
import math

import jax
import jax.numpy as jnp
from jax import lax
from jax.experimental import pallas as pl
from jax.experimental.pallas import tpu as pltpu
from jax.sharding import PartitionSpec as P

GRAM_TILE = 1024
VELOCITY_TILE = 1024
GRAM_DEPTH = 4
VELOCITY_DEPTH = 4
MIB = 1024 * 1024
BOTH = ("dim", "blk")


def params(limit):
    return pltpu.CompilerParams(vmem_limit_bytes=limit * MIB)


def split(x):
    hi = x.astype(jnp.bfloat16)
    lo = (x - hi.astype(jnp.float32)).astype(jnp.bfloat16)
    return hi, lo


def nt_dot(left, right):
    return lax.dot_general(left, right, (((1,), (1,)), ((), ())), preferred_element_type=jnp.float32)


def nn_dot(left, right):
    return jnp.dot(left, right, preferred_element_type=jnp.float32)


def lane_sums(values):
    total = values[:, :128]
    for start in range(128, values.shape[1], 128):
        total = total + values[:, start:start + 128]
    return total


def fetch(sources, buffers, sems, first=0):
    step, steps = pl.program_id(0), pl.num_programs(0)
    depth, _, tile = buffers[0].shape

    def each(at, act):
        slot = lax.rem(at, depth)
        for n, (source, buffer) in enumerate(zip(sources, buffers)):

            def one(source, block):
                columns = pl.ds(pl.multiple_of(block * tile, tile), tile)
                act(pltpu.make_async_copy(source.at[:, columns], buffer.at[slot], sems.at[n, slot]))

            if isinstance(source, tuple):
                begin = 0
                for piece in source:
                    end = begin + piece.shape[1] // tile
                    pl.when((at >= begin) & (at < end))(functools.partial(one, piece, at - begin))
                    begin = end
            else:
                one(source, lax.rem(first + at, source.shape[1] // tile))

    def start(at):
        @pl.when(at < steps)
        def _():
            each(at, lambda copy: copy.start())

    @pl.when(step == 0)
    def _():
        for ahead in range(depth - 1):
            start(ahead)

    start(step + depth - 1)
    each(step, lambda copy: copy.wait())
    return [buffer.at[lax.rem(step, depth)] for buffer in buffers]


def slots(depth, count, rows, tile):
    return [pltpu.VMEM((depth, rows, tile), jnp.float32)] * count + [pltpu.SemaphoreType.DMA((count, depth))]


def in_hbm():
    return pl.BlockSpec(memory_space=pl.ANY)


def whole(array):
    return pl.BlockSpec(array.shape, lambda i, core: (0,) * len(array.shape))


def f32(*shape):
    return jax.ShapeDtypeStruct(shape, jnp.float32)


def on_diagonal(rows):
    return lax.broadcasted_iota(jnp.int32, (rows, rows), 0) == lax.broadcasted_iota(jnp.int32, (rows, rows), 1)


def strips(rows, columns):
    for column in range(0, columns, 256):
        for row in range(0, rows, 32):
            yield slice(row, row + 32), slice(column, column + 256)


def below(where, rows):
    return slice(where.start + rows, where.stop + rows)


def call(kernel, name, steps, in_specs, out_specs, out_shape, scratch, limit):
    return pl.pallas_call(
        kernel,
        grid_spec=pltpu.PrefetchScalarGridSpec(
            num_scalar_prefetch=1, grid=(steps,), in_specs=in_specs, out_specs=out_specs, scratch_shapes=scratch
        ),
        out_shape=out_shape,
        compiler_params=params(limit),
        cost_estimate=pl.CostEstimate(flops=1024, bytes_accessed=1024, transcendentals=0),
        name=name,
    )


def add_own(x, halves_ref, gram_ref, squares_ref):
    rows = x.shape[0]
    for row, column in strips(*x.shape):
        part = x[row, column]
        hi, lo = split(part)
        halves_ref[row, column] = hi
        halves_ref[below(row, rows), column] = lo
        squares_ref[row, :] += lane_sums(part * part)
    gram_ref[...] += nt_dot(halves_ref[...], halves_ref[:rows, :])


def sent_kernel(piece, core_ref, x_ref, *refs):
    gram_in, squares_in = refs[:2] if piece else (None, None)
    copy_ref, gram_ref, squares_ref, halves_ref, buffer, sems = refs[-6:]
    steps = pl.num_programs(0)

    @pl.when(pl.program_id(0) == 0)
    def _():
        gram_ref[...] = gram_in[...] if piece else jnp.zeros_like(gram_ref)
        squares_ref[...] = squares_in[...] if piece else jnp.zeros_like(squares_ref)

    (x,) = fetch([x_ref], [buffer], sems, (1 - core_ref[0]) * 2 * steps + piece * steps)
    copy_ref[...] = x[...]
    add_own(x, halves_ref, gram_ref, squares_ref)


def kept_kernel(core_ref, x_ref, gram_in, squares_in, copy_ref, out_ref, gram_ref, squares_ref, halves_ref, buffer, sems):
    steps = pl.num_programs(0)

    @pl.when(pl.program_id(0) == 0)
    def _():
        gram_ref[...] = gram_in[...]
        squares_ref[...] = squares_in[...]

    (x,) = fetch([x_ref], [buffer], sems, core_ref[0] * steps)
    copy_ref[...] = x[...]
    add_own(x, halves_ref, gram_ref, squares_ref)

    @pl.when(pl.program_id(0) == steps - 1)
    def _():
        rows = x.shape[0]
        half = rows // 2
        mixed = gram_ref[rows:, :]
        gram = gram_ref[:rows, :] + mixed + mixed.T
        norms = jnp.sum(squares_ref[...], axis=1, keepdims=True)
        distance = norms + norms.T - 2.0 * gram
        down = lax.broadcasted_iota(jnp.int32, (half, half), 0)
        across = lax.broadcasted_iota(jnp.int32, (half, half), 1)
        square = jnp.where(across > down, distance[:half, :half], distance[half:, half:])
        out_ref[:, :half] = jnp.where(across == down, 0.0, square)
        out_ref[:, half:] = distance[:half, half:]


def own_parts(core, particles):
    rows, columns = particles.shape
    width = columns // 2
    tile = min(GRAM_TILE, width // 2)
    block = pl.BlockSpec((rows, tile), lambda i, core: (0, i))
    sums = [f32(2 * rows, rows), f32(rows, 128)]
    scratch = [pltpu.VMEM((2 * rows, tile), jnp.bfloat16), *slots(GRAM_DEPTH, 1, rows, tile)]
    sent, partial = [], []
    for piece in range(2):
        copy, *partial = call(
            functools.partial(sent_kernel, piece), "own_gram_sent", width // tile // 2,
            [in_hbm()] + [whole(p) for p in partial], [block] + [whole(o) for o in sums],
            [f32(rows, width // 2)] + sums, scratch, 60,
        )(core, particles, *partial)
        sent.append(copy)
    packed = f32(rows // 2, rows)
    kept, packed = call(
        kept_kernel, "own_gram_kept", width // tile, [in_hbm()] + [whole(o) for o in sums], [block, whole(packed)],
        [f32(rows, width), packed], [pltpu.VMEM(o.shape, jnp.float32) for o in sums] + scratch, 60,
    )(core, particles, *partial)
    return sent, kept, packed


def pair_kernel(
    core_ref, mine_ref, first_ref, second_ref, packed_ref, out_ref, gram_ref, squares_ref, my_halves, halves, *scratch
):
    my_buffer, buffer, sems = scratch
    steps = pl.num_programs(0)
    rows = gram_ref.shape[0]

    @pl.when(pl.program_id(0) == 0)
    def _():
        gram_ref[...] = jnp.zeros_like(gram_ref)
        squares_ref[...] = jnp.zeros_like(squares_ref)

    mine, other = fetch([mine_ref, (first_ref, second_ref)], [my_buffer, buffer], sems, core_ref[0] * steps)
    for offset, source, halves_ref in ((0, mine, my_halves), (rows, other, halves)):
        for row, column in strips(*source.shape):
            part = source[row, column]
            hi, lo = split(part)
            halves_ref[row, column] = hi
            halves_ref[below(row, rows), column] = lo
            squares_ref[below(row, offset), :] += lane_sums(part * part)
    both = nt_dot(my_halves[...], halves[:rows, :])
    gram_ref[...] += both[:rows] + both[rows:] + nt_dot(my_halves[:rows, :], halves[rows:, :])

    @pl.when(pl.program_id(0) == steps - 1)
    def _():
        norms = jnp.sum(squares_ref[:rows, :], axis=1, keepdims=True)
        others = jnp.sum(squares_ref[rows:, :], axis=1, keepdims=True)
        pair = norms + others.T - 2.0 * gram_ref[...]
        gram_ref[...] = jnp.where(core_ref[0] == 0, pair, pair.T)
        count = out_ref.shape[0]
        depth, few = rows // count, rows // 2 // count
        for shard in range(count):
            out_ref[shard, :depth, :] = gram_ref[shard * depth:(shard + 1) * depth, :]
            out_ref[shard, depth:, :] = packed_ref[shard * few:(shard + 1) * few, :]


def pair_part(core, particles, visitors, packed, count):
    rows, width = particles.shape[0], particles.shape[1] // 2
    tile = min(GRAM_TILE, width // 2)
    out = f32(count, rows * 3 // 2 // count, rows)
    return call(
        pair_kernel, "pair_gram", width // tile, [in_hbm()] * 3 + [whole(packed)], whole(out), out,
        [
            pltpu.VMEM((rows, rows), jnp.float32),
            pltpu.VMEM((2 * rows, 128), jnp.float32),
            pltpu.VMEM((2 * rows, tile), jnp.bfloat16),
            pltpu.VMEM((2 * rows, tile), jnp.bfloat16),
            *slots(GRAM_DEPTH, 2, rows, tile),
        ],
        60,
    )(core, particles, *visitors, packed)


def sum_kernel(place_ref, arrived_ref, out_ref):
    count, height, rows = arrived_ref.shape
    depth = rows // count
    few = height - depth
    pair = arrived_ref[0, :depth, :]
    for source in range(1, count):
        pair = pair + arrived_ref[source, :depth, :]
    own = []
    for core in range(2):
        total = arrived_ref[core, depth:, :]
        for source in range(core + 2, count, 2):
            total = total + arrived_ref[source, depth:, :]
        own.append(total)
    down = lax.broadcasted_iota(jnp.int32, (few, rows), 0) + place_ref[0] * few
    free = down == lax.broadcasted_iota(jnp.int32, (few, rows), 1)
    for core in range(2):
        elsewhere = jnp.sum(jnp.where(free, 0.0, own[1 - core]), keepdims=True)
        shard = jnp.where(free, elsewhere * (2.0 / few), own[core])
        for target in range(core, count, 2):
            out_ref[target, :depth, :] = pair
            out_ref[target, depth:, :] = shard


def summed_shards(place, arrived):
    return pl.pallas_call(
        sum_kernel,
        in_specs=[pl.BlockSpec(memory_space=pltpu.SMEM), pl.BlockSpec(memory_space=pltpu.VMEM)],
        out_shape=f32(*arrived.shape),
        compiler_params=params(12),
        name="sum_shards",
    )(place, arrived)


def weights_kernel(scale_base, core_ref, shards_ref, hi_ref, lo_ref, weight_ref, half_ref, pair_ref, packed_ref):
    count, height, rows = shards_ref.shape
    depth, half = rows // count, rows // 2
    few = height - depth
    for shard in range(count):
        pair_ref[shard * depth:(shard + 1) * depth, :] = shards_ref[shard, :depth, :]
        packed_ref[shard * few:(shard + 1) * few, :] = shards_ref[shard, depth:, :]
    pair = pair_ref[...]
    pair = jnp.where(core_ref[0] == 0, pair, pair.T)
    square, corner = packed_ref[:, :half], packed_ref[:, half:]
    down = lax.broadcasted_iota(jnp.int32, (half, half), 0)
    across = lax.broadcasted_iota(jnp.int32, (half, half), 1)
    elsewhere = jnp.sum(jnp.where(across == down, square, 0.0), keepdims=True)
    upper = jnp.where(across == down, 0.0, jnp.where(across > down, square, square.T))
    lower = jnp.where(across == down, 0.0, jnp.where(across < down, square, square.T))
    own = jnp.concatenate(
        [jnp.concatenate([upper, corner], axis=1), jnp.concatenate([corner.T, lower], axis=1)], axis=0
    )
    spread = elsewhere + jnp.sum(own, keepdims=True) + 2.0 * jnp.sum(pair, keepdims=True)
    width = spread / scale_base
    inverse = -1.0 / width
    own_weights = jnp.where(on_diagonal(rows), 0.0, jnp.exp(own * inverse))
    pair_weights = jnp.exp(pair * inverse)
    weights = jnp.concatenate([own_weights, pair_weights], axis=1)
    hi_ref[...], lo_ref[...] = split(weights)
    weight_ref[...] = jnp.broadcast_to(jnp.sum(weights, axis=1, keepdims=True), weight_ref.shape)
    half_ref[...] = jnp.broadcast_to(0.5 * width, half_ref.shape)


def weights_part(core, shards, scale_base):
    rows = shards.shape[2]
    bf16 = jax.ShapeDtypeStruct((rows, 2 * rows), jnp.bfloat16)
    return pl.pallas_call(
        functools.partial(weights_kernel, scale_base),
        in_specs=[pl.BlockSpec(memory_space=pltpu.SMEM), pl.BlockSpec(memory_space=pltpu.VMEM)],
        out_shape=[bf16, bf16, f32(rows, 128), f32(32, 256)],
        scratch_shapes=[pltpu.VMEM((rows, rows), jnp.float32), pltpu.VMEM((rows // 2, rows), jnp.float32)],
        compiler_params=params(16),
        name="kernel_weights",
    )(core, shards)


def velocity_kernel(
    core_ref, x_ref, s_ref, first_x_ref, second_x_ref, last_x_ref, other_s_ref, hi_ref, lo_ref, weight_ref, half_ref, out_ref, moved_ref, *scratch
):
    rows, columns = out_ref.shape
    half = half_ref[...]
    weights = jnp.concatenate([hi_ref[...], lo_ref[...]], axis=0)
    x, s, other_x, other_s = fetch(
        [x_ref, s_ref, (first_x_ref, second_x_ref, last_x_ref), other_s_ref],
        scratch[:4],
        scratch[4],
        core_ref[0] * (pl.num_programs(0) // 2),
    )
    for start in range(0, columns, 256):
        column = slice(start, start + 256)
        for offset, points, slopes in ((0, x, s), (rows, other_x, other_s)):
            for start_row in range(0, rows, 32):
                row = slice(start_row, start_row + 32)
                hi, lo = split(half * slopes[row, column] - points[row, column])
                moved_ref[below(row, offset), column] = hi
                moved_ref[below(row, offset + 2 * rows), column] = lo
        both = nn_dot(weights, moved_ref[:2 * rows, column])
        rest = nn_dot(hi_ref[...], moved_ref[2 * rows:, column])
        for start_row in range(0, rows, 32):
            row = slice(start_row, start_row + 32)
            weight = weight_ref[row, :]
            weight = jnp.concatenate([weight, weight], axis=1)
            out_ref[row, column] = (
                half * s[row, column] + weight * x[row, column] + both[row] + both[below(row, rows)] + rest[row]
            )


def velocity_part(core, particles, scores, visitors, visitor_scores, weights):
    rows, columns = particles.shape
    tile = min(VELOCITY_TILE, columns // 4)
    steps = columns // tile
    return call(
        velocity_kernel, "velocity", steps, [in_hbm()] * 6 + [whole(w) for w in weights],
        pl.BlockSpec((rows, tile), lambda i, core: (0, lax.rem(core[0] * (steps // 2) + i, steps))),
        f32(rows, columns), [pltpu.VMEM((4 * rows, tile), jnp.bfloat16), *slots(VELOCITY_DEPTH, 4, rows, tile)],
        52,
    )(core, particles, scores, *visitors, visitor_scores, *weights)


def swap(array):
    return lax.ppermute(array, "blk", [(0, 1), (1, 0)])


def body(particles, scores):
    total_rows = particles.shape[0] * lax.axis_size("blk")
    scale_base = total_rows * total_rows * math.log(total_rows)
    core = lax.axis_index("blk").reshape(1)
    place = lax.axis_index("dim").reshape(1) * 2 + core

    core, place = lax.optimization_barrier((core, place))

    sent, kept, packed = own_parts(core, particles)
    visitors = [swap(part) for part in sent]
    kept, scores_late, *_ = lax.optimization_barrier((kept, scores, *visitors))
    visitor_scores = swap(scores_late)

    shards = pair_part(core, particles, visitors, packed, lax.axis_size(BOTH))
    visitors.append(swap(kept))
    shards = summed_shards(place, lax.all_to_all(shards, BOTH, 0, 0))
    weights = weights_part(core, lax.all_to_all(shards, BOTH, 0, 0), scale_base)
    return velocity_part(core, particles, scores, visitors, visitor_scores, weights)


def solution(mesh):
    return jax.shard_map(
        body,
        mesh=mesh,
        in_specs=(P(("grp", "blk"), "dim"), P(("grp", "blk"), "dim")),
        out_specs=P(("grp", "blk"), "dim"),
        check_vma=False,
    )
```
